32 devices in a mesh: fs: 4 (over y, x), ep: 8 (over z, core).
Axes of the slice: x: 2, y: 2, z: 4, core: 2. Of those that a mesh axis runs over, the one named last changes fastest.
Arguments:
- tokens: bfloat16 [4096, 2880], P(('fs', 'ep')), may hold values from -6 to 6
- seq_lengths: int32 [32, 3], P(('fs', 'ep')), may hold values from 1 to 64, 128 in all within a row
- routes: int32 [4096, 4], P(('fs', 'ep')), may hold values from 0 to 15, all different within a row; in each aligned block of 128 rows (0 to 127, 128 to 255, ...) at most 48 rows name the same one
- attn_gain: bfloat16 [2880], P('fs'), may hold values from 0.5 to 1.5
- w_query: bfloat16 [2880, 4096], P('fs'), may hold values from -0.109375 to 0.109375
- b_query: bfloat16 [4096], P('fs'), may hold values from -3 to 3
- w_key: bfloat16 [2880, 512], P('fs'), may hold values from -0.109375 to 0.109375
- b_key: bfloat16 [512], P('fs'), may hold values from -3 to 3
- w_value: bfloat16 [2880, 512], P('fs'), may hold values from -0.109375 to 0.109375
- b_value: bfloat16 [512], P('fs'), may hold values from -3 to 3
- sinks: bfloat16 [64], P('fs'), may hold values from -1 to 2
- w_out: bfloat16 [4096, 2880], P('fs'), may hold values from -0.75 to 0.75
- b_out: bfloat16 [2880], P('fs'), may hold values from -2 to 2
- ffn_gain: bfloat16 [2880], P('fs'), may hold values from 0.5 to 1.5
- w_router: bfloat16 [2880, 16], P('fs'), may hold values from -0.0546875 to 0.0546875
- b_router: bfloat16 [16], P('fs'), may hold values from -1 to 1
- w_gate: bfloat16 [16, 2880, 2880], P('ep', None, 'fs'), may hold values from -0.109375 to 0.109375
- b_gate: bfloat16 [16, 2880], P('ep', 'fs'), may hold values from -1 to 1
- w_up: bfloat16 [16, 2880, 2880], P('ep', None, 'fs'), may hold values from -0.109375 to 0.109375
- b_up: bfloat16 [16, 2880], P('ep', 'fs'), may hold values from -1 to 1
- w_down: bfloat16 [16, 2880, 2880], P('ep', 'fs'), may hold values from -0.21875 to 0.21875
- b_down: bfloat16 [16, 2880], P('ep'), may hold values from -0.59765625 to 0.59765625
- cotangent: bfloat16 [4096, 2880], P(('fs', 'ep')), may hold values from -6 to 6
Outputs:
- block_out: bfloat16 [4096, 2880], P(('fs', 'ep'))
- grad_tokens: float32 [4096, 2880], P(('fs', 'ep'))
- grad_attn_gain: float32 [2880], P('fs')
- grad_w_query: float32 [2880, 4096], P('fs')
- grad_b_query: float32 [4096], P('fs')
- grad_w_key: float32 [2880, 512], P('fs')
- grad_b_key: float32 [512], P('fs')
- grad_w_value: float32 [2880, 512], P('fs')
- grad_b_value: float32 [512], P('fs')
- grad_sinks: float32 [64], P('fs')
- grad_w_out: float32 [4096, 2880], P('fs')
- grad_b_out: float32 [2880], P('fs')
- grad_ffn_gain: float32 [2880], P('fs')
- grad_w_router: float32 [2880, 16], P('fs')
- grad_b_router: float32 [16], P('fs')
- grad_w_gate: float32 [16, 2880, 2880], P('ep', None, 'fs')
- grad_b_gate: float32 [16, 2880], P('ep', 'fs')
- grad_w_up: float32 [16, 2880, 2880], P('ep', None, 'fs')
- grad_b_up: float32 [16, 2880], P('ep', 'fs')
- grad_w_down: float32 [16, 2880, 2880], P('ep', 'fs')
- grad_b_down: float32 [16, 2880], P('ep')
The draws below stay inside these ranges and needn't reach their ends.
Inputs may be any that keep to these rules, and one draw needn't show every extreme that they name: `routes`: each row names 4 different experts; among the 128 rows of one device no expert is named more than 48 times. `seq_lengths`: each device's 3 lengths sum to 128.
All inputs are finite; a program needn't handle non-finite values.
Results may differ from the reference program's by a relative error of at most 0.028.
Values may be sent and summed in bfloat16 or wider, within the bound.
A program may use at most 704 MiB of HBM per device.

```python
import math
import jax
import jax.numpy as jnp
import numpy as np
from jax import lax

D = 2880
QUERY_HEADS = 64
KEY_VALUE_HEADS = 8
HEAD_SIZE = 64
FF = 2880
TOP = 4
SEQ_DEV = 3
TOKENS_PER_CARD = 128
EXPERTS = 16
QW = 4096
KW = 512
TOKENS = 4096
CAP = 48
DEVICES = 32


def shard_levels(stream_key, extent, cuts, smallest, largest):
    level, own = 1.0, jax.random.fold_in(stream_key, 6)
    for dim, parts in cuts:
        steps = jnp.exp(jax.random.uniform(jax.random.fold_in(own, dim), (parts,), jnp.float32, smallest / len(cuts), largest / len(cuts)))
        level = level * jnp.repeat(steps, extent[dim] // parts).reshape([-1 if axis == dim else 1 for axis in range(len(extent))])
    return level


def split_up(number_of, total, bound, skew):
    weights = [(1 << 20) // math.isqrt(rank ** skew) + 1 for rank in range(2, number_of + 1)]
    spare, given = total - bound - (number_of - 1), [1] * (number_of - 1)
    while spare > 0:
        candidates = [i for i in range(number_of - 1) if given[i] < bound]
        whole, left = sum([weights[i] for i in candidates]), spare
        for i in candidates:
            more = min(bound - given[i], max(1, left * weights[i] // whole), spare)
            given[i] = given[i] + more
            spare = spare - more
    return np.array([bound] + given)


def uneven_parts(stream_key, amount, total, limit, skew):
    if amount == 2:
        one = jax.random.randint(stream_key, (), max(1, total - limit), min(limit, total - 1) + 1)
        return jnp.stack([one, total - one])
    tallies = jnp.asarray(split_up(amount, total, limit, skew), jnp.int32)
    pairs = (amount - 1) // 2
    source_of, receiver = tallies[1:1 + 2 * pairs:2], tallies[2:2 + 2 * pairs:2]
    margin = jnp.minimum(source_of - 1, limit - receiver)
    shifted = jax.random.randint(jax.random.fold_in(stream_key, 1), (pairs,), 0, 1 << 20) % (margin + 1)
    tallies = tallies.at[1:1 + 2 * pairs:2].set(source_of - shifted).at[2:2 + 2 * pairs:2].set(receiver + shifted)
    return tallies[jax.random.permutation(jax.random.fold_in(stream_key, 2), amount)]


def shared_out(own_key, own, number, rows, number_of, top, limit, skew):
    sequence = jax.random.permutation(own_key, number_of)
    crowded, usual = portions_of(number_of, rows * top, limit, skew, True), portions_of(number_of, rows * top, limit, skew, False)
    places = jnp.arange(number_of)

    def named(sizes, rotation):
        used = int((sizes > 0).sum())
        fixed = max(1, used // 4)
        moved = fixed + (places - fixed + rotation * (used - fixed)) % max(1, number_of - fixed)
        return jnp.zeros((number_of,), jnp.int32).at[sequence[jnp.where(places < fixed, places, moved)]].set(jnp.asarray(sizes, jnp.int32))

    sizes = jnp.where(number % 4 == 0, named(crowded, number // 4), named(usual, number - number // 4 - 1))
    mixed = jax.random.permutation(jax.random.fold_in(own, 3), number_of)
    source_of, sink = mixed[0:number_of // 2 * 2:2], mixed[1:number_of // 2 * 2:2]
    margin = jnp.minimum(sizes[source_of] - 1, limit - sizes[sink]) // 2
    margin = jnp.where((source_of == sequence[0]) | (sink == sequence[0]) | (sizes[sink] == 0), 0, jnp.maximum(margin, 0))
    moved = jax.random.randint(jax.random.fold_in(own, 4), (number_of // 2,), 0, 1 << 20) % (margin + 1)
    sizes = sizes.at[source_of].add(-moved).at[sink].add(moved)
    labels = jnp.searchsorted(jnp.cumsum(sizes), jnp.arange(rows * top), side="right").astype(jnp.int32)
    listing = labels.reshape(top, rows).T
    listing = listing[jax.random.permutation(jax.random.fold_in(own, 1), rows)]
    rotation = jax.random.randint(jax.random.fold_in(own, 2), (rows, 1), 0, top)
    return jnp.take_along_axis(listing, (jnp.arange(top)[None, :] + rotation) % top, axis=1)


def portions_of(amount, total, most, skew, full):
    portions = [(1 << 20) // math.isqrt(rank ** skew) + 1 for rank in range(1, amount + 1)]
    largest = most if full else min(most, max(-(-total // amount), total * portions[0] // sum(portions)))
    least = 1 if total - largest >= amount - 1 else 0
    counts, surplus = [largest] + [least] * (amount - 1), total - largest - least * (amount - 1)
    while surplus > 0:
        candidates = [i for i in range(1, amount) if counts[i] < largest] or [i for i in range(1, amount) if counts[i] < most]
        pool, left = sum([portions[i] for i in candidates]), surplus
        for i in candidates:
            addition = min(most - counts[i], max(1, left * portions[i] // pool), surplus)
            counts[i] = counts[i] + addition
            surplus = surplus - addition
    return np.array(counts)


def scatter_about(key, dims, width, limit, cuts=(), kind=jnp.bfloat16):
    values = width * jax.random.normal(key, dims, jnp.float32)
    if cuts:
        values = values * shard_levels(key, dims, cuts, -0.22, 0.18)
    return jnp.clip(values, -limit, limit).astype(kind)


def setup_inputs(seed: int = 0) -> dict:
    key_list = jax.random.split(jax.random.key(seed), 24)
    tokens = scatter_about(key_list[0], (TOKENS, D), 1.0, 6.0, ((0, 32),))
    seq_lengths = jax.vmap(lambda own: uneven_parts(own, SEQ_DEV, TOKENS_PER_CARD, TOKENS_PER_CARD // 2, 1))(jax.random.split(key_list[1], DEVICES)).reshape((DEVICES, SEQ_DEV)).astype(jnp.int32)
    routes_keys = jax.random.split(jax.random.fold_in(key_list[2], 1), TOKENS // TOKENS_PER_CARD)
    routes_turns = jax.random.permutation(jax.random.fold_in(key_list[2], 3), TOKENS // TOKENS_PER_CARD)
    routes = jax.vmap(lambda own, number: shared_out(jax.random.fold_in(key_list[2], 2), own, number, TOKENS_PER_CARD, EXPERTS, TOP, CAP, 1))(routes_keys, routes_turns).reshape((TOKENS, TOP))
    attn_gain = jnp.clip(1.0 + 0.1 * jax.random.normal(key_list[3], (D,), jnp.float32), 0.5, 1.5).astype(jnp.bfloat16)
    w_query = scatter_about(key_list[4], (D, QW), D ** -0.5, 0.109375, ((0, 4),))
    b_query = scatter_about(key_list[5], (QW,), 0.5, 3.0, ((0, 4),))
    w_key = scatter_about(key_list[6], (D, KW), D ** -0.5, 0.109375, ((0, 4),))
    b_key = scatter_about(key_list[7], (KW,), 0.5, 3.0, ((0, 4),))
    w_value = scatter_about(key_list[8], (D, KW), D ** -0.5, 0.109375, ((0, 4),))
    b_value = scatter_about(key_list[9], (KW,), 0.5, 3.0, ((0, 4),))
    sinks = jnp.clip(-1.0 + 3.0 * jax.random.uniform(key_list[10], (QUERY_HEADS,), jnp.float32) ** shard_levels(key_list[10], (QUERY_HEADS,), ((0, 4),), -0.2, 0.2), -1.0, 2.0).astype(jnp.bfloat16)
    w_out = scatter_about(key_list[11], (QW, D), HEAD_SIZE ** -0.5, 0.75, ((0, 4),))
    b_out = scatter_about(key_list[12], (D,), 0.3, 2.0, ((0, 4),))
    ffn_gain = jnp.clip(1.0 + 0.1 * jax.random.normal(key_list[13], (D,), jnp.float32), 0.5, 1.5).astype(jnp.bfloat16)
    w_router = scatter_about(key_list[14], (D, EXPERTS), (4 * D) ** -0.5, 0.0546875, ((0, 4),))
    b_router = scatter_about(key_list[15], (EXPERTS,), 0.2, 1.0, ((0, 4),))
    w_gate = scatter_about(key_list[16], (EXPERTS, D, FF), D ** -0.5, 0.109375, ((0, 8), (2, 4)))
    b_gate = scatter_about(key_list[17], (EXPERTS, FF), 0.2, 1.0, ((0, 8), (1, 4)))
    w_up = scatter_about(key_list[18], (EXPERTS, D, FF), D ** -0.5, 0.109375, ((0, 8), (2, 4)))
    b_up = scatter_about(key_list[19], (EXPERTS, FF), 0.2, 1.0, ((0, 8), (1, 4)))
    w_down = scatter_about(key_list[20], (EXPERTS, FF, D), (FF // 4) ** -0.5, 0.21875, ((0, 8), (1, 4)))
    b_down = scatter_about(key_list[21], (EXPERTS, D), 0.1, 0.59765625, ((0, 8),))
    cotangent = scatter_about(key_list[22], (TOKENS, D), 1.0, 6.0, ((0, 32),))
    return {"tokens": tokens, "seq_lengths": seq_lengths, "routes": routes, "attn_gain": attn_gain, "w_query": w_query, "b_query": b_query, "w_key": w_key, "b_key": b_key, "w_value": w_value, "b_value": b_value, "sinks": sinks, "w_out": w_out, "b_out": b_out, "ffn_gain": ffn_gain, "w_router": w_router, "b_router": b_router, "w_gate": w_gate, "b_gate": b_gate, "w_up": w_up, "b_up": b_up, "w_down": w_down, "b_down": b_down, "cotangent": cotangent}


EPSILON = 1e-05
ROPE_BASE = 150000.0
SWIGLU_ALPHA = 1.702
CLAMP_LIMIT = 7.0
MASKED_SCORE = -1e+30
HIGHEST = lax.Precision.HIGHEST

@jax.custom_vjp
def lower_precision(v):
    return lax.optimization_barrier(v.astype(jnp.bfloat16)).astype(jnp.float32)

@jax.custom_vjp
def low_back(v):
    return v

def low_keep(v):
    return (lower_precision(v), None)

def low_pass(kept, grad):
    return (grad,)

def back_keep(v):
    return (v, None)

def back_low(kept, grad):
    return (lower_precision(grad),)
lower_precision.defvjp(low_keep, low_pass)
low_back.defvjp(back_keep, back_low)

def hi_dot(left, right):
    return jnp.dot(left, right, precision=HIGHEST, preferred_element_type=jnp.float32)

def normalize(value_matrix, gain):
    return value_matrix * lax.rsqrt(lax.optimization_barrier(jnp.mean(value_matrix * value_matrix, axis=-1, keepdims=True)) + EPSILON) * gain

def layout(lengths, card_rows):
    seq_ends = jnp.cumsum(lengths).astype(jnp.int32)
    places = jnp.arange(card_rows, dtype=jnp.int32)
    past_end = (places[:, None] >= seq_ends[None, :]).astype(jnp.int32)
    segment_ids = lax.optimization_barrier(jnp.sum(past_end, axis=1))
    position = places - lax.optimization_barrier(jnp.sum(past_end * lengths[None, :], axis=1))
    return (segment_ids, position)

def tables(position, half_dim):
    inv_freq = jnp.exp(-jnp.log(ROPE_BASE) * jnp.arange(half_dim, dtype=jnp.float32) / half_dim)
    angles = position.astype(jnp.float32)[:, None] * inv_freq[None, :]
    return (jnp.cos(angles)[:, None, :], jnp.sin(angles)[:, None, :])

def apply_rotation(value_matrix, cosine_table, sine_table):
    half_dim = value_matrix.shape[-1] // 2
    lower_half = value_matrix[..., :half_dim]
    upper_half = value_matrix[..., half_dim:]
    return jnp.concatenate([lower_half * cosine_table - upper_half * sine_table, upper_half * cosine_table + lower_half * sine_table], axis=-1)

def attend_sinks(block_item):
    query, key_rot, value_rot, segment_ids, sink_score = block_item
    card_rows = query.shape[0]
    raw_scores = low_back(jnp.einsum('qhgd,khd->hgqk', query, key_rot, precision=HIGHEST) * HEAD_SIZE ** (-0.5))
    places = jnp.arange(card_rows, dtype=jnp.int32)
    allowed = (segment_ids[:, None] == segment_ids[None, :]) & (places[:, None] >= places[None, :])
    masked = jnp.where(allowed[None, None], raw_scores, MASKED_SCORE)
    top_score = jnp.maximum(lax.optimization_barrier(jnp.max(masked, axis=-1)), sink_score[:, :, None])
    exponent = jnp.exp(masked - top_score[..., None])
    denominator = lax.optimization_barrier(jnp.sum(exponent, axis=-1)) + jnp.exp(sink_score[:, :, None] - top_score)
    weights_att = lower_precision(exponent / denominator[..., None])
    return jnp.einsum('hgqk,khd->qhgd', weights_att, value_rot, precision=HIGHEST)

def slot_tables(routes):
    block_list = routes.shape[0] // TOKENS_PER_CARD
    flat_rows = routes.reshape(block_list, TOKENS_PER_CARD * TOP)
    one_hot = (flat_rows[:, :, None] == jnp.arange(EXPERTS, dtype=jnp.int32)[None, None, :]).astype(jnp.int32)
    before = jnp.cumsum(one_hot, axis=1) - one_hot
    pair_rank = lax.optimization_barrier(jnp.sum(before * one_hot, axis=2))
    block_ids = jnp.arange(block_list, dtype=jnp.int32)[:, None]
    pair_ids = jnp.arange(TOKENS_PER_CARD * TOP, dtype=jnp.int32)[None, :]
    column = block_ids * CAP + pair_rank
    pair_global = block_ids * (TOKENS_PER_CARD * TOP) + pair_ids
    token_global = block_ids * TOKENS_PER_CARD + pair_ids // TOP
    slot_width = block_list * CAP
    slot_token = jnp.zeros((EXPERTS, slot_width), jnp.int32).at[flat_rows, column].set(token_global)
    slot_pair = jnp.zeros((EXPERTS, slot_width), jnp.int32).at[flat_rows, column].set(pair_global)
    slot_live = jnp.zeros((EXPERTS, slot_width), jnp.float32).at[flat_rows, column].set(1.0)
    return (slot_token, slot_pair, slot_live)

def forward(x_float, params, segment_ids, position, routes, slot_token, slot_pair, slot_live):
    gain_one, wq, bq, wk, bk, wv, bv, sink_every_head, wo, bo, gain_two, wr, br, wg, bg, wu, bu, wd, bd = params
    every_row = x_float.shape[0]
    query_group = QUERY_HEADS // KEY_VALUE_HEADS
    block_list = every_row // TOKENS_PER_CARD
    norm_attn = lower_precision(normalize(x_float, gain_one))
    query_pre = low_back(hi_dot(norm_attn, wq) + bq)
    key_unrotated = low_back(hi_dot(norm_attn, wk) + bk)
    value_projected = low_back(hi_dot(norm_attn, wv) + bv)
    cosine_table, sine_table = tables(position, HEAD_SIZE // 2)
    query_matrix = lower_precision(apply_rotation(query_pre.reshape(every_row, QUERY_HEADS, HEAD_SIZE), cosine_table, sine_table))
    key_matrix = lower_precision(apply_rotation(key_unrotated.reshape(every_row, KEY_VALUE_HEADS, HEAD_SIZE), cosine_table, sine_table))
    value_matrix = lower_precision(value_projected).reshape(every_row, KEY_VALUE_HEADS, HEAD_SIZE)
    sink_block_list = jnp.broadcast_to(sink_every_head.reshape(1, KEY_VALUE_HEADS, query_group), (block_list, KEY_VALUE_HEADS, query_group))
    mixed_heads = lax.map(jax.checkpoint(attend_sinks), (query_matrix.reshape(block_list, TOKENS_PER_CARD, KEY_VALUE_HEADS, query_group, HEAD_SIZE), key_matrix.reshape(block_list, TOKENS_PER_CARD, KEY_VALUE_HEADS, HEAD_SIZE), value_matrix.reshape(block_list, TOKENS_PER_CARD, KEY_VALUE_HEADS, HEAD_SIZE), segment_ids.reshape(block_list, TOKENS_PER_CARD), sink_block_list))
    mixed_heads = lower_precision(low_back(mixed_heads.reshape(every_row, QUERY_HEADS * HEAD_SIZE)))
    resid = x_float + low_back(hi_dot(mixed_heads, wo) + bo)
    norm_ffn = lower_precision(normalize(resid, gain_two))
    logits = low_back(hi_dot(norm_ffn, wr) + br)
    one_hot = (routes[:, :, None] == jnp.arange(EXPERTS, dtype=jnp.int32)[None, None, :]).astype(jnp.float32)
    chosen = lax.optimization_barrier(jnp.sum(one_hot * logits[:, None, :], axis=-1))
    peak = lax.optimization_barrier(jnp.max(chosen, axis=-1, keepdims=True))
    gate_exp = jnp.exp(chosen - peak)
    gate_probs = gate_exp / lax.optimization_barrier(jnp.sum(gate_exp, axis=-1, keepdims=True))

    def expert(block_item):
        w_g, b_g, w_u, b_u, w_d, b_d, rows_token, rows_live = block_item
        expert_rows = low_back(norm_ffn[rows_token] * rows_live[:, None])
        gate_pre = low_back(hi_dot(expert_rows, w_g) + b_g)
        up_pre = low_back(hi_dot(expert_rows, w_u) + b_u)
        gate_soft = CLAMP_LIMIT * jnp.tanh(gate_pre / CLAMP_LIMIT)
        up_soft = CLAMP_LIMIT * jnp.tanh(up_pre / CLAMP_LIMIT)
        middle = lower_precision((up_soft + 1.0) * gate_soft * jax.nn.sigmoid(SWIGLU_ALPHA * gate_soft))
        return lower_precision(low_back(hi_dot(middle, w_d) + b_d))
    outputs = lax.map(jax.checkpoint(expert), (wg, bg, wu, bu, wd, bd, slot_token, slot_live))
    flat_out = outputs.reshape(-1, D)
    slot_weight = gate_probs.reshape(-1)[slot_pair.reshape(-1)] * slot_live.reshape(-1)
    expert_sum = jnp.zeros_like(resid).at[slot_token.reshape(-1)].add(slot_weight[:, None] * flat_out)
    return resid + expert_sum

def reference(tokens, seq_lengths, routes, attn_gain, w_query, b_query, w_key, b_key, w_value, b_value, sinks, w_out, b_out, ffn_gain, w_router, b_router, w_gate, b_gate, w_up, b_up, w_down, b_down, cotangent):
    segment_ids, position = jax.vmap(lambda lengths: layout(lengths, TOKENS_PER_CARD))(seq_lengths)
    segment_ids = segment_ids.reshape(-1)
    position = position.reshape(-1)
    slot_token, slot_pair, slot_live = slot_tables(routes)
    params = tuple((item.astype(jnp.float32) for item in (attn_gain, w_query, b_query, w_key, b_key, w_value, b_value, sinks, w_out, b_out, ffn_gain, w_router, b_router, w_gate, b_gate, w_up, b_up, w_down, b_down)))
    x_float = tokens.astype(jnp.float32)

    def run(inputs, weights):
        return forward(inputs, weights, segment_ids, position, routes, slot_token, slot_pair, slot_live)
    result, pullback = jax.vjp(run, x_float, params)
    grad_input, grad_params = pullback(cotangent.astype(jnp.float32))
    g_gain_one, g_wq, g_bq, g_wk, g_bk, g_wv, g_bv, g_sink, g_wo, g_bo, g_gain_two, g_wr, g_br, g_wg, g_bg, g_wu, g_bu, g_wd, g_bd = grad_params
    return (result.astype(jnp.bfloat16), grad_input, g_gain_one, g_wq, g_bq, g_wk, g_bk, g_wv, g_bv, g_sink, g_wo, g_bo, g_gain_two, g_wr, g_br, g_wg, g_bg, g_wu, g_bu, g_wd, g_bd)
```

```python
from functools import partial

import jax
import jax.numpy as jnp
from jax import lax
from jax.experimental import pallas as pl
from jax.experimental.pallas import tpu as pltpu
from jax.sharding import PartitionSpec as P

QUERY_HEADS = 64
KEY_VALUE_HEADS = 8
HEAD_SIZE = 64
TOP = 4
EXP_DEV = 2


EPSILON = 1e-05
ROPE_BASE = 150000.0
SWIGLU_ALPHA = 1.702
CLAMP_LIMIT = 7.0
MASKED_SCORE = -1e30


F32 = jnp.float32
BF = jnp.bfloat16
MESH = pl.DeviceIdType.MESH


def layout(lengths, card_rows):
    seq_ends = jnp.cumsum(lengths)
    places = jnp.arange(card_rows, dtype=jnp.int32)
    past_end = (places[:, None] >= seq_ends[None, :]).astype(jnp.int32)
    segment_ids = jnp.sum(past_end, axis=1)
    position = places - jnp.sum(past_end * lengths[None, :], axis=1)
    return (segment_ids, position)


def tables(position, half_dim):
    inv_freq = jnp.exp(-jnp.log(ROPE_BASE) * jnp.arange(half_dim, dtype=jnp.float32) / half_dim)
    angles = position.astype(jnp.float32)[:, None] * inv_freq[None, :]
    return (jnp.cos(angles)[:, None, :], jnp.sin(angles)[:, None, :])


def apply_rotation(value_matrix, cosine_table, sine_table):
    half_dim = value_matrix.shape[-1] // 2
    lower_half = value_matrix[..., :half_dim]
    upper_half = value_matrix[..., half_dim:]
    return jnp.concatenate(
        [
            lower_half * cosine_table - upper_half * sine_table,
            upper_half * cosine_table + lower_half * sine_table,
        ],
        axis=-1,
    )


def undo_rotation(value_matrix, cosine_table, sine_table):
    half_dim = value_matrix.shape[-1] // 2
    lower_half = value_matrix[..., :half_dim]
    upper_half = value_matrix[..., half_dim:]
    return jnp.concatenate(
        [
            lower_half * cosine_table + upper_half * sine_table,
            upper_half * cosine_table - lower_half * sine_table,
        ],
        axis=-1,
    )


def norm_scale(value_matrix):
    return lax.rsqrt(jnp.mean(value_matrix * value_matrix, axis=-1, keepdims=True) + EPSILON)


def norm_back(value_matrix, inv_scale, gain, grad_norm):
    weighted = grad_norm * gain
    grad_values = inv_scale * weighted - value_matrix * inv_scale**3 * jnp.mean(
        weighted * value_matrix, axis=-1, keepdims=True
    )
    grad_gain = jnp.sum(grad_norm * value_matrix * inv_scale, axis=0)
    return (grad_values, grad_gain)


def left_dot(left, right):
    return jnp.dot(left.T, right, preferred_element_type=jnp.float32)


def mm(spec, left, right):
    return jnp.einsum(spec, left, right, preferred_element_type=jnp.float32)


def gather_all(value):
    return lax.all_gather(value, ("fs", "ep"), axis=0, tiled=True)


def scatter_all(value):
    return lax.psum_scatter(value, ("fs", "ep"), scatter_dimension=0, tiled=True)


def gather_fs(value):
    return lax.all_gather(value, "fs", axis=0, tiled=True)


def scatter_fs(value):
    return lax.psum_scatter(value, "fs", scatter_dimension=0, tiled=True)


def spot():
    fs=lax.axis_index("fs"); ep=lax.axis_index("ep")
    return fs, ep, fs//2, fs%2, ep//2, ep%2

def greet(fs, ep, z, more=0):
    y, x, c = fs//2, fs%2, ep%2
    bar=pltpu.get_barrier_semaphore()
    def hi(f,e): pl.semaphore_signal(bar,inc=1,device_id=(f,e),device_id_type=MESH)
    hi(fs+1-2*x,ep); hi(fs+2-4*y,ep); hi(fs,ep+1-2*c)
    if more: hi(3-fs,ep)
    @pl.when(z>0)
    def _(): hi(fs,ep-2)
    @pl.when(z<3)
    def _(): hi(fs,ep+2)
    @pl.when((z>0)&(z<3))
    def _(): pl.semaphore_wait(bar,5+more)
    @pl.when((z==0)|(z==3))
    def _(): pl.semaphore_wait(bar,4+more)

def scatter_kernel(na, parts, *refs):
    ps=refs[:na]; out=refs[na]; far=refs[na+1]
    q,v1,v2,vu,vd,stg,load,s0,r0,gsem,s1,r1,s2,r2,su,ru,sd,rd,osem = refs[na+2:]
    fs,ep,y,x,z,c = spot()
    rows=ps[0].shape[2]; pr=rows//parts; half=pr//2
    items=na*4*parts
    xn=(fs+1-2*x,ep); yn=(fs+2-4*y,ep); cn=(fs,ep+1-2*c)
    A=pl.ds(0,half); B=pl.ds(half,half)
    def rem(src,dst,s,r,dev): return pltpu.make_async_remote_copy(src,dst,s,r,device_id=dev,device_id_type=MESH)
    def where(i):
        a=i//(4*parts); j=i%(4*parts); k=j//parts; part=j%parts
        zz=(k%2)*(k//2)+(1-k%2)*(3-k//2)
        return a,part,zz
    def block(i,par):
        a,part,zz=where(i)
        return a,zz*2+par,pl.ds(part*pr,pr)
    def on_array(i,f):
        if na==1: f(ps[0])
        else:
            a=i//(4*parts)
            for n in range(na):
                @pl.when(a==n)
                def _(): f(ps[n])
    def give(i,p):
        _,e,r=block(i,1-c)
        return rem(p.at[:,e,r],far.at[i],s0.at[i],r0.at[i],cn)
    def mine(i,p):
        _,e,r=block(i,c)
        return pltpu.make_async_copy(p.at[:,e,r],q.at[i],load.at[i])
    def fetch(i):
        return pltpu.make_async_copy(far.at[i],stg.at[i%2],gsem.at[i%2])
    def one(i):
        return ([rem(q.at[i,2*j+1-x,A],v1.at[i,0,j],s1.at[i,j],r1.at[i,j],xn) for j in range(2)],
                rem(q.at[i,pl.ds((1-y)*2,2),B],v1.at[i,1],s1.at[i,2],r1.at[i,2],yn))
    def two(i):
        return (rem(q.at[i,(1-y)*2+x,A],v2.at[i,0],s2.at[i,0],r2.at[i,0],yn),
                rem(q.at[i,y*2+1-x,B],v2.at[i,1],s2.at[i,1],r2.at[i,1],xn))
    def up(i): return rem(q.at[i,fs],vu.at[i],su.at[i],ru.at[i],(fs,ep+2))
    def down(i): return rem(q.at[i,fs],vd.at[i],sd.at[i],rd.at[i],(fs,ep-2))
    greet(fs,ep,z)
    @pl.loop(0,items)
    def _(i):
        on_array(i,lambda p: give(i,p).start())
        on_array(i,lambda p: mine(i,p).start())
    def valid(i): return (i>=0)&(i<items)
    def add(dst,src,n):
        for lo in range(0,n,16):
            s=pl.ds(lo,16)
            dst(s,src(s))
    def getfar(i):
        on_array(i,lambda p: give(i,p).wait_recv())
        fetch(i).start()
    getfar(0)
    @pl.loop(0,items+6)
    def _(t):
        @pl.when(t<items)
        def _():
            i=t
            @pl.when(i+1<items)
            def _(): getfar(i+1)
            fetch(i).wait()
            on_array(i,lambda p: mine(i,p).wait())
            for g in range(4):
                q[i,g]=q[i,g]+stg[i%2,g]
            a,b=one(i)
            for k in a: k.start()
            b.start()
        i=t-1
        @pl.when(valid(i))
        def _():
            a,b=one(i)
            for k in a: k.wait_recv()
            for j in range(2):
                q[i,2*j+x,A]=q[i,2*j+x,A]+v1[i,0,j]
            ta,tb=two(i)
            ta.start()
            b.wait_recv()
            for j in range(2):
                q[i,2*y+j,B]=q[i,2*y+j,B]+v1[i,1,j]
            tb.start()
        i2=t-2
        @pl.when(valid(i2))
        def _():
            ta,tb=two(i2)
            ta.wait_recv()
            q[i2,fs,A]=q[i2,fs,A]+v2[i2,0]
            tb.wait_recv()
            q[i2,fs,B]=q[i2,fs,B]+v2[i2,1]
        iu=t-2-z
        @pl.when(valid(iu))
        def _():
            _,_,zz=where(iu)
            @pl.when(zz>=z)
            def _():
                @pl.when(z>0)
                def _():
                    up(iu).wait_recv()
                    q[iu,fs]=q[iu,fs]+vu[iu]
                @pl.when(zz>z)
                def _(): up(iu).start()
        idn=t-2-(3-z)
        @pl.when(valid(idn))
        def _():
            _,_,zz=where(idn)
            @pl.when(zz<=z)
            def _():
                @pl.when(z<3)
                def _():
                    down(idn).wait_recv()
                    q[idn,fs]=q[idn,fs]+vd[idn]
                @pl.when(zz<z)
                def _(): down(idn).start()
    @pl.loop(0,items)
    def _(i):
        a,part,zz=where(i)
        @pl.when(zz==z)
        def _():
            pltpu.make_async_copy(q.at[i,fs],out.at[a,pl.ds(part*pr,pr)],osem.at[i]).start()
    @pl.loop(0,items)
    def _(i):
        a,part,zz=where(i)
        on_array(i,lambda p: give(i,p).wait_send())
        a1,b1=one(i)
        for k in a1: k.wait_send()
        b1.wait_send()
        ta,tb=two(i); ta.wait_send(); tb.wait_send()
        @pl.when(zz>z)
        def _(): up(i).wait_send()
        @pl.when(zz<z)
        def _(): down(i).wait_send()
        @pl.when(zz==z)
        def _(): pltpu.make_async_copy(q.at[i,fs],out.at[a,pl.ds(part*pr,pr)],osem.at[i]).wait()

def scatter_blocks(arrays, cid, parts=2):
    na=len(arrays); rows,width=arrays[0].shape[-2:]
    arrays=[a.reshape(4,8,rows,width) for a in arrays]
    pr=rows//parts; items=na*4*parts; half=pr//2
    any_=pl.BlockSpec(memory_space=pl.ANY)
    D=pltpu.SemaphoreType.DMA
    V=lambda *s: pltpu.VMEM(s+(width,),BF)
    out,_=pl.pallas_call(partial(scatter_kernel,na,parts),
        out_shape=[jax.ShapeDtypeStruct((na,rows,width),BF),jax.ShapeDtypeStruct((items,4,pr,width),BF)],
        in_specs=[any_]*na,out_specs=[any_,any_],
        scratch_shapes=[V(items,4,pr),V(items,2,2,half),V(items,2,half),V(items,pr),V(items,pr),V(2,4,pr),
            D((items,)),D((items,)),D((items,)),D((2,)),D((items,3)),D((items,3)),D((items,2)),D((items,2)),
            D((items,)),D((items,)),D((items,)),D((items,)),D((items,))],
        compiler_params=pltpu.CompilerParams(collective_id=cid,has_side_effects=True,vmem_limit_bytes=63*1024*1024),
        name="scatter_blocks")(*arrays)
    return out


def reduce_kernel(
    wide_n, slab_n, gw, gq, tw, tq,
    own_w, own_q, all_q, far_w, far_q, pin_w, pin_q, pout_w, pout_q, din_w, din_q, dout_w, dout_q, tot_w, tot_q,
    wload, qload, s0w, r0w, s0q, r0q, sa, ra, su, ru, sd, rd, keep, sc, rc,
):
    fs, ep, y, x, z, c = spot()
    mate = (fs, ep + 1 - 2 * c)
    rows_w, rows_q = own_w.shape[1], own_q.shape[1]
    parts = slab_n // 4
    items = wide_n + slab_n

    def rem(src, dst, s, r, dev):
        return pltpu.make_async_remote_copy(src, dst, s, r, device_id=dev, device_id_type=MESH)

    def source(s):
        return ((y + s // 2) % 2) * 2 + (x + s) % 2

    def give_w(i):
        return rem(gw.at[1 - c, i], far_w.at[i], s0w.at[i], r0w.at[i], mate)

    def give_q(s):
        return rem(gq.at[source(s), 1 - c], far_q.at[s], s0q.at[s], r0q.at[s], mate)

    def load_w(i):
        return pltpu.make_async_copy(gw.at[c, i], own_w.at[i], wload.at[i])

    def load_q(s):
        return pltpu.make_async_copy(gq.at[source(s), c], all_q.at[s], qload.at[s])

    def pass_q(s):
        dev = (source(s), ep)
        return rem(all_q.at[s], own_q.at[pl.ds(s * parts, parts)], sa.at[s], ra.at[s], dev)

    def on_item(i, f):
        @pl.when(i < wide_n)
        def _():
            f(own_w, pin_w, pout_w, din_w, dout_w, tot_w, i)

        @pl.when(i >= wide_n)
        def _():
            f(own_q, pin_q, pout_q, din_q, dout_q, tot_q, i - wide_n)

    def valid(i):
        return (i >= 0) & (i < items)

    def back(i, f):
        @pl.when(i < wide_n)
        def _():
            dst = tw.at[c, i]
            f(pltpu.make_async_copy(tot_w.at[i], dst, keep.at[i]), rem(tot_w.at[i], dst, sc.at[i], rc.at[i], mate))

        @pl.when(i >= wide_n)
        def _():
            j = i - wide_n
            dst = tq.at[source(j // parts), c, j % parts]
            f(pltpu.make_async_copy(tot_q.at[j], dst, keep.at[i]), rem(tot_q.at[j], dst, sc.at[i], rc.at[i], mate))

    greet(fs, ep, z, 1)

    @pl.loop(0, wide_n)
    def _(i):
        give_w(i).start()
        load_w(i).start()

    for s in (1, 2, 3, 0):
        give_q(s).start()
        load_q(s).start()

    @pl.loop(0, items + 4)
    def _(t):
        @pl.when(t < wide_n)
        def _():
            load_w(t).wait()
            give_w(t).wait_recv()
            own_w[t] = own_w[t] + far_w[t]

        for n, s in enumerate((1, 2, 3, 0)):

            @pl.when(t == n)
            def _():
                load_q(s).wait()
                give_q(s).wait_recv()

                @pl.loop(0, parts)
                def _(j):
                    if s:
                        all_q[s, j] = all_q[s, j] + far_q[s, j]
                    else:
                        own_q[j] = all_q[0, j] + far_q[0, j]

                if s:
                    pass_q(s).start()

        for s in (1, 2, 3):

            @pl.when(t == wide_n + s * parts)
            def _():
                pass_q(s).wait_recv()

        iu = t - z

        @pl.when(valid(iu))
        def _():
            def go(own, pin, pout, din, dout, tot, i):
                @pl.when(z == 0)
                def _():
                    rem(own.at[i], pin.at[i], su.at[iu], ru.at[iu], (fs, ep + 2)).start()

                @pl.when(z > 0)
                def _():
                    rem(own.at[i], pin.at[i], su.at[iu], ru.at[iu], (fs, ep - 2)).wait_recv()

                @pl.when((z > 0) & (z < 3))
                def _():
                    pout[i] = pin[i] + own[i]
                    rem(pout.at[i], pin.at[i], su.at[iu], ru.at[iu], (fs, ep + 2)).start()

            on_item(iu, go)

        idn = t - 3 + z

        @pl.when(valid(idn))
        def _():
            def go(own, pin, pout, din, dout, tot, i):
                @pl.when(z == 3)
                def _():
                    rem(own.at[i], din.at[i], sd.at[idn], rd.at[idn], (fs, ep - 2)).start()

                @pl.when(z < 3)
                def _():
                    rem(own.at[i], din.at[i], sd.at[idn], rd.at[idn], (fs, ep + 2)).wait_recv()

                @pl.when((z > 0) & (z < 3))
                def _():
                    dout[i] = din[i] + own[i]
                    rem(dout.at[i], din.at[i], sd.at[idn], rd.at[idn], (fs, ep - 2)).start()

            on_item(idn, go)

        last = t - 3

        @pl.when(valid(last))
        def _():
            def go(own, pin, pout, din, dout, tot, i):
                @pl.when(z == 0)
                def _():
                    tot[i] = own[i] + din[i]

                @pl.when(z == 3)
                def _():
                    tot[i] = own[i] + pin[i]

                @pl.when((z == 1) | (z == 2))
                def _():
                    tot[i] = own[i] + pin[i] + din[i]

            on_item(last, go)

            def start(a, b):
                a.start()
                b.start()

            back(last, start)

    @pl.loop(0, items)
    def _(i):
        def finish(a, b):
            a.wait()
            b.wait()

        back(i, finish)

        def go(own, pin, pout, din, dout, tot, j):
            @pl.when(z < 3)
            def _():
                rem(own.at[j], pin.at[j], su.at[i], ru.at[i], (fs, ep + 2)).wait_send()

            @pl.when(z > 0)
            def _():
                rem(own.at[j], din.at[j], sd.at[i], rd.at[i], (fs, ep - 2)).wait_send()

        on_item(i, go)

    @pl.loop(0, wide_n)
    def _(i):
        give_w(i).wait_send()

    for s in range(4):
        give_q(s).wait_send()
        if s:
            pass_q(s).wait_send()


def reduce_parts(gw, gq, cid):
    wide_n = gw.shape[1]
    parts = gq.shape[2]
    slab_n = 4 * parts
    free = pl.BlockSpec(memory_space=pl.ANY)
    D = pltpu.SemaphoreType.DMA
    W = pltpu.VMEM((wide_n,) + gw.shape[2:], BF)
    Q = pltpu.VMEM((slab_n,) + gq.shape[3:], BF)
    Q4 = pltpu.VMEM((4, parts) + gq.shape[3:], BF)
    items = wide_n + slab_n
    return pl.pallas_call(
        partial(reduce_kernel, wide_n, slab_n),
        out_shape=[jax.ShapeDtypeStruct(gw.shape, BF), jax.ShapeDtypeStruct(gq.shape, BF)],
        in_specs=[free, free],
        out_specs=[free, free],
        scratch_shapes=[W, Q, Q4, W, Q4] + [W, Q] * 5
        + [D((wide_n,)), D((4,)), D((wide_n,)), D((wide_n,)), D((4,)), D((4,)), D((4,)), D((4,))]
        + [D((items,))] * 7,
        compiler_params=pltpu.CompilerParams(
            collective_id=cid, has_side_effects=True, vmem_limit_bytes=63 * 1024 * 1024
        ),
        name="reduce_parts",
    )(gw, gq)


def nn(left, right):
    return lax.dot_general(left, right, (((1,), (0,)), ((), ())), preferred_element_type=F32)


def nt(left, right):
    return lax.dot_general(left, right, (((1,), (1,)), ((), ())), preferred_element_type=F32)


def tn(left, right):
    return lax.dot_general(left, right, (((0,), (0,)), ((), ())), preferred_element_type=F32)


def strips(total, size):
    return [(at, min(size, total - at)) for at in range(0, total, size)]


def remote(src, dst, send, recv, device):
    return pltpu.make_async_remote_copy(
        src, dst, send, recv, device_id=device, device_id_type=MESH
    )


def line_order(z, i):
    code = jnp.where(z == 0, 228, jnp.where(z == 1, 225, jnp.where(z == 2, 54, 27)))
    power = jnp.where(i == 0, 1, jnp.where(i == 1, 4, jnp.where(i == 2, 16, 64)))
    return (code // power) % 4


class Gather:
    def __init__(self, full, sems):
        self.full = full
        self.sz, self.rz, self.s1, self.r1, self.s2, self.r2, self.sc, self.rc = sems
        self.fs, self.ep, self.y, self.x, self.z, self.c = spot()
        half = full.shape[3] // 2
        self.upper, self.lower = pl.ds(0, half), pl.ds(half, half)
        self.xn = (self.fs + 1 - 2 * self.x, self.ep)
        self.yn = (self.fs + 2 - 4 * self.y, self.ep)
        self.mate = (self.fs, self.ep + 1 - 2 * self.c)

    def item(self, t):
        return t // 4, line_order(self.z, t % 4)

    def along(self, a, zz, up):
        view = self.full.at[a, self.fs, zz * 2 + self.c]
        other = (self.fs, self.ep + (2 if up else -2))
        return remote(view, view, self.sz.at[a, zz, up], self.rz.at[a, zz], other)

    def first(self, a, zz):
        e = zz * 2 + self.c
        v = self.full.at[a, self.fs, e, self.upper]
        w = self.full.at[a, self.fs, e, self.lower]
        return (
            remote(v, v, self.s1.at[a, zz, 0], self.r1.at[a, zz, 0], self.xn),
            remote(w, w, self.s1.at[a, zz, 1], self.r1.at[a, zz, 1], self.yn),
        )

    def second(self, a, zz):
        e = zz * 2 + self.c
        v = self.full.at[a, pl.ds(self.y * 2, 2), e, self.upper]
        out = [remote(v, v, self.s2.at[a, zz, 0], self.r2.at[a, zz, 0], self.yn)]
        for j in range(2):
            w = self.full.at[a, 2 * j + self.x, e, self.lower]
            out.append(remote(w, w, self.s2.at[a, zz, 1 + j], self.r2.at[a, zz, 1 + j], self.xn))
        return out

    def across(self, a, zz, e):
        v = self.full.at[a, :, zz * 2 + e]
        return remote(v, v, self.sc.at[a, zz], self.rc.at[a, zz], self.mate)

    def step1(self, t):
        @pl.when(t < 8)
        def _():
            a, zz = self.item(t)

            @pl.when(zz != self.z)
            def _():
                self.along(a, zz, 0).wait_recv()

            @pl.when((zz <= self.z) & (self.z < 3))
            def _():
                self.along(a, zz, 1).start()

            @pl.when((zz >= self.z) & (self.z > 0))
            def _():
                self.along(a, zz, 0).start()

            for copy in self.first(a, zz):
                copy.start()

    def step2(self, t):
        @pl.when(t < 8)
        def _():
            a, zz = self.item(t)
            one, two = self.first(a, zz)
            copies = self.second(a, zz)
            one.wait_recv()
            copies[0].start()
            two.wait_recv()
            copies[1].start()
            copies[2].start()

    def step3(self, t):
        @pl.when(t < 8)
        def _():
            a, zz = self.item(t)
            for copy in self.second(a, zz):
                copy.wait_recv()
            self.across(a, zz, self.c).start()

    def step4(self, t):
        a, zz = self.item(t)
        self.across(a, zz, 1 - self.c).wait_recv()

    def finish(self):
        @pl.loop(0, 8)
        def _(t):
            a, zz = self.item(t)
            self.across(a, zz, self.c).wait_send()
            for copy in (*self.first(a, zz), *self.second(a, zz)):
                copy.wait_send()

            @pl.when((zz <= self.z) & (self.z < 3))
            def _():
                self.along(a, zz, 1).wait_send()

            @pl.when((zz >= self.z) & (self.z > 0))
            def _():
                self.along(a, zz, 0).wait_send()


def experts_kernel(
    cap, width,
    n_own, g_own, wg_hbm, wu_hbm, wd_hbm, bg_ref, bu_ref, bd_ref,
    full, out_hbm, row_hbm, xs_hbm, eg_hbm, mid_hbm, ug_hbm, gg_hbm, cu_hbm, cg_hbm,
    sum_g, sum_u, sum_d,
    wg_ref, wu_ref, wd_ref, bin_, meta, pmat, gates, xs, res, mid, ugb, ggb, cub, cgb, dots, stage,
    w_sem, own_sem, in_sem, st_sem, save_sem,
    *sems,
):
    gather = Gather(full, sems)
    fs, ep, z = gather.fs, gather.ep, gather.z
    card_rows, wpad = bin_.shape[1:]
    tail = wpad - 128
    off = width - tail
    first = jnp.where(fs == 0, 1.0, 0.0).astype(F32)
    nb = 8
    rows = nb * cap
    weights = [
        pltpu.make_async_copy(src, dst, w_sem.at[n])
        for n, (src, dst) in enumerate(((wg_hbm, wg_ref), (wu_hbm, wu_ref), (wd_hbm, wd_ref)))
    ]
    keep = [
        pltpu.make_async_copy(src, full.at[a, fs, ep], own_sem.at[a])
        for a, src in enumerate((n_own, g_own))
    ]
    for copy in keep + weights:
        copy.start()
    greet(fs, ep, z)
    for copy in keep:
        copy.wait()
    gather.step1(0)
    gather.step2(0)
    gather.step1(1)
    gather.step3(0)
    gather.step2(1)
    gather.step1(2)
    for copy in weights:
        copy.wait()

    def load(a, zz, b, slot):
        return pltpu.make_async_copy(full.at[a, b // 2, zz * 2 + b % 2], bin_.at[slot], in_sem.at[slot])

    def save(src, dst, k, i, n):
        return pltpu.make_async_copy(
            src.at[k], dst.at[k, pl.ds(pl.multiple_of(i * rows, 16), rows)], save_sem.at[n, k]
        )

    def fetch(src, dst, k, i, n):
        return pltpu.make_async_copy(
            src.at[k, pl.ds(pl.multiple_of(i * rows, 16), rows)], dst.at[k], save_sem.at[n, k]
        )

    def spread(a, i, zz, prepare):
        load(a, zz, 0, 0).start()

        @pl.loop(0, nb)
        def _(b):
            slot = lax.rem(b, 2)

            @pl.when(b + 1 < nb)
            def _():
                load(a, zz, b + 1, 1 - slot).start()

            load(a, zz, b, slot).wait()
            at = pl.ds(pl.multiple_of(b * cap, 16), cap)
            if prepare:
                meta[...] = jnp.transpose(bin_[slot, :, tail:].astype(F32))
                for k in range(2):
                    e = ep * 2 + k
                    place = meta[pl.ds(off + e, 1), :]
                    gate = meta[pl.ds(off + 16 + e, 1), :] + meta[pl.ds(off + 32 + e, 1), :]
                    hit = lax.broadcasted_iota(jnp.int32, (cap, card_rows), 0).astype(F32) == place
                    pmat[i, b, k * cap : (k + 1) * cap, :] = jnp.where(hit, 1.0, 0.0).astype(BF)
                    gates[i, k, at, :] = jnp.sum(jnp.where(hit, gate, 0.0), axis=1, keepdims=True)
            pick = pmat[i, b]
            for lo, n in strips(width, 768):
                got = nn(pick, bin_[slot, :, lo : lo + n]).astype(BF)
                xs[0, at, lo : lo + n] = got[:cap]
                xs[1, at, lo : lo + n] = got[cap:]

    def combine(dst, i, zz, with_dots):
        column = lax.broadcasted_iota(jnp.int32, (cap, wpad - width), 1)

        def store(b, slot):
            return pltpu.make_async_copy(
                stage.at[slot], dst.at[b // 2, zz * 2 + b % 2], st_sem.at[slot]
            )

        @pl.loop(0, nb)
        def _(b):
            slot = lax.rem(b, 2)

            @pl.when(b >= 2)
            def _():
                store(b - 2, slot).wait()

            pick = pmat[i, b]
            at = pl.ds(pl.multiple_of(b * cap, 16), cap)
            for lo, n in strips(width, 768):
                both = jnp.concatenate([res[0, at, lo : lo + n], res[1, at, lo : lo + n]], axis=0)
                stage[slot, :, lo : lo + n] = tn(pick, both).astype(BF)
            if with_dots:
                own_dots = jnp.concatenate(
                    [
                        jnp.where(column == ep * 2 + k, dots[k, at, :], 0.0).astype(BF)
                        for k in range(2)
                    ],
                    axis=0,
                )
                stage[slot, :, width:] = tn(pick, own_dots).astype(BF)
            else:
                stage[slot, :, width:] = jnp.zeros((card_rows, wpad - width), BF)
            store(b, slot).start()

        for b in (nb - 2, nb - 1):
            store(b, b % 2).wait()

    @pl.loop(0, 4)
    def _(i):
        zz = line_order(z, i)
        gather.step4(i)
        gather.step1(i + 3)
        spread(0, i, zz, True)
        for k in range(2):
            save(xs, xs_hbm, k, i, 0).start()
        gather.step2(i + 2)

        @pl.loop(0, 2)
        def _(k):
            @pl.when(k == 1)
            def _():
                gather.step3(i + 1)

            gate_soft = CLAMP_LIMIT * jnp.tanh((nt(xs[k], wg_ref[k]) + bg_ref[k]) * (1.0 / CLAMP_LIMIT))
            up_soft = CLAMP_LIMIT * jnp.tanh((nt(xs[k], wu_ref[k]) + bu_ref[k]) * (1.0 / CLAMP_LIMIT))
            sig = jax.nn.sigmoid(SWIGLU_ALPHA * gate_soft)
            glu = gate_soft * sig
            mid[k] = ((up_soft + 1.0) * glu).astype(BF)
            cub[k] = (glu * (1.0 - (up_soft * (1.0 / CLAMP_LIMIT)) ** 2)).astype(BF)
            cgb[k] = (
                (up_soft + 1.0)
                * (sig + SWIGLU_ALPHA * glu * (1.0 - sig))
                * (1.0 - (gate_soft * (1.0 / CLAMP_LIMIT)) ** 2)
            ).astype(BF)
            save(mid, mid_hbm, k, i, 1).start()
            save(cub, cu_hbm, k, i, 2).start()
            save(cgb, cg_hbm, k, i, 3).start()
            for lo, n in strips(width, 768):
                part = nn(mid[k], wd_ref[k, :, lo : lo + n]) + first * bd_ref[k, :, lo : lo + n]
                res[k, :, lo : lo + n] = (part * gates[i, k]).astype(BF)

        combine(out_hbm, i, zz, False)
        for k in range(2):
            save(xs, xs_hbm, k, i, 0).wait()
            save(mid, mid_hbm, k, i, 1).wait()
            save(cub, cu_hbm, k, i, 2).wait()
            save(cgb, cg_hbm, k, i, 3).wait()

    sum_g[...] = jnp.zeros_like(sum_g)
    sum_u[...] = jnp.zeros_like(sum_u)
    sum_d[...] = jnp.zeros_like(sum_d)

    @pl.loop(0, 4)
    def _(i):
        zz = line_order(z, i)
        for k in range(2):
            fetch(mid_hbm, mid, k, i, 1).start()
            fetch(cu_hbm, cub, k, i, 2).start()
            fetch(cg_hbm, cgb, k, i, 3).start()
        gather.step4(i + 4)
        gather.step1(i + 7)
        spread(1, i, zz, False)
        gather.step2(i + 6)
        ones = jnp.ones((8, rows), BF)

        @pl.loop(0, 2)
        def _(k):
            @pl.when(k == 1)
            def _():
                gather.step3(i + 5)

            fetch(mid_hbm, mid, k, i, 1).wait()
            fetch(cu_hbm, cub, k, i, 2).wait()
            fetch(cg_hbm, cgb, k, i, 3).wait()
            plain = nt(xs[k], wd_ref[k])
            gate = gates[i, k]
            grad = plain * gate
            dots[k] = jnp.sum(plain * mid[k].astype(F32), axis=1, keepdims=True) + first * jnp.sum(
                xs[k].astype(F32) * bd_ref[k], axis=1, keepdims=True
            )
            ugb[k] = (grad * cub[k].astype(F32)).astype(BF)
            ggb[k] = (grad * cgb[k].astype(F32)).astype(BF)
            xs[k] = (xs[k].astype(F32) * gate).astype(BF)
            save(xs, eg_hbm, k, i, 0).start()
            save(ugb, ug_hbm, k, i, 4).start()
            save(ggb, gg_hbm, k, i, 5).start()
            sum_g[k] += nn(ones, ggb[k])
            sum_u[k] += nn(ones, ugb[k])
            sum_d[k] += nn(ones, xs[k])
            for lo, n in strips(width, 768):
                part = nn(ggb[k], wg_ref[k, :, lo : lo + n]) + nn(ugb[k], wu_ref[k, :, lo : lo + n])
                res[k, :, lo : lo + n] = part.astype(BF)

        combine(row_hbm, i, zz, True)
        for k in range(2):
            save(xs, eg_hbm, k, i, 0).wait()
            save(ugb, ug_hbm, k, i, 4).wait()
            save(ggb, gg_hbm, k, i, 5).wait()

    gather.finish()


def experts(n_own, g_own, wg_t, b_gate, wu_t, b_up, w_down, b_down, cap, cid):
    rows, wpad = n_own.shape
    ff, width = w_down.shape[1:]
    n, m = 32 * cap, 8 * cap
    free = pl.BlockSpec(memory_space=pl.ANY)
    near = pl.BlockSpec(memory_space=pltpu.VMEM)
    shape = jax.ShapeDtypeStruct
    V = pltpu.VMEM
    D = pltpu.SemaphoreType.DMA
    biases = [b.astype(F32)[:, None] for b in (b_gate, b_up, b_down)]
    out = pl.pallas_call(
        partial(experts_kernel, cap, width),
        out_shape=[shape((2, 4, 8, rows, wpad), BF)]
        + [shape((4, 8, rows, wpad), BF)] * 2
        + [shape((2, n, width), BF)] * 2
        + [shape((2, n, ff), BF)] * 5
        + [shape((2, 8, ff), F32)] * 2
        + [shape((2, 8, width), F32)],
        in_specs=[free] * 5 + [near] * 3,
        out_specs=[free] * 10 + [near] * 3,
        scratch_shapes=[
            V((2, ff, width), BF), V((2, ff, width), BF), V((2, ff, width), BF),
            V((2, rows, wpad), BF), V((128, rows), F32), V((4, 8, 2 * cap, rows), BF),
            V((4, 2, m, 1), F32), V((2, m, width), BF), V((2, m, width), BF),
            V((2, m, ff), BF), V((2, m, ff), BF), V((2, m, ff), BF), V((2, m, ff), BF), V((2, m, ff), BF),
            V((2, m, 1), F32), V((2, rows, wpad), BF),
            D((3,)), D((2,)), D((2,)), D((2,)), D((6, 2)),
            D((2, 4, 2)), D((2, 4)), D((2, 4, 2)), D((2, 4, 2)), D((2, 4, 3)), D((2, 4, 3)), D((2, 4)), D((2, 4)),
        ],
        compiler_params=pltpu.CompilerParams(
            collective_id=cid, has_side_effects=True, vmem_limit_bytes=63 * 1024 * 1024
        ),
        cost_estimate=pl.CostEstimate(
            flops=24 * n * width * ff, bytes_accessed=300_000_000, transcendentals=6 * n * ff
        ),
        name="experts",
    )(n_own, g_own, wg_t, wu_t, w_down, *biases)
    return (*out[1:8], *(total[:, 0] for total in out[10:]))


def this_slice(
    tokens,
    seq_lengths,
    routes,
    attn_gain,
    w_query,
    b_query,
    w_key,
    b_key,
    w_value,
    b_value,
    sinks,
    w_out,
    b_out,
    ffn_gain,
    w_router,
    b_router,
    w_gate,
    b_gate,
    w_up,
    b_up,
    w_down,
    b_down,
    cotangent,
):
    rows, width = tokens.shape
    fs_size = lax.axis_size("fs")
    ep_size = lax.axis_size("ep")
    my_fs = lax.axis_index("fs")
    my_ep = lax.axis_index("ep")
    blocks = fs_size * ep_size
    expert_count = EXP_DEV * ep_size
    capacity = 3 * rows * TOP // (2 * expert_count)
    shard = w_query.shape[0]
    kv_heads = KEY_VALUE_HEADS // fs_size
    group = QUERY_HEADS // KEY_VALUE_HEADS
    q_cols = kv_heads * group * HEAD_SIZE
    kv_cols = kv_heads * HEAD_SIZE

    spare = (-width) % 128
    small = jnp.concatenate(
        [attn_gain, ffn_gain, b_out, w_router.reshape(-1), b_router, seq_lengths[0].astype(BF)]
    )
    extra = -(-small.shape[0] // (16 * width)) * 16
    small = jnp.pad(small, (0, extra * width - small.shape[0])).reshape(extra, width)
    packed = lax.all_gather(jnp.concatenate([tokens, small], axis=0), "fs", axis=0)
    x_group = packed[:, :rows].reshape(fs_size * rows, width).astype(F32)
    small = packed[:, rows:].reshape(fs_size, -1)
    gain_one = small[:, :shard].reshape(-1).astype(F32)
    gain_two = small[:, shard : 2 * shard].reshape(-1).astype(F32)
    bo = small[:, 2 * shard : 3 * shard].reshape(-1).astype(F32)
    at = (3 + expert_count) * shard
    wr = small[:, 3 * shard : at].reshape(width, expert_count)
    br = small[:, at : at + b_router.shape[0]].reshape(-1).astype(F32)
    at += b_router.shape[0]
    lengths = small[:, at : at + seq_lengths.shape[1]].astype(jnp.int32)

    w_qkv = jnp.concatenate(
        [
            w_query.reshape(shard, fs_size, q_cols),
            w_key.reshape(shard, fs_size, kv_cols),
            w_value.reshape(shard, fs_size, kv_cols),
        ],
        axis=2,
    )
    w_qkv = lax.all_to_all(w_qkv, "fs", split_axis=1, concat_axis=0, tiled=True)
    w_qkv = w_qkv.reshape(width, q_cols + 2 * kv_cols)
    b_qkv = jnp.concatenate([b_query, b_key, b_value]).astype(jnp.float32)
    sink_score = sinks.astype(jnp.float32).reshape(1, kv_heads, group, 1)

    x_float = tokens.astype(jnp.float32)
    scale_one = norm_scale(x_float)
    norm_attn = (x_group * norm_scale(x_group) * gain_one).astype(jnp.bfloat16)
    segment_ids, position = jax.vmap(lambda own: layout(own, rows))(lengths)
    cosine_table, sine_table = tables(position.reshape(-1), HEAD_SIZE // 2)
    qkv = jnp.dot(norm_attn, w_qkv, preferred_element_type=jnp.float32) + b_qkv
    many = fs_size * rows
    heads = kv_heads * group
    query = apply_rotation(
        qkv[:, :q_cols].reshape(many, heads, HEAD_SIZE), cosine_table, sine_table
    ).astype(jnp.bfloat16)
    query = query.reshape(fs_size, rows, kv_heads, group, HEAD_SIZE)
    key = apply_rotation(
        qkv[:, q_cols : q_cols + kv_cols].reshape(many, kv_heads, HEAD_SIZE),
        cosine_table,
        sine_table,
    ).astype(jnp.bfloat16)
    key = key.reshape(fs_size, rows, kv_heads, HEAD_SIZE)
    value = qkv[:, q_cols + kv_cols :].astype(jnp.bfloat16)
    value = value.reshape(fs_size, rows, kv_heads, HEAD_SIZE)
    places = jnp.arange(rows, dtype=jnp.int32)
    allowed = (segment_ids[:, :, None] == segment_ids[:, None, :]) & (
        places[:, None] >= places[None, :]
    )
    scores = mm("bqhgd,bkhd->bhgqk", query, key) * HEAD_SIZE ** (-0.5)
    masked = jnp.where(allowed[:, None, None], scores, MASKED_SCORE)
    top_score = jnp.maximum(jnp.max(masked, axis=-1), sink_score)
    exponent = jnp.exp(masked - top_score[..., None])
    sink_exp = jnp.exp(sink_score - top_score)
    denominator = jnp.sum(exponent, axis=-1) + sink_exp
    probs = exponent / denominator[..., None]
    sink_prob = sink_exp / denominator
    probs_b = probs.astype(jnp.bfloat16)
    mixed = mm("bhgqk,bkhd->bqhgd", probs_b, value).astype(jnp.bfloat16)
    mixed = mixed.reshape(many, q_cols)
    out_part = jnp.dot(mixed, w_out, preferred_element_type=jnp.float32)
    resid = x_float + scatter_fs(out_part.astype(jnp.bfloat16)).astype(jnp.float32) + bo
    scale_two = norm_scale(resid)
    norm_ffn = (resid * scale_two * gain_two).astype(jnp.bfloat16)

    logits = jnp.dot(norm_ffn, wr, preferred_element_type=F32) + br
    one_hot = (routes[:, :, None] == jnp.arange(expert_count, dtype=jnp.int32)).astype(F32)
    member = jnp.sum(one_hot, axis=1)
    peak = jnp.max(jnp.where(member > 0, logits, MASKED_SCORE), axis=-1, keepdims=True)
    gate_exp = jnp.where(member > 0, jnp.exp(logits - peak), 0.0)
    gates_here = gate_exp / jnp.sum(gate_exp, axis=-1, keepdims=True)
    place = jnp.where(member > 0, jnp.cumsum(member, axis=0) - member, -1.0)
    gate_high = lax.reduce_precision(gates_here, 8, 7)
    block = jnp.concatenate(
        [norm_ffn]
        + [v.astype(BF) for v in (place, gate_high, gates_here - gate_high)]
        + [jnp.zeros((rows, spare - 3 * expert_count), BF)],
        axis=1,
    )
    wg_t = jnp.swapaxes(w_gate, 1, 2)
    wu_t = jnp.swapaxes(w_up, 1, 2)
    (
        out_part,
        row_part,
        x_slots,
        expert_grad,
        middle,
        up_grad,
        gate_grad_pre,
        grad_b_gate,
        grad_b_up,
        grad_b_down,
    ) = experts(
        block,
        jnp.pad(cotangent, ((0, 0), (0, spare))),
        wg_t,
        b_gate,
        wu_t,
        b_up,
        w_down,
        b_down,
        capacity,
        1,
    )
    sums = scatter_blocks([out_part, row_part], 2)
    block_out = resid + sums[0, :, :width].astype(F32)
    grad_w_down = mm("erf,erd->efd", middle, expert_grad)
    grad_w_gate = jnp.swapaxes(mm("erf,erd->efd", gate_grad_pre, x_slots), 1, 2)
    grad_w_up = jnp.swapaxes(mm("erf,erd->efd", up_grad, x_slots), 1, 2)
    row_sum = sums[1].astype(F32)
    gate_grad = row_sum[:, width : width + expert_count]
    logit_grad = gates_here * (
        gate_grad - jnp.sum(gates_here * gate_grad, axis=-1, keepdims=True)
    )
    logit_grad = logit_grad.astype(jnp.bfloat16)
    grad_br = jnp.sum(logit_grad, axis=0, dtype=jnp.float32)
    grad_wr = left_dot(norm_ffn, logit_grad)
    norm_ffn_grad = row_sum[:, :width] + jnp.dot(
        logit_grad, wr.T, preferred_element_type=jnp.float32
    )
    resid_norm_grad, grad_gain_two = norm_back(resid, scale_two, gain_two, norm_ffn_grad)
    resid_grad = cotangent.astype(jnp.float32) + resid_norm_grad

    branch_grad = gather_fs(resid_grad.astype(jnp.bfloat16))
    grad_bo = jnp.sum(branch_grad, axis=0, dtype=jnp.float32)
    mixed_grad = mm("td,fd->tf", branch_grad, w_out).astype(jnp.bfloat16)
    mixed_grad = mixed_grad.reshape(fs_size, rows, kv_heads, group, HEAD_SIZE)
    grad_wo = left_dot(mixed, branch_grad)
    grad_probs = mm("bqhgd,bkhd->bhgqk", mixed_grad, value)
    value_grad = mm("bhgqk,bqhgd->bkhd", probs_b, mixed_grad)
    row_delta = jnp.sum(probs * grad_probs, axis=-1)
    score_grad = (probs * (grad_probs - row_delta[..., None])).astype(jnp.bfloat16)
    query_grad = mm("bhgqk,bkhd->bqhgd", score_grad, key) * HEAD_SIZE ** (-0.5)
    key_grad = mm("bhgqk,bqhgd->bkhd", score_grad, query) * HEAD_SIZE ** (-0.5)
    grad_sink = -jnp.sum(sink_prob * row_delta, axis=(0, 3)).reshape(-1)
    query_pre_grad = undo_rotation(
        query_grad.reshape(many, heads, HEAD_SIZE), cosine_table, sine_table
    ).reshape(many, q_cols)
    key_pre_grad = undo_rotation(
        key_grad.reshape(many, kv_heads, HEAD_SIZE), cosine_table, sine_table
    ).reshape(many, kv_cols)
    qkv_grad = jnp.concatenate(
        [query_pre_grad, key_pre_grad, value_grad.reshape(many, kv_cols)], axis=1
    ).astype(jnp.bfloat16)
    grad_b_qkv = jnp.sum(qkv_grad, axis=0, dtype=jnp.float32)
    norm_attn_grad = scatter_fs(
        mm("tf,df->td", qkv_grad, w_qkv).astype(jnp.bfloat16)
    ).astype(jnp.float32)
    input_norm_grad, grad_gain_one = norm_back(x_float, scale_one, gain_one, norm_attn_grad)
    grad_tokens = resid_grad + input_norm_grad
    by_shard = jnp.concatenate(
        [
            grad_wr.reshape(fs_size, -1),
            grad_gain_one.reshape(fs_size, -1),
            grad_gain_two.reshape(fs_size, -1),
            grad_br.reshape(fs_size, -1),
        ],
        axis=1,
    ).astype(BF)
    own = jnp.concatenate(
        [grad_b_qkv, grad_sink, lax.dynamic_slice_in_dim(grad_bo, my_fs * shard, shard)]
    ).astype(BF)
    cols = q_cols + 2 * kv_cols
    slab_rows, slab_part = 768, 128
    wide_rows, wide_part = 1056, 48
    spare_q = (slab_rows - shard) * cols - by_shard.shape[1]
    gq = jnp.concatenate(
        [
            left_dot(norm_attn, qkv_grad).astype(BF).reshape(fs_size, shard, cols),
            jnp.pad(by_shard, ((0, 0), (0, spare_q))).reshape(fs_size, slab_rows - shard, cols),
        ],
        axis=1,
    ).reshape(fs_size, 2, slab_rows // (2 * slab_part), slab_part, cols)
    spare_w = (wide_rows - q_cols) * width - own.shape[0]
    gw = jnp.concatenate(
        [grad_wo.astype(BF), jnp.pad(own, (0, spare_w)).reshape(wide_rows - q_cols, width)], axis=0
    ).reshape(2, wide_rows // (2 * wide_part), wide_part, width)
    tw, tq = reduce_parts(gw, gq, 3)
    tw = tw.reshape(wide_rows, width)
    tq = tq.reshape(fs_size, slab_rows, cols)
    sum_wo = tw[:q_cols].astype(F32)
    own = tw[q_cols:].reshape(-1)[: own.shape[0]].astype(F32)
    sums_q = tq[:, :shard].astype(F32).transpose(1, 0, 2)
    sum_wq = sums_q[:, :, :q_cols].reshape(shard, -1)
    sum_wk = sums_q[:, :, q_cols : q_cols + kv_cols].reshape(shard, -1)
    sum_wv = sums_q[:, :, q_cols + kv_cols :].reshape(shard, -1)
    by_shard = jnp.sum(
        tq[:, shard:].reshape(fs_size, -1)[:, : by_shard.shape[1]].astype(F32), axis=0
    )
    sum_wr = by_shard[: shard * expert_count].reshape(shard, expert_count)
    rest = by_shard[shard * expert_count :]
    sum_b = own[:cols]
    return (
        block_out.astype(jnp.bfloat16),
        grad_tokens,
        rest[:shard],
        sum_wq,
        sum_b[:q_cols],
        sum_wk,
        sum_b[q_cols : q_cols + kv_cols],
        sum_wv,
        sum_b[q_cols + kv_cols :],
        own[q_cols + 2 * kv_cols : q_cols + 2 * kv_cols + heads],
        sum_wo,
        own[q_cols + 2 * kv_cols + heads :],
        rest[shard : 2 * shard],
        sum_wr,
        rest[2 * shard :],
        grad_w_gate,
        grad_b_gate,
        grad_w_up,
        grad_b_up,
        grad_w_down,
        grad_b_down,
    )


def any_slice(
    tokens,
    seq_lengths,
    routes,
    attn_gain,
    w_query,
    b_query,
    w_key,
    b_key,
    w_value,
    b_value,
    sinks,
    w_out,
    b_out,
    ffn_gain,
    w_router,
    b_router,
    w_gate,
    b_gate,
    w_up,
    b_up,
    w_down,
    b_down,
    cotangent,
):
    rows, width = tokens.shape
    fs_size = lax.axis_size("fs")
    ep_size = lax.axis_size("ep")
    my_fs = lax.axis_index("fs")
    my_ep = lax.axis_index("ep")
    blocks = fs_size * ep_size
    expert_count = EXP_DEV * ep_size
    capacity = 3 * rows * TOP // (2 * expert_count)
    shard = w_query.shape[0]
    kv_heads = KEY_VALUE_HEADS // fs_size
    group = QUERY_HEADS // KEY_VALUE_HEADS
    q_cols = kv_heads * group * HEAD_SIZE
    kv_cols = kv_heads * HEAD_SIZE

    packed = jnp.concatenate(
        [attn_gain, ffn_gain, b_out, w_router.reshape(-1), b_router]
    )
    packed = lax.all_gather(packed, "fs", axis=0)
    gain_one = packed[:, :shard].reshape(-1).astype(jnp.float32)
    gain_two = packed[:, shard : 2 * shard].reshape(-1).astype(jnp.float32)
    bo = packed[:, 2 * shard : 3 * shard].reshape(-1).astype(jnp.float32)
    wr = packed[:, 3 * shard : (3 + expert_count) * shard].reshape(width, expert_count)
    br = packed[:, (3 + expert_count) * shard :].reshape(-1).astype(jnp.float32)
    whole_numbers = gather_all(
        jnp.concatenate([routes.reshape(-1), seq_lengths.reshape(-1)])[None]
    )
    routes_all = whole_numbers[:, : rows * TOP].reshape(blocks, rows, TOP)
    lengths_all = whole_numbers[:, rows * TOP :]
    lengths = lax.dynamic_index_in_dim(
        lengths_all.reshape(fs_size, ep_size, -1), my_ep, 1, keepdims=False
    )
    g_all = gather_all(cotangent)

    w_qkv = jnp.concatenate(
        [
            w_query.reshape(shard, fs_size, q_cols),
            w_key.reshape(shard, fs_size, kv_cols),
            w_value.reshape(shard, fs_size, kv_cols),
        ],
        axis=2,
    )
    w_qkv = lax.all_to_all(w_qkv, "fs", split_axis=1, concat_axis=0, tiled=True)
    w_qkv = w_qkv.reshape(width, q_cols + 2 * kv_cols)
    b_qkv = jnp.concatenate([b_query, b_key, b_value]).astype(jnp.float32)
    sink_score = sinks.astype(jnp.float32).reshape(1, kv_heads, group, 1)

    x_float = tokens.astype(jnp.float32)
    scale_one = norm_scale(x_float)
    norm_attn = gather_fs((x_float * scale_one * gain_one).astype(jnp.bfloat16))
    segment_ids, position = jax.vmap(lambda own: layout(own, rows))(lengths)
    cosine_table, sine_table = tables(position.reshape(-1), HEAD_SIZE // 2)
    qkv = jnp.dot(norm_attn, w_qkv, preferred_element_type=jnp.float32) + b_qkv
    many = fs_size * rows
    heads = kv_heads * group
    query = apply_rotation(
        qkv[:, :q_cols].reshape(many, heads, HEAD_SIZE), cosine_table, sine_table
    ).astype(jnp.bfloat16)
    query = query.reshape(fs_size, rows, kv_heads, group, HEAD_SIZE)
    key = apply_rotation(
        qkv[:, q_cols : q_cols + kv_cols].reshape(many, kv_heads, HEAD_SIZE),
        cosine_table,
        sine_table,
    ).astype(jnp.bfloat16)
    key = key.reshape(fs_size, rows, kv_heads, HEAD_SIZE)
    value = qkv[:, q_cols + kv_cols :].astype(jnp.bfloat16)
    value = value.reshape(fs_size, rows, kv_heads, HEAD_SIZE)
    places = jnp.arange(rows, dtype=jnp.int32)
    allowed = (segment_ids[:, :, None] == segment_ids[:, None, :]) & (
        places[:, None] >= places[None, :]
    )
    scores = mm("bqhgd,bkhd->bhgqk", query, key) * HEAD_SIZE ** (-0.5)
    masked = jnp.where(allowed[:, None, None], scores, MASKED_SCORE)
    top_score = jnp.maximum(jnp.max(masked, axis=-1), sink_score)
    exponent = jnp.exp(masked - top_score[..., None])
    sink_exp = jnp.exp(sink_score - top_score)
    denominator = jnp.sum(exponent, axis=-1) + sink_exp
    probs = exponent / denominator[..., None]
    sink_prob = sink_exp / denominator
    probs_b = probs.astype(jnp.bfloat16)
    mixed = mm("bhgqk,bkhd->bqhgd", probs_b, value).astype(jnp.bfloat16)
    mixed = mixed.reshape(many, q_cols)
    out_part = jnp.dot(mixed, w_out, preferred_element_type=jnp.float32)
    resid = x_float + scatter_fs(out_part.astype(jnp.bfloat16)).astype(jnp.float32) + bo
    scale_two = norm_scale(resid)
    norm_ffn = (resid * scale_two * gain_two).astype(jnp.bfloat16)

    n_all = gather_all(norm_ffn)
    logits = jnp.dot(n_all, wr, preferred_element_type=jnp.float32) + br
    logits = logits.reshape(blocks, rows, expert_count)
    one_hot = (
        routes_all[:, :, :, None] == jnp.arange(expert_count, dtype=jnp.int32)
    ).astype(jnp.float32)
    member = jnp.sum(one_hot, axis=2)
    peak = jnp.max(jnp.where(member > 0, logits, MASKED_SCORE), axis=-1, keepdims=True)
    gate_exp = jnp.where(member > 0, jnp.exp(logits - peak), 0.0)
    gates = gate_exp / jnp.sum(gate_exp, axis=-1, keepdims=True)
    own_member = lax.dynamic_slice_in_dim(member, my_ep * EXP_DEV, EXP_DEV, axis=2)
    own_gates = lax.dynamic_slice_in_dim(gates, my_ep * EXP_DEV, EXP_DEV, axis=2)
    rank = jnp.cumsum(own_member, axis=1) - own_member
    slots = jnp.arange(capacity, dtype=jnp.float32)
    pick = (rank.transpose(0, 2, 1)[:, :, None, :] == slots[:, None]) & (
        own_member.transpose(0, 2, 1)[:, :, None, :] > 0
    )
    pick_b = pick.astype(jnp.bfloat16)
    slot_gate = jnp.sum(
        jnp.where(pick, own_gates.transpose(0, 2, 1)[:, :, None, :], 0.0), axis=-1
    )
    slot_gate = slot_gate.transpose(1, 0, 2).reshape(EXP_DEV, blocks * capacity, 1)

    def spread(full):
        parts = mm("bekt,btd->ebkd", pick_b, full.reshape(blocks, rows, -1))
        return parts.astype(jnp.bfloat16).reshape(EXP_DEV, blocks * capacity, -1)

    def combine(parts):
        parts = parts.reshape(EXP_DEV, blocks, capacity, -1)
        return mm("bekt,ebkd->btd", pick_b, parts).reshape(blocks * rows, -1)

    x_slots = spread(n_all)
    g_slots = spread(g_all)
    gate_pre = mm("erd,edf->erf", x_slots, w_gate) + b_gate.astype(jnp.float32)[:, None]
    up_pre = mm("erd,edf->erf", x_slots, w_up) + b_up.astype(jnp.float32)[:, None]
    gate_soft = CLAMP_LIMIT * jnp.tanh(gate_pre / CLAMP_LIMIT)
    up_soft = CLAMP_LIMIT * jnp.tanh(up_pre / CLAMP_LIMIT)
    gate_sig = jax.nn.sigmoid(SWIGLU_ALPHA * gate_soft)
    glu_part = gate_soft * gate_sig
    middle = ((up_soft + 1.0) * glu_part).astype(jnp.bfloat16)
    first = (my_fs == 0).astype(jnp.float32)
    down_bias = b_down.astype(jnp.float32) * first
    expert_out = mm("erf,efd->erd", middle, w_down) + down_bias[:, None]
    expert_sum = scatter_all(
        combine((expert_out * slot_gate).astype(jnp.bfloat16)).astype(jnp.bfloat16)
    )
    block_out = resid + expert_sum.astype(jnp.float32)

    expert_grad = (g_slots.astype(jnp.float32) * slot_gate).astype(jnp.bfloat16)
    plain_grad = mm("erd,efd->erf", g_slots, w_down)
    middle_grad = plain_grad * slot_gate
    gate_dot = jnp.sum(plain_grad * middle.astype(jnp.float32), axis=-1) + jnp.sum(
        g_slots.astype(jnp.float32) * down_bias[:, None], axis=-1
    )
    grad_w_down = mm("erf,erd->efd", middle, expert_grad)
    grad_b_down = jnp.sum(expert_grad, axis=1, dtype=jnp.float32)
    up_grad = (middle_grad * glu_part * (1.0 - (up_soft / CLAMP_LIMIT) ** 2)).astype(jnp.bfloat16)
    gate_grad_pre = (
        middle_grad
        * (up_soft + 1.0)
        * (gate_sig + SWIGLU_ALPHA * gate_soft * gate_sig * (1.0 - gate_sig))
        * (1.0 - (gate_soft / CLAMP_LIMIT) ** 2)
    ).astype(jnp.bfloat16)
    grad_w_gate = mm("erd,erf->edf", x_slots, gate_grad_pre)
    grad_b_gate = jnp.sum(gate_grad_pre, axis=1, dtype=jnp.float32)
    grad_w_up = mm("erd,erf->edf", x_slots, up_grad)
    grad_b_up = jnp.sum(up_grad, axis=1, dtype=jnp.float32)
    row_part = mm("erf,edf->erd", gate_grad_pre, w_gate) + mm("erf,edf->erd", up_grad, w_up)
    row_sum = combine(row_part.astype(jnp.bfloat16))
    own_dot = jnp.sum(
        jnp.where(pick, gate_dot.reshape(EXP_DEV, blocks, capacity).transpose(1, 0, 2)[..., None], 0.0),
        axis=2,
    )
    dots = jnp.sum(
        own_dot[..., None]
        * (
            (my_ep * EXP_DEV + jnp.arange(EXP_DEV))[:, None] == jnp.arange(expert_count)[None]
        ).astype(jnp.float32)[None, :, None, :],
        axis=1,
    ).reshape(blocks * rows, expert_count)
    row_sum = scatter_all(jnp.concatenate([row_sum, dots], axis=1).astype(jnp.bfloat16))
    row_sum = row_sum.astype(jnp.float32)
    gate_grad = row_sum[:, width:]
    mine = my_fs * ep_size + my_ep
    gates_here = lax.dynamic_index_in_dim(gates, mine, 0, keepdims=False)
    logit_grad = gates_here * (
        gate_grad - jnp.sum(gates_here * gate_grad, axis=-1, keepdims=True)
    )
    logit_grad = logit_grad.astype(jnp.bfloat16)
    grad_br = jnp.sum(logit_grad, axis=0, dtype=jnp.float32)
    grad_wr = left_dot(norm_ffn, logit_grad)
    norm_ffn_grad = row_sum[:, :width] + jnp.dot(
        logit_grad, wr.T, preferred_element_type=jnp.float32
    )
    resid_norm_grad, grad_gain_two = norm_back(resid, scale_two, gain_two, norm_ffn_grad)
    resid_grad = cotangent.astype(jnp.float32) + resid_norm_grad

    branch_grad = gather_fs(resid_grad.astype(jnp.bfloat16))
    grad_bo = jnp.sum(branch_grad, axis=0, dtype=jnp.float32)
    mixed_grad = mm("td,fd->tf", branch_grad, w_out).astype(jnp.bfloat16)
    mixed_grad = mixed_grad.reshape(fs_size, rows, kv_heads, group, HEAD_SIZE)
    grad_wo = left_dot(mixed, branch_grad)
    grad_probs = mm("bqhgd,bkhd->bhgqk", mixed_grad, value)
    value_grad = mm("bhgqk,bqhgd->bkhd", probs_b, mixed_grad)
    row_delta = jnp.sum(probs * grad_probs, axis=-1)
    score_grad = (probs * (grad_probs - row_delta[..., None])).astype(jnp.bfloat16)
    query_grad = mm("bhgqk,bkhd->bqhgd", score_grad, key) * HEAD_SIZE ** (-0.5)
    key_grad = mm("bhgqk,bqhgd->bkhd", score_grad, query) * HEAD_SIZE ** (-0.5)
    grad_sink = -jnp.sum(sink_prob * row_delta, axis=(0, 3)).reshape(-1)
    query_pre_grad = undo_rotation(
        query_grad.reshape(many, heads, HEAD_SIZE), cosine_table, sine_table
    ).reshape(many, q_cols)
    key_pre_grad = undo_rotation(
        key_grad.reshape(many, kv_heads, HEAD_SIZE), cosine_table, sine_table
    ).reshape(many, kv_cols)
    qkv_grad = jnp.concatenate(
        [query_pre_grad, key_pre_grad, value_grad.reshape(many, kv_cols)], axis=1
    ).astype(jnp.bfloat16)
    grad_b_qkv = jnp.sum(qkv_grad, axis=0, dtype=jnp.float32)
    norm_attn_grad = scatter_fs(
        mm("tf,df->td", qkv_grad, w_qkv).astype(jnp.bfloat16)
    ).astype(jnp.float32)
    input_norm_grad, grad_gain_one = norm_back(x_float, scale_one, gain_one, norm_attn_grad)
    grad_tokens = resid_grad + input_norm_grad
    grad_qkv = left_dot(norm_attn, qkv_grad).astype(jnp.bfloat16)
    if shard % ep_size == 0:
        grad_qkv = grad_qkv.reshape(fs_size, ep_size, shard // ep_size, q_cols + 2 * kv_cols)
        grad_qkv = lax.psum_scatter(grad_qkv, "ep", scatter_dimension=1, tiled=False)
        grad_qkv = lax.all_to_all(grad_qkv, "fs", split_axis=0, concat_axis=1, tiled=False)
        grad_qkv = lax.all_gather(grad_qkv, "ep", axis=0, tiled=True).astype(jnp.float32)
    else:
        grad_qkv = lax.psum(grad_qkv.reshape(fs_size, shard, q_cols + 2 * kv_cols), "ep")
        grad_qkv = lax.all_to_all(grad_qkv, "fs", split_axis=0, concat_axis=1, tiled=False)
        grad_qkv = grad_qkv.astype(jnp.float32)
    sum_wq = grad_qkv[:, :, :q_cols].reshape(shard, -1)
    sum_wk = grad_qkv[:, :, q_cols : q_cols + kv_cols].reshape(shard, -1)
    sum_wv = grad_qkv[:, :, q_cols + kv_cols :].reshape(shard, -1)
    sum_wo = lax.psum(grad_wo.astype(jnp.bfloat16), "ep").astype(jnp.float32)
    by_shard = jnp.concatenate(
        [
            grad_wr.reshape(fs_size, -1),
            grad_gain_one.reshape(fs_size, -1),
            grad_gain_two.reshape(fs_size, -1),
            grad_br.reshape(fs_size, -1),
        ],
        axis=1,
    )
    by_shard = lax.psum(by_shard, ("fs", "ep"))
    by_shard = lax.dynamic_index_in_dim(by_shard, my_fs, 0, keepdims=False)
    sum_wr = by_shard[: shard * expert_count].reshape(shard, expert_count)
    rest = by_shard[shard * expert_count :]
    own = jnp.concatenate(
        [
            grad_b_qkv,
            grad_sink,
            lax.dynamic_slice_in_dim(grad_bo, my_fs * shard, shard),
        ]
    )
    own = lax.psum(own, "ep")
    sum_b = own[: q_cols + 2 * kv_cols]
    return (
        block_out.astype(jnp.bfloat16),
        grad_tokens,
        rest[:shard],
        sum_wq,
        sum_b[:q_cols],
        sum_wk,
        sum_b[q_cols : q_cols + kv_cols],
        sum_wv,
        sum_b[q_cols + kv_cols :],
        own[q_cols + 2 * kv_cols : q_cols + 2 * kv_cols + heads],
        sum_wo,
        own[q_cols + 2 * kv_cols + heads :],
        rest[shard : 2 * shard],
        sum_wr,
        rest[2 * shard :],
        grad_w_gate,
        grad_b_gate,
        grad_w_up,
        grad_b_up,
        grad_w_down,
        grad_b_down,
    )


def solution(mesh):
    in_specs = (
        P(("fs", "ep"), None),
        P(("fs", "ep"), None),
        P(("fs", "ep"), None),
        P("fs"),
        P("fs", None),
        P("fs"),
        P("fs", None),
        P("fs"),
        P("fs", None),
        P("fs"),
        P("fs"),
        P("fs", None),
        P("fs"),
        P("fs"),
        P("fs", None),
        P("fs"),
        P("ep", None, "fs"),
        P("ep", "fs"),
        P("ep", None, "fs"),
        P("ep", "fs"),
        P("ep", "fs", None),
        P("ep", None),
        P(("fs", "ep"), None),
    )
    out_specs = (
        P(("fs", "ep"), None),
        P(("fs", "ep"), None),
        P("fs"),
        P("fs", None),
        P("fs"),
        P("fs", None),
        P("fs"),
        P("fs", None),
        P("fs"),
        P("fs"),
        P("fs", None),
        P("fs"),
        P("fs"),
        P("fs", None),
        P("fs"),
        P("ep", None, "fs"),
        P("ep", "fs"),
        P("ep", None, "fs"),
        P("ep", "fs"),
        P("ep", "fs", None),
        P("ep", None),
    )
    run = this_slice if (mesh.shape["fs"], mesh.shape["ep"]) == (4, 8) else any_slice
    return jax.shard_map(
        run, mesh=mesh, in_specs=in_specs, out_specs=out_specs, check_vma=False
    )
```

```python
from functools import partial

import jax
import jax.numpy as jnp
from jax import lax
from jax.experimental import pallas as pl
from jax.experimental.pallas import tpu as pltpu
from jax.sharding import PartitionSpec as P

QUERY_HEADS = 64
KEY_VALUE_HEADS = 8
HEAD_SIZE = 64
TOP = 4
EXP_DEV = 2


EPSILON = 1e-05
ROPE_BASE = 150000.0
SWIGLU_ALPHA = 1.702
CLAMP_LIMIT = 7.0
MASKED_SCORE = -1e30


F32 = jnp.float32
BF = jnp.bfloat16
MESH = pl.DeviceIdType.MESH


def layout(lengths, card_rows):
    seq_ends = jnp.cumsum(lengths)
    places = jnp.arange(card_rows, dtype=jnp.int32)
    past_end = (places[:, None] >= seq_ends[None, :]).astype(jnp.int32)
    segment_ids = jnp.sum(past_end, axis=1)
    position = places - jnp.sum(past_end * lengths[None, :], axis=1)
    return (segment_ids, position)


def tables(position, half_dim):
    inv_freq = jnp.exp(-jnp.log(ROPE_BASE) * jnp.arange(half_dim, dtype=jnp.float32) / half_dim)
    angles = position.astype(jnp.float32)[:, None] * inv_freq[None, :]
    return (jnp.cos(angles)[:, None, :], jnp.sin(angles)[:, None, :])


def apply_rotation(value_matrix, cosine_table, sine_table):
    half_dim = value_matrix.shape[-1] // 2
    lower_half = value_matrix[..., :half_dim]
    upper_half = value_matrix[..., half_dim:]
    return jnp.concatenate(
        [
            lower_half * cosine_table - upper_half * sine_table,
            upper_half * cosine_table + lower_half * sine_table,
        ],
        axis=-1,
    )


def undo_rotation(value_matrix, cosine_table, sine_table):
    half_dim = value_matrix.shape[-1] // 2
    lower_half = value_matrix[..., :half_dim]
    upper_half = value_matrix[..., half_dim:]
    return jnp.concatenate(
        [
            lower_half * cosine_table + upper_half * sine_table,
            upper_half * cosine_table - lower_half * sine_table,
        ],
        axis=-1,
    )


def norm_scale(value_matrix):
    return lax.rsqrt(jnp.mean(value_matrix * value_matrix, axis=-1, keepdims=True) + EPSILON)


def norm_back(value_matrix, inv_scale, gain, grad_norm):
    weighted = grad_norm * gain
    grad_values = inv_scale * weighted - value_matrix * inv_scale**3 * jnp.mean(
        weighted * value_matrix, axis=-1, keepdims=True
    )
    grad_gain = jnp.sum(grad_norm * value_matrix * inv_scale, axis=0)
    return (grad_values, grad_gain)


def left_dot(left, right):
    return jnp.dot(left.T, right, preferred_element_type=jnp.float32)


def mm(spec, left, right):
    return jnp.einsum(spec, left, right, preferred_element_type=jnp.float32)


def gather_all(value):
    return lax.all_gather(value, ("fs", "ep"), axis=0, tiled=True)


def scatter_all(value):
    return lax.psum_scatter(value, ("fs", "ep"), scatter_dimension=0, tiled=True)


def gather_fs(value):
    return lax.all_gather(value, "fs", axis=0, tiled=True)


def scatter_fs(value):
    return lax.psum_scatter(value, "fs", scatter_dimension=0, tiled=True)


def spot():
    fs=lax.axis_index("fs"); ep=lax.axis_index("ep")
    return fs, ep, fs//2, fs%2, ep//2, ep%2

def greet(fs, ep, z, more=0):
    y, x, c = fs//2, fs%2, ep%2
    bar=pltpu.get_barrier_semaphore()
    def hi(f,e): pl.semaphore_signal(bar,inc=1,device_id=(f,e),device_id_type=MESH)
    hi(fs+1-2*x,ep); hi(fs+2-4*y,ep); hi(fs,ep+1-2*c)
    if more: hi(3-fs,ep)
    @pl.when(z>0)
    def _(): hi(fs,ep-2)
    @pl.when(z<3)
    def _(): hi(fs,ep+2)
    @pl.when((z>0)&(z<3))
    def _(): pl.semaphore_wait(bar,5+more)
    @pl.when((z==0)|(z==3))
    def _(): pl.semaphore_wait(bar,4+more)

def scatter_kernel(na, parts, *refs):
    ps=refs[:na]; out=refs[na]; far=refs[na+1]
    q,v1,v2,vu,vd,stg,load,s0,r0,gsem,s1,r1,s2,r2,su,ru,sd,rd,osem = refs[na+2:]
    fs,ep,y,x,z,c = spot()
    rows=ps[0].shape[2]; pr=rows//parts; half=pr//2
    items=na*4*parts
    xn=(fs+1-2*x,ep); yn=(fs+2-4*y,ep); cn=(fs,ep+1-2*c)
    A=pl.ds(0,half); B=pl.ds(half,half)
    def rem(src,dst,s,r,dev): return pltpu.make_async_remote_copy(src,dst,s,r,device_id=dev,device_id_type=MESH)
    def where(i):
        a=i//(4*parts); j=i%(4*parts); k=j//parts; part=j%parts
        zz=(k%2)*(k//2)+(1-k%2)*(3-k//2)
        return a,part,zz
    def block(i,par):
        a,part,zz=where(i)
        return a,zz*2+par,pl.ds(part*pr,pr)
    def on_array(i,f):
        if na==1: f(ps[0])
        else:
            a=i//(4*parts)
            for n in range(na):
                @pl.when(a==n)
                def _(): f(ps[n])
    def give(i,p):
        _,e,r=block(i,1-c)
        return rem(p.at[:,e,r],far.at[i],s0.at[i],r0.at[i],cn)
    def mine(i,p):
        _,e,r=block(i,c)
        return pltpu.make_async_copy(p.at[:,e,r],q.at[i],load.at[i])
    def fetch(i):
        return pltpu.make_async_copy(far.at[i],stg.at[i%2],gsem.at[i%2])
    def one(i):
        return ([rem(q.at[i,2*j+1-x,A],v1.at[i,0,j],s1.at[i,j],r1.at[i,j],xn) for j in range(2)],
                rem(q.at[i,pl.ds((1-y)*2,2),B],v1.at[i,1],s1.at[i,2],r1.at[i,2],yn))
    def two(i):
        return (rem(q.at[i,(1-y)*2+x,A],v2.at[i,0],s2.at[i,0],r2.at[i,0],yn),
                rem(q.at[i,y*2+1-x,B],v2.at[i,1],s2.at[i,1],r2.at[i,1],xn))
    def up(i): return rem(q.at[i,fs],vu.at[i],su.at[i],ru.at[i],(fs,ep+2))
    def down(i): return rem(q.at[i,fs],vd.at[i],sd.at[i],rd.at[i],(fs,ep-2))
    greet(fs,ep,z)
    @pl.loop(0,items)
    def _(i):
        on_array(i,lambda p: give(i,p).start())
        on_array(i,lambda p: mine(i,p).start())
    def valid(i): return (i>=0)&(i<items)
    def add(dst,src,n):
        for lo in range(0,n,16):
            s=pl.ds(lo,16)
            dst(s,src(s))
    def getfar(i):
        on_array(i,lambda p: give(i,p).wait_recv())
        fetch(i).start()
    getfar(0)
    @pl.loop(0,items+6)
    def _(t):
        @pl.when(t<items)
        def _():
            i=t
            @pl.when(i+1<items)
            def _(): getfar(i+1)
            fetch(i).wait()
            on_array(i,lambda p: mine(i,p).wait())
            for g in range(4):
                q[i,g]=q[i,g]+stg[i%2,g]
            a,b=one(i)
            for k in a: k.start()
            b.start()
        i=t-1
        @pl.when(valid(i))
        def _():
            a,b=one(i)
            for k in a: k.wait_recv()
            for j in range(2):
                q[i,2*j+x,A]=q[i,2*j+x,A]+v1[i,0,j]
            ta,tb=two(i)
            ta.start()
            b.wait_recv()
            for j in range(2):
                q[i,2*y+j,B]=q[i,2*y+j,B]+v1[i,1,j]
            tb.start()
        i2=t-2
        @pl.when(valid(i2))
        def _():
            ta,tb=two(i2)
            ta.wait_recv()
            q[i2,fs,A]=q[i2,fs,A]+v2[i2,0]
            tb.wait_recv()
            q[i2,fs,B]=q[i2,fs,B]+v2[i2,1]
        iu=t-2-z
        @pl.when(valid(iu))
        def _():
            _,_,zz=where(iu)
            @pl.when(zz>=z)
            def _():
                @pl.when(z>0)
                def _():
                    up(iu).wait_recv()
                    q[iu,fs]=q[iu,fs]+vu[iu]
                @pl.when(zz>z)
                def _(): up(iu).start()
        idn=t-2-(3-z)
        @pl.when(valid(idn))
        def _():
            _,_,zz=where(idn)
            @pl.when(zz<=z)
            def _():
                @pl.when(z<3)
                def _():
                    down(idn).wait_recv()
                    q[idn,fs]=q[idn,fs]+vd[idn]
                @pl.when(zz<z)
                def _(): down(idn).start()
    @pl.loop(0,items)
    def _(i):
        a,part,zz=where(i)
        @pl.when(zz==z)
        def _():
            pltpu.make_async_copy(q.at[i,fs],out.at[a,pl.ds(part*pr,pr)],osem.at[i]).start()
    @pl.loop(0,items)
    def _(i):
        a,part,zz=where(i)
        on_array(i,lambda p: give(i,p).wait_send())
        a1,b1=one(i)
        for k in a1: k.wait_send()
        b1.wait_send()
        ta,tb=two(i); ta.wait_send(); tb.wait_send()
        @pl.when(zz>z)
        def _(): up(i).wait_send()
        @pl.when(zz<z)
        def _(): down(i).wait_send()
        @pl.when(zz==z)
        def _(): pltpu.make_async_copy(q.at[i,fs],out.at[a,pl.ds(part*pr,pr)],osem.at[i]).wait()

def scatter_blocks(arrays, cid, parts=2):
    na=len(arrays); rows,width=arrays[0].shape[-2:]
    arrays=[a.reshape(4,8,rows,width) for a in arrays]
    pr=rows//parts; items=na*4*parts; half=pr//2
    any_=pl.BlockSpec(memory_space=pl.ANY)
    D=pltpu.SemaphoreType.DMA
    V=lambda *s: pltpu.VMEM(s+(width,),BF)
    out,_=pl.pallas_call(partial(scatter_kernel,na,parts),
        out_shape=[jax.ShapeDtypeStruct((na,rows,width),BF),jax.ShapeDtypeStruct((items,4,pr,width),BF)],
        in_specs=[any_]*na,out_specs=[any_,any_],
        scratch_shapes=[V(items,4,pr),V(items,2,2,half),V(items,2,half),V(items,pr),V(items,pr),V(2,4,pr),
            D((items,)),D((items,)),D((items,)),D((2,)),D((items,3)),D((items,3)),D((items,2)),D((items,2)),
            D((items,)),D((items,)),D((items,)),D((items,)),D((items,))],
        compiler_params=pltpu.CompilerParams(collective_id=cid,has_side_effects=True,vmem_limit_bytes=63*1024*1024),
        name="scatter_blocks")(*arrays)
    return out


def reduce_kernel(
    wide_n, slab_n, splits, gw, gq, tw, tq, tk, tv,
    own_w, own_q, all_q, far_w, far_q, pin_w, pin_q, pout_w, pout_q, din_w, din_q, dout_w, dout_q, tot_w, tot_q, mate_q,
    wload, qload, s0w, r0w, s0q, r0q, sa, ra, su, ru, sd, rd, keep, keep_q, keep_m, sc, rc,
):
    fs, ep, y, x, z, c = spot()
    mate = (fs, ep + 1 - 2 * c)
    rows_w, rows_q = own_w.shape[1], own_q.shape[1]
    parts = slab_n // 4
    items = wide_n + slab_n

    def rem(src, dst, s, r, dev):
        return pltpu.make_async_remote_copy(src, dst, s, r, device_id=dev, device_id_type=MESH)

    def source(s):
        return ((y + s // 2) % 2) * 2 + (x + s) % 2

    def give_w(i):
        return rem(gw.at[1 - c, i], far_w.at[i], s0w.at[i], r0w.at[i], mate)

    def give_q(s):
        return rem(gq.at[source(s), 1 - c], far_q.at[s], s0q.at[s], r0q.at[s], mate)

    def load_w(i):
        return pltpu.make_async_copy(gw.at[c, i], own_w.at[i], wload.at[i])

    def load_q(s):
        return pltpu.make_async_copy(gq.at[source(s), c], all_q.at[s], qload.at[s])

    def pass_q(s):
        dev = (source(s), ep)
        return rem(all_q.at[s], own_q.at[pl.ds(s * parts, parts)], sa.at[s], ra.at[s], dev)

    def on_item(i, f):
        @pl.when(i < wide_n)
        def _():
            f(own_w, pin_w, pout_w, din_w, dout_w, tot_w, i)

        @pl.when(i >= wide_n)
        def _():
            f(own_q, pin_q, pout_q, din_q, dout_q, tot_q, i - wide_n)

    def valid(i):
        return (i >= 0) & (i < items)

    def place(buf, sem, j, core):
        at = pl.ds(pl.multiple_of((core * parts + j % parts) * rows_q, 16), rows_q)
        lo, out = 0, []
        for n, (dst, size) in enumerate(zip((tq, tk, tv), splits)):
            to = pl.ds(pl.multiple_of(source(j // parts) * size, 128), size)
            out.append(
                pltpu.make_async_copy(buf.at[j, :, pl.ds(lo, size)], dst.at[at, to], sem.at[j, n])
            )
            lo += size
        return out

    def share_w(i):
        dst = tw.at[c, i]
        return (
            pltpu.make_async_copy(tot_w.at[i], dst, keep.at[i]),
            rem(tot_w.at[i], dst, sc.at[i], rc.at[i], mate),
        )

    def share_q(j):
        i = j + wide_n
        return rem(tot_q.at[j], mate_q.at[j], sc.at[i], rc.at[i], mate)

    greet(fs, ep, z, 1)

    @pl.loop(0, wide_n)
    def _(i):
        give_w(i).start()
        load_w(i).start()

    for s in (1, 2, 3, 0):
        give_q(s).start()
        load_q(s).start()

    @pl.loop(0, items + 4)
    def _(t):
        @pl.when(t < wide_n)
        def _():
            load_w(t).wait()
            give_w(t).wait_recv()
            own_w[t] = own_w[t] + far_w[t]

        for n, s in enumerate((1, 2, 3, 0)):

            @pl.when(t == n)
            def _():
                load_q(s).wait()
                give_q(s).wait_recv()

                @pl.loop(0, parts)
                def _(j):
                    if s:
                        all_q[s, j] = all_q[s, j] + far_q[s, j]
                    else:
                        own_q[j] = all_q[0, j] + far_q[0, j]

                if s:
                    pass_q(s).start()

        for s in (1, 2, 3):

            @pl.when(t == wide_n + s * parts)
            def _():
                pass_q(s).wait_recv()

        iu = t - z

        @pl.when(valid(iu))
        def _():
            def go(own, pin, pout, din, dout, tot, i):
                @pl.when(z == 0)
                def _():
                    rem(own.at[i], pin.at[i], su.at[iu], ru.at[iu], (fs, ep + 2)).start()

                @pl.when(z > 0)
                def _():
                    rem(own.at[i], pin.at[i], su.at[iu], ru.at[iu], (fs, ep - 2)).wait_recv()

                @pl.when((z > 0) & (z < 3))
                def _():
                    pout[i] = pin[i] + own[i]
                    rem(pout.at[i], pin.at[i], su.at[iu], ru.at[iu], (fs, ep + 2)).start()

            on_item(iu, go)

        idn = t - 3 + z

        @pl.when(valid(idn))
        def _():
            def go(own, pin, pout, din, dout, tot, i):
                @pl.when(z == 3)
                def _():
                    rem(own.at[i], din.at[i], sd.at[idn], rd.at[idn], (fs, ep - 2)).start()

                @pl.when(z < 3)
                def _():
                    rem(own.at[i], din.at[i], sd.at[idn], rd.at[idn], (fs, ep + 2)).wait_recv()

                @pl.when((z > 0) & (z < 3))
                def _():
                    dout[i] = din[i] + own[i]
                    rem(dout.at[i], din.at[i], sd.at[idn], rd.at[idn], (fs, ep - 2)).start()

            on_item(idn, go)

        last = t - 3

        @pl.when(valid(last))
        def _():
            def go(own, pin, pout, din, dout, tot, i):
                @pl.when(z == 0)
                def _():
                    tot[i] = own[i] + din[i]

                @pl.when(z == 3)
                def _():
                    tot[i] = own[i] + pin[i]

                @pl.when((z == 1) | (z == 2))
                def _():
                    tot[i] = own[i] + pin[i] + din[i]

            on_item(last, go)

            @pl.when(last < wide_n)
            def _():
                for copy in share_w(last):
                    copy.start()

            @pl.when(last >= wide_n)
            def _():
                j = last - wide_n
                for copy in (share_q(j), *place(tot_q, keep_q, j, c)):
                    copy.start()

    @pl.loop(0, items)
    def _(i):
        @pl.when(i < wide_n)
        def _():
            for copy in share_w(i):
                copy.wait()

        @pl.when(i >= wide_n)
        def _():
            j = i - wide_n
            share_q(j).wait()
            for copy in place(mate_q, keep_m, j, 1 - c):
                copy.start()

        def go(own, pin, pout, din, dout, tot, j):
            @pl.when(z < 3)
            def _():
                rem(own.at[j], pin.at[j], su.at[i], ru.at[i], (fs, ep + 2)).wait_send()

            @pl.when(z > 0)
            def _():
                rem(own.at[j], din.at[j], sd.at[i], rd.at[i], (fs, ep - 2)).wait_send()

        on_item(i, go)

    @pl.loop(0, slab_n)
    def _(j):
        for copy in (*place(tot_q, keep_q, j, c), *place(mate_q, keep_m, j, 1 - c)):
            copy.wait()

    @pl.loop(0, wide_n)
    def _(i):
        give_w(i).wait_send()

    for s in range(4):
        give_q(s).wait_send()
        if s:
            pass_q(s).wait_send()


def reduce_parts(gw, gq, splits, cid):
    wide_n = gw.shape[1]
    parts = gq.shape[2]
    slab_n = 4 * parts
    free = pl.BlockSpec(memory_space=pl.ANY)
    D = pltpu.SemaphoreType.DMA
    W = pltpu.VMEM((wide_n,) + gw.shape[2:], BF)
    Q = pltpu.VMEM((slab_n,) + gq.shape[3:], BF)
    Q4 = pltpu.VMEM((4, parts) + gq.shape[3:], BF)
    items = wide_n + slab_n
    slab_rows = 2 * parts * gq.shape[3]
    return pl.pallas_call(
        partial(reduce_kernel, wide_n, slab_n, splits),
        out_shape=[jax.ShapeDtypeStruct(gw.shape, BF)]
        + [jax.ShapeDtypeStruct((slab_rows, 4 * size), BF) for size in splits],
        in_specs=[free, free],
        out_specs=[free] * 4,
        scratch_shapes=[W, Q, Q4, W, Q4] + [W, Q] * 5 + [Q]
        + [D((wide_n,)), D((4,)), D((wide_n,)), D((wide_n,)), D((4,)), D((4,)), D((4,)), D((4,))]
        + [D((items,))] * 4 + [D((wide_n,)), D((slab_n, 3)), D((slab_n, 3)), D((items,)), D((items,))],
        compiler_params=pltpu.CompilerParams(
            collective_id=cid, has_side_effects=True, vmem_limit_bytes=63 * 1024 * 1024
        ),
        name="reduce_parts",
    )(gw, gq)


def start_kernel(
    splits, own, wq, wk, wv, rows_out, w_out, here, own_w, sx, rx, sw, rw, sm, rm,
):
    fs, ep, y, x, z, c = spot()
    mate = (fs, ep + 1 - 2 * c)
    shard = wq.shape[0]
    cut = -(-shard // 32) * 16
    halves = ((0, cut), (cut, shard - cut))

    def peer(s):
        return ((y + s // 2) % 2) * 2 + (x + s) % 2

    def rem(src, dst, s, r, dev):
        return pltpu.make_async_remote_copy(src, dst, s, r, device_id=dev, device_id_type=MESH)

    def columns(dev, at):
        lo, out = 0, []
        for src, size in zip((wq, wk, wv), splits):
            cols = pl.ds(pl.multiple_of(dev * size, 128), size)
            out.append((src.at[at, cols], pl.ds(lo, size)))
            lo += size
        return out

    def send(s, lo, n):
        at = pl.ds(lo, n)
        return [
            rem(src, w_out.at[fs, at, cols], sw.at[s, k], rw.at[s, k], (peer(s), ep))
            for k, (src, cols) in enumerate(columns(peer(s), at))
        ]

    def arrive(s, lo, n):
        at = pl.ds(lo, n)
        return [
            rem(w_out.at[peer(s), at, cols], w_out.at[peer(s), at, cols], sw.at[s, k], rw.at[s, k], mate)
            for k, (_, cols) in enumerate(columns(fs, at))
        ]

    def share(s, lo, n):
        v = w_out.at[peer(s), pl.ds(lo, n)]
        return rem(v, v, sm.at[s], rm.at[s], mate)

    def give(s):
        return rem(own, rows_out.at[fs], sx.at[s], rx.at[s], (peer(s), ep))

    locals_ = [pltpu.make_async_copy(own, rows_out.at[fs], here)]
    for k, (src, cols) in enumerate(columns(fs, pl.ds(0, shard))):
        locals_.append(pltpu.make_async_copy(src, w_out.at[fs, :, cols], own_w.at[k]))
    for copy in locals_:
        copy.start()
    greet(fs, ep, z, 1)
    for s in (3, 1, 2):
        give(s).start()
    for core in range(2):

        @pl.when(c == core)
        def _():
            mine, other = halves[core], halves[1 - core]
            for s in (3, 1, 2):
                for copy in send(s, *mine):
                    copy.start()
            for s in (1, 2, 3):
                for copy in arrive(s, *mine):
                    copy.wait_recv()
                share(s, *mine).start()
            for s in (1, 2, 3):
                share(s, *other).wait_recv()
            for s in (1, 2, 3):
                for copy in send(s, *mine):
                    copy.wait_send()
                share(s, *mine).wait_send()

    for s in (1, 2, 3):
        rem(own, rows_out.at[peer(s)], sx.at[s], rx.at[s], mate).wait_recv()
        give(s).wait_send()
    for copy in locals_:
        copy.wait()


def start_exchange(own, wq, wk, wv, cid):
    shard = wq.shape[0]
    splits = tuple(w.shape[1] // 4 for w in (wq, wk, wv))
    free = pl.BlockSpec(memory_space=pl.ANY)
    D = pltpu.SemaphoreType.DMA
    return pl.pallas_call(
        partial(start_kernel, splits),
        out_shape=[
            jax.ShapeDtypeStruct((4,) + own.shape, BF),
            jax.ShapeDtypeStruct((4, shard, sum(splits)), BF),
        ],
        in_specs=[free] * 4,
        out_specs=[free] * 2,
        scratch_shapes=[D, D((3,)), D((4,)), D((4,)), D((4, 3)), D((4, 3)), D((4,)), D((4,))],
        compiler_params=pltpu.CompilerParams(collective_id=cid, has_side_effects=True),
        name="start_exchange",
    )(own, wq, wk, wv)


def nn(left, right):
    return lax.dot_general(left, right, (((1,), (0,)), ((), ())), preferred_element_type=F32)


def nt(left, right):
    return lax.dot_general(left, right, (((1,), (1,)), ((), ())), preferred_element_type=F32)


def tn(left, right):
    return lax.dot_general(left, right, (((0,), (0,)), ((), ())), preferred_element_type=F32)


def strips(total, size):
    return [(at, min(size, total - at)) for at in range(0, total, size)]


def remote(src, dst, send, recv, device):
    return pltpu.make_async_remote_copy(
        src, dst, send, recv, device_id=device, device_id_type=MESH
    )


def line_order(z, i):
    code = jnp.where(z == 0, 228, jnp.where(z == 1, 225, jnp.where(z == 2, 30, 27)))
    power = jnp.where(i == 0, 1, jnp.where(i == 1, 4, jnp.where(i == 2, 16, 64)))
    return (code // power) % 4


class Gather:
    def __init__(self, full, sems):
        self.full = full
        self.sz, self.rz, self.s1, self.r1, self.s2, self.r2, self.sc, self.rc = sems
        self.fs, self.ep, self.y, self.x, self.z, self.c = spot()
        half = full.shape[3] // 2
        self.upper, self.lower = pl.ds(0, half), pl.ds(half, half)
        self.xn = (self.fs + 1 - 2 * self.x, self.ep)
        self.yn = (self.fs + 2 - 4 * self.y, self.ep)
        self.mate = (self.fs, self.ep + 1 - 2 * self.c)

    def item(self, t):
        return t // 4, line_order(self.z, t % 4)

    def along(self, a, zz, up):
        view = self.full.at[a, self.fs, zz * 2 + self.c]
        other = (self.fs, self.ep + (2 if up else -2))
        return remote(view, view, self.sz.at[a, zz, up], self.rz.at[a, zz], other)

    def first(self, a, zz):
        e = zz * 2 + self.c
        v = self.full.at[a, self.fs, e, self.upper]
        w = self.full.at[a, self.fs, e, self.lower]
        s, r = self.s1.at[a, zz], self.r1.at[a, zz]
        return (
            remote(v, v, s.at[0], r.at[0], self.xn),
            remote(w, w, s.at[1], r.at[1], self.yn),
            remote(w, w, s.at[2], r.at[2], self.xn),
            remote(v, v, s.at[3], r.at[3], self.yn),
        )

    def second(self, a, zz):
        e = zz * 2 + self.c
        v = self.full.at[a, self.y * 2 + 1 - self.x, e, self.upper]
        w = self.full.at[a, (1 - self.y) * 2 + self.x, e, self.lower]
        s, r = self.s2.at[a, zz], self.r2.at[a, zz]
        return remote(v, v, s.at[0], r.at[0], self.yn), remote(w, w, s.at[1], r.at[1], self.xn)

    def across(self, a, zz, e):
        v = self.full.at[a, :, zz * 2 + e]
        return remote(v, v, self.sc.at[a, zz], self.rc.at[a, zz], self.mate)

    def step0(self, t):
        @pl.when(t < 8)
        def _():
            a, zz = self.item(t)

            @pl.when(zz != self.z)
            def _():
                self.along(a, zz, 0).wait_recv()

            @pl.when((zz <= self.z) & (self.z < 3))
            def _():
                self.along(a, zz, 1).start()

            @pl.when((zz >= self.z) & (self.z > 0))
            def _():
                self.along(a, zz, 0).start()

    def step0_if(self, t, inner):
        inside = (self.z == 1) | (self.z == 2)

        @pl.when(inside == inner)
        def _():
            self.step0(t)

    def step1(self, t):
        @pl.when(t < 8)
        def _():
            for copy in self.first(*self.item(t)):
                copy.start()

    def step2(self, t):
        @pl.when(t < 8)
        def _():
            a, zz = self.item(t)
            from_x, from_y, _, _ = self.first(a, zz)
            to_y, to_x = self.second(a, zz)
            from_x.wait_recv()
            to_y.start()
            from_y.wait_recv()
            to_x.start()

    def step3(self, t):
        @pl.when(t < 8)
        def _():
            a, zz = self.item(t)
            for copy in (*self.first(a, zz)[2:], *self.second(a, zz)):
                copy.wait_recv()
            self.across(a, zz, self.c).start()

    def step4(self, t):
        a, zz = self.item(t)
        self.across(a, zz, 1 - self.c).wait_recv()

    def finish(self):
        @pl.loop(0, 8)
        def _(t):
            a, zz = self.item(t)
            self.across(a, zz, self.c).wait_send()
            for copy in (*self.first(a, zz), *self.second(a, zz)):
                copy.wait_send()

            @pl.when((zz <= self.z) & (self.z < 3))
            def _():
                self.along(a, zz, 1).wait_send()

            @pl.when((zz >= self.z) & (self.z > 0))
            def _():
                self.along(a, zz, 0).wait_send()


def experts_kernel(
    cap, width,
    n_own, g_own, wg_hbm, wu_hbm, wd_hbm, bg_ref, bu_ref, bd_ref,
    full, out_hbm, row_hbm, xs_hbm, eg_hbm, mid_hbm, ug_hbm, gg_hbm, cu_hbm, cg_hbm,
    sum_g, sum_u, sum_d,
    wg_ref, wu_ref, wd_ref, bin_, meta, pmat, pmat_t, gates, xs, res, mid, cub, cgb, dots, stage,
    w_sem, own_sem, in_sem, st_sem, save_sem,
    *sems,
):
    gather = Gather(full, sems)
    fs, ep, z = gather.fs, gather.ep, gather.z
    card_rows, wpad = bin_.shape[2:]
    tail = wpad - 128
    off = width - tail
    first = jnp.where(fs == 0, 1.0, 0.0).astype(F32)
    nb = 8
    rows = nb * cap
    weights = [
        pltpu.make_async_copy(src, dst, w_sem.at[n])
        for n, (src, dst) in enumerate(((wg_hbm, wg_ref), (wu_hbm, wu_ref), (wd_hbm, wd_ref)))
    ]
    keep = [
        pltpu.make_async_copy(src, full.at[a, fs, ep], own_sem.at[a])
        for a, src in enumerate((n_own, g_own))
    ]
    for copy in keep + weights:
        copy.start()
    greet(fs, ep, z)
    for copy in keep:
        copy.wait()
    gather.step0(0)
    gather.step1(0)
    gather.step0(1)
    gather.step2(0)
    gather.step1(1)
    gather.step3(0)
    gather.step0(2)

    def load(t):
        a, zz = gather.item(t)
        return pltpu.make_async_copy(full.at[a, :, pl.ds(zz * 2, 2)], bin_, in_sem)

    def save(src, dst, k, i, n):
        return pltpu.make_async_copy(src.at[k], dst.at[k, i], save_sem.at[n, k])

    def save_rows(dst, k, i):
        return pltpu.make_async_copy(xs.at[:, k], dst.at[k, i], save_sem.at[0, k])

    def fetch(src, dst, k, i, n):
        return pltpu.make_async_copy(src.at[k, i], dst.at[k], save_sem.at[n, k])

    def rows_of(ref, k, lo=0, n=width):
        return ref[:, k, :, lo : lo + n].reshape(rows, n)

    def next_load(t):
        @pl.when(t < 8)
        def _():
            gather.step4(t)
            load(t).start()

    def spread(i, prepare):
        @pl.loop(0, nb)
        def _(b):
            j, c = b // 2, b % 2
            if prepare:
                meta[...] = jnp.transpose(bin_[j, c, :, tail:].astype(F32))
                at = pl.ds(pl.multiple_of(b * cap, 16), cap)
                hits = []
                for k in range(2):
                    e = ep * 2 + k
                    place = meta[pl.ds(off + e, 1), :]
                    gate = meta[pl.ds(off + 16 + e, 1), :] + meta[pl.ds(off + 32 + e, 1), :]
                    hit = lax.broadcasted_iota(jnp.int32, (cap, card_rows), 0).astype(F32) == place
                    gates[i, k, at, :] = jnp.sum(jnp.where(hit, gate, 0.0), axis=1, keepdims=True)
                    hits.append(jnp.where(hit, 1.0, 0.0))
                hits.append(jnp.zeros((card_rows - 2 * cap, card_rows), F32))
                hits = jnp.concatenate(hits, axis=0)
                pmat[i, b] = hits[: 2 * cap].astype(BF)
                pmat_t[i, b] = jnp.transpose(hits).astype(BF)
            pick = pmat[i, b]
            for lo, n in strips(width, 768):
                got = nn(pick, bin_[j, c, :, lo : lo + n]).astype(BF)
                xs[b, :, :, lo : lo + n] = got.reshape(2, cap, n)

    def group_store(dst, zz):
        return pltpu.make_async_copy(stage, dst.at[:, pl.ds(zz * 2, 2)], st_sem)

    def combine(i, with_dots):
        column = lax.broadcasted_iota(jnp.int32, (cap, wpad - width), 1)

        @pl.loop(0, nb)
        def _(b):
            j, c = b // 2, b % 2
            pick = pmat_t[i, b, :, : 2 * cap]
            for lo, n in strips(width, 768):
                both = res[b, :, :, lo : lo + n].reshape(2 * cap, n)
                stage[j, c, :, lo : lo + n] = nn(pick, both).astype(BF)
            if with_dots:
                at = pl.ds(pl.multiple_of(b * cap, 16), cap)
                own_dots = jnp.concatenate(
                    [
                        jnp.where(column == ep * 2 + k, dots[k, at, :], 0.0).astype(BF)
                        for k in range(2)
                    ],
                    axis=0,
                )
                stage[j, c, :, width:] = nn(pick, own_dots).astype(BF)
            else:
                stage[j, c, :, width:] = jnp.zeros((card_rows, wpad - width), BF)

    next_load(0)
    for copy in weights:
        copy.wait()

    @pl.loop(0, 4)
    def _(i):
        zz = line_order(z, i)
        gather.step2(i + 1)
        gather.step1(i + 2)
        gather.step0_if(i + 3, True)
        load(i).wait()
        spread(i, True)
        for k in range(2):
            save_rows(xs_hbm, k, i).start()

        @pl.loop(0, 2)
        def _(k):
            @pl.when(k == 1)
            def _():
                gather.step3(i + 1)

            x = rows_of(xs, k)
            gate_soft = CLAMP_LIMIT * jnp.tanh((nt(x, wg_ref[k]) + bg_ref[k]) * (1.0 / CLAMP_LIMIT))
            up_soft = CLAMP_LIMIT * jnp.tanh((nt(x, wu_ref[k]) + bu_ref[k]) * (1.0 / CLAMP_LIMIT))
            sig = jax.nn.sigmoid(SWIGLU_ALPHA * gate_soft)
            glu = gate_soft * sig
            mid[k] = ((up_soft + 1.0) * glu).astype(BF)
            cub[k] = (glu * (1.0 - (up_soft * (1.0 / CLAMP_LIMIT)) ** 2)).astype(BF)
            cgb[k] = (
                (up_soft + 1.0)
                * (sig + SWIGLU_ALPHA * glu * (1.0 - sig))
                * (1.0 - (gate_soft * (1.0 / CLAMP_LIMIT)) ** 2)
            ).astype(BF)
            save(mid, mid_hbm, k, i, 1).start()
            save(cub, cu_hbm, k, i, 2).start()
            save(cgb, cg_hbm, k, i, 3).start()
            for lo, n in strips(width, 768):
                part = nn(mid[k], wd_ref[k, :, lo : lo + n]) + first * bd_ref[k, :, lo : lo + n]
                res[:, k, :, lo : lo + n] = (part * gates[i, k]).astype(BF).reshape(nb, cap, n)

        gather.step0_if(i + 3, False)
        next_load(i + 1)

        @pl.when(i > 0)
        def _():
            group_store(out_hbm, line_order(z, i - 1)).wait()

        combine(i, False)
        group_store(out_hbm, zz).start()
        for k in range(2):
            save_rows(xs_hbm, k, i).wait()
            save(mid, mid_hbm, k, i, 1).wait()
            save(cub, cu_hbm, k, i, 2).wait()
            save(cgb, cg_hbm, k, i, 3).wait()

    group_store(out_hbm, line_order(z, 3)).wait()
    sum_g[...] = jnp.zeros_like(sum_g)
    sum_u[...] = jnp.zeros_like(sum_u)
    sum_d[...] = jnp.zeros_like(sum_d)

    @pl.loop(0, 4)
    def _(i):
        zz = line_order(z, i)
        for k in range(2):
            fetch(mid_hbm, mid, k, i, 1).start()
            fetch(cu_hbm, cub, k, i, 2).start()
            fetch(cg_hbm, cgb, k, i, 3).start()
        gather.step2(i + 5)
        gather.step1(i + 6)
        gather.step0_if(i + 7, True)
        load(i + 4).wait()
        spread(i, False)

        @pl.loop(0, 2)
        def _(k):
            @pl.when(k == 1)
            def _():
                gather.step3(i + 5)

            fetch(mid_hbm, mid, k, i, 1).wait()
            fetch(cu_hbm, cub, k, i, 2).wait()
            fetch(cg_hbm, cgb, k, i, 3).wait()
            g_rows = rows_of(xs, k)
            plain = nt(g_rows, wd_ref[k])
            gate = gates[i, k]
            grad = plain * gate
            g_rows = g_rows.astype(F32)
            dots[k] = jnp.sum(plain * mid[k].astype(F32), axis=1, keepdims=True) + first * jnp.sum(
                g_rows * bd_ref[k], axis=1, keepdims=True
            )
            up_grad = (grad * cub[k].astype(F32)).astype(BF)
            cub[k] = up_grad
            sum_u[k] += jnp.sum(up_grad.astype(F32), axis=0, keepdims=True)
            gate_grad = (grad * cgb[k].astype(F32)).astype(BF)
            cgb[k] = gate_grad
            sum_g[k] += jnp.sum(gate_grad.astype(F32), axis=0, keepdims=True)
            scaled = (g_rows * gate).astype(BF)
            xs[:, k] = scaled.reshape(nb, cap, width)
            sum_d[k] += jnp.sum(scaled.astype(F32), axis=0, keepdims=True)
            save_rows(eg_hbm, k, i).start()
            save(cub, ug_hbm, k, i, 4).start()
            save(cgb, gg_hbm, k, i, 5).start()
            for lo, n in strips(width, 768):
                part = nn(cgb[k], wg_ref[k, :, lo : lo + n]) + nn(cub[k], wu_ref[k, :, lo : lo + n])
                res[:, k, :, lo : lo + n] = part.astype(BF).reshape(nb, cap, n)

        gather.step0_if(i + 7, False)
        next_load(i + 5)

        @pl.when(i > 0)
        def _():
            group_store(row_hbm, line_order(z, i - 1)).wait()

        combine(i, True)
        group_store(row_hbm, zz).start()
        for k in range(2):
            save_rows(eg_hbm, k, i).wait()
            save(cub, ug_hbm, k, i, 4).wait()
            save(cgb, gg_hbm, k, i, 5).wait()

    group_store(row_hbm, line_order(z, 3)).wait()
    gather.finish()


def experts(n_own, g_own, wg_t, b_gate, wu_t, b_up, w_down, b_down, cap, cid):
    rows, wpad = n_own.shape
    ff, width = w_down.shape[1:]
    n, m = 32 * cap, 8 * cap
    free = pl.BlockSpec(memory_space=pl.ANY)
    near = pl.BlockSpec(memory_space=pltpu.VMEM)
    shape = jax.ShapeDtypeStruct
    V = pltpu.VMEM
    D = pltpu.SemaphoreType.DMA
    biases = [b.astype(F32)[:, None] for b in (b_gate, b_up, b_down)]
    out = pl.pallas_call(
        partial(experts_kernel, cap, width),
        out_shape=[shape((2, 4, 8, rows, wpad), BF)]
        + [shape((4, 8, rows, wpad), BF)] * 2
        + [shape((2, 4, 8, cap, width), BF)] * 2
        + [shape((2, 4, m, ff), BF)] * 5
        + [shape((2, 1, ff), F32)] * 2
        + [shape((2, 1, width), F32)],
        in_specs=[free] * 5 + [near] * 3,
        out_specs=[free] * 10 + [near] * 3,
        scratch_shapes=[
            V((2, ff, width), BF), V((2, ff, width), BF), V((2, ff, width), BF),
            V((4, 2, rows, wpad), BF), V((128, rows), F32),
            V((4, 8, 2 * cap, rows), BF), V((4, 8, rows, rows), BF), V((4, 2, m, 1), F32),
            V((8, 2, cap, width), BF), V((8, 2, cap, width), BF),
            V((2, m, ff), BF), V((2, m, ff), BF), V((2, m, ff), BF),
            V((2, m, 1), F32), V((4, 2, rows, wpad), BF),
            D((3,)), D((2,)), D, D, D((6, 2)),
            D((2, 4, 2)), D((2, 4)), D((2, 4, 4)), D((2, 4, 4)), D((2, 4, 2)), D((2, 4, 2)), D((2, 4)), D((2, 4)),
        ],
        compiler_params=pltpu.CompilerParams(
            collective_id=cid, has_side_effects=True, vmem_limit_bytes=63 * 1024 * 1024
        ),
        cost_estimate=pl.CostEstimate(
            flops=24 * n * width * ff, bytes_accessed=300_000_000, transcendentals=6 * n * ff
        ),
        name="experts",
    )(n_own, g_own, wg_t, wu_t, w_down, *biases)
    saved = [v.reshape(2, n, -1) for v in out[3:8]]
    return (*out[1:3], *saved, *(total[:, 0] for total in out[10:]))


def this_slice(
    tokens,
    seq_lengths,
    routes,
    attn_gain,
    w_query,
    b_query,
    w_key,
    b_key,
    w_value,
    b_value,
    sinks,
    w_out,
    b_out,
    ffn_gain,
    w_router,
    b_router,
    w_gate,
    b_gate,
    w_up,
    b_up,
    w_down,
    b_down,
    cotangent,
):
    rows, width = tokens.shape
    fs_size = lax.axis_size("fs")
    ep_size = lax.axis_size("ep")
    my_fs = lax.axis_index("fs")
    my_ep = lax.axis_index("ep")
    blocks = fs_size * ep_size
    expert_count = EXP_DEV * ep_size
    capacity = 3 * rows * TOP // (2 * expert_count)
    shard = w_query.shape[0]
    kv_heads = KEY_VALUE_HEADS // fs_size
    group = QUERY_HEADS // KEY_VALUE_HEADS
    q_cols = kv_heads * group * HEAD_SIZE
    kv_cols = kv_heads * HEAD_SIZE

    spare = (-width) % 128
    small = jnp.concatenate(
        [attn_gain, ffn_gain, b_out, w_router.reshape(-1), b_router, seq_lengths[0].astype(BF)]
    )
    extra = -(-small.shape[0] // (16 * width)) * 16
    small = jnp.pad(small, (0, extra * width - small.shape[0])).reshape(extra, width)
    packed, w_qkv = start_exchange(
        jnp.concatenate([tokens, small], axis=0), w_query, w_key, w_value, 4
    )
    x_group = packed[:, :rows].reshape(fs_size * rows, width).astype(F32)
    small = packed[:, rows:].reshape(fs_size, -1)
    gain_one = small[:, :shard].reshape(-1).astype(F32)
    gain_two = small[:, shard : 2 * shard].reshape(-1).astype(F32)
    bo = small[:, 2 * shard : 3 * shard].reshape(-1).astype(F32)
    at = (3 + expert_count) * shard
    wr = small[:, 3 * shard : at].reshape(width, expert_count)
    br = small[:, at : at + b_router.shape[0]].reshape(-1).astype(F32)
    at += b_router.shape[0]
    lengths = small[:, at : at + seq_lengths.shape[1]].astype(jnp.int32)

    w_qkv = w_qkv.reshape(width, q_cols + 2 * kv_cols)
    b_qkv = jnp.concatenate([b_query, b_key, b_value]).astype(jnp.float32)
    sink_score = sinks.astype(jnp.float32).reshape(1, kv_heads, group, 1)

    x_float = tokens.astype(jnp.float32)
    scale_one = norm_scale(x_float)
    norm_attn = (x_group * norm_scale(x_group) * gain_one).astype(jnp.bfloat16)
    segment_ids, position = jax.vmap(lambda own: layout(own, rows))(lengths)
    cosine_table, sine_table = tables(position.reshape(-1), HEAD_SIZE // 2)
    qkv = jnp.dot(norm_attn, w_qkv, preferred_element_type=jnp.float32) + b_qkv
    many = fs_size * rows
    heads = kv_heads * group
    query = apply_rotation(
        qkv[:, :q_cols].reshape(many, heads, HEAD_SIZE), cosine_table, sine_table
    ).astype(jnp.bfloat16)
    query = query.reshape(fs_size, rows, kv_heads, group, HEAD_SIZE)
    key = apply_rotation(
        qkv[:, q_cols : q_cols + kv_cols].reshape(many, kv_heads, HEAD_SIZE),
        cosine_table,
        sine_table,
    ).astype(jnp.bfloat16)
    key = key.reshape(fs_size, rows, kv_heads, HEAD_SIZE)
    value = qkv[:, q_cols + kv_cols :].astype(jnp.bfloat16)
    value = value.reshape(fs_size, rows, kv_heads, HEAD_SIZE)
    places = jnp.arange(rows, dtype=jnp.int32)
    allowed = (segment_ids[:, :, None] == segment_ids[:, None, :]) & (
        places[:, None] >= places[None, :]
    )
    scores = mm("bqhgd,bkhd->bhgqk", query, key) * HEAD_SIZE ** (-0.5)
    masked = jnp.where(allowed[:, None, None], scores, MASKED_SCORE)
    top_score = jnp.maximum(jnp.max(masked, axis=-1), sink_score)
    exponent = jnp.exp(masked - top_score[..., None])
    sink_exp = jnp.exp(sink_score - top_score)
    denominator = jnp.sum(exponent, axis=-1) + sink_exp
    probs = exponent / denominator[..., None]
    sink_prob = sink_exp / denominator
    probs_b = probs.astype(jnp.bfloat16)
    mixed = mm("bhgqk,bkhd->bqhgd", probs_b, value).astype(jnp.bfloat16)
    mixed = mixed.reshape(many, q_cols)
    out_part = jnp.dot(mixed, w_out, preferred_element_type=jnp.float32)
    resid = x_float + scatter_fs(out_part.astype(jnp.bfloat16)).astype(jnp.float32) + bo
    scale_two = norm_scale(resid)
    norm_ffn = (resid * scale_two * gain_two).astype(jnp.bfloat16)

    logits = jnp.dot(norm_ffn, wr, preferred_element_type=F32) + br
    one_hot = (routes[:, :, None] == jnp.arange(expert_count, dtype=jnp.int32)).astype(F32)
    member = jnp.sum(one_hot, axis=1)
    peak = jnp.max(jnp.where(member > 0, logits, MASKED_SCORE), axis=-1, keepdims=True)
    gate_exp = jnp.where(member > 0, jnp.exp(logits - peak), 0.0)
    gates_here = gate_exp / jnp.sum(gate_exp, axis=-1, keepdims=True)
    place = jnp.where(member > 0, jnp.cumsum(member, axis=0) - member, -1.0)
    gate_high = lax.reduce_precision(gates_here, 8, 7)
    block = jnp.concatenate(
        [norm_ffn]
        + [v.astype(BF) for v in (place, gate_high, gates_here - gate_high)]
        + [jnp.zeros((rows, spare - 3 * expert_count), BF)],
        axis=1,
    )
    wg_t = jnp.swapaxes(w_gate, 1, 2)
    wu_t = jnp.swapaxes(w_up, 1, 2)
    (
        out_part,
        row_part,
        x_slots,
        expert_grad,
        middle,
        up_grad,
        gate_grad_pre,
        grad_b_gate,
        grad_b_up,
        grad_b_down,
    ) = experts(
        block,
        jnp.pad(cotangent, ((0, 0), (0, spare))),
        wg_t,
        b_gate,
        wu_t,
        b_up,
        w_down,
        b_down,
        capacity,
        1,
    )
    sums = scatter_blocks([out_part, row_part], 2)
    block_out = resid + sums[0, :, :width].astype(F32)
    grad_w_down = mm("erf,erd->efd", middle, expert_grad)
    grad_w_gate = jnp.swapaxes(mm("erf,erd->efd", gate_grad_pre, x_slots), 1, 2)
    grad_w_up = jnp.swapaxes(mm("erf,erd->efd", up_grad, x_slots), 1, 2)
    row_sum = sums[1].astype(F32)
    gate_grad = row_sum[:, width : width + expert_count]
    logit_grad = gates_here * (
        gate_grad - jnp.sum(gates_here * gate_grad, axis=-1, keepdims=True)
    )
    logit_grad = logit_grad.astype(jnp.bfloat16)
    grad_br = jnp.sum(logit_grad, axis=0, dtype=jnp.float32)
    grad_wr = left_dot(norm_ffn, logit_grad)
    norm_ffn_grad = row_sum[:, :width] + jnp.dot(
        logit_grad, wr.T, preferred_element_type=jnp.float32
    )
    resid_norm_grad, grad_gain_two = norm_back(resid, scale_two, gain_two, norm_ffn_grad)
    resid_grad = cotangent.astype(jnp.float32) + resid_norm_grad

    branch_grad = gather_fs(resid_grad.astype(jnp.bfloat16))
    grad_bo = jnp.sum(branch_grad, axis=0, dtype=jnp.float32)
    mixed_grad = mm("td,fd->tf", branch_grad, w_out).astype(jnp.bfloat16)
    mixed_grad = mixed_grad.reshape(fs_size, rows, kv_heads, group, HEAD_SIZE)
    grad_probs = mm("bqhgd,bkhd->bhgqk", mixed_grad, value)
    value_grad = mm("bhgqk,bqhgd->bkhd", probs_b, mixed_grad)
    row_delta = jnp.sum(probs * grad_probs, axis=-1)
    score_grad = (probs * (grad_probs - row_delta[..., None])).astype(jnp.bfloat16)
    query_grad = mm("bhgqk,bkhd->bqhgd", score_grad, key) * HEAD_SIZE ** (-0.5)
    key_grad = mm("bhgqk,bqhgd->bkhd", score_grad, query) * HEAD_SIZE ** (-0.5)
    grad_sink = -jnp.sum(sink_prob * row_delta, axis=(0, 3)).reshape(-1)
    query_pre_grad = undo_rotation(
        query_grad.reshape(many, heads, HEAD_SIZE), cosine_table, sine_table
    ).reshape(many, q_cols)
    key_pre_grad = undo_rotation(
        key_grad.reshape(many, kv_heads, HEAD_SIZE), cosine_table, sine_table
    ).reshape(many, kv_cols)
    qkv_grad = jnp.concatenate(
        [query_pre_grad, key_pre_grad, value_grad.reshape(many, kv_cols)], axis=1
    ).astype(jnp.bfloat16)
    grad_b_qkv = jnp.sum(qkv_grad, axis=0, dtype=jnp.float32)
    norm_attn_grad = scatter_fs(
        mm("tf,df->td", qkv_grad, w_qkv).astype(jnp.bfloat16)
    ).astype(jnp.float32)
    input_norm_grad, grad_gain_one = norm_back(x_float, scale_one, gain_one, norm_attn_grad)
    grad_tokens = resid_grad + input_norm_grad
    by_shard = jnp.concatenate(
        [
            grad_wr.reshape(fs_size, -1),
            grad_gain_one.reshape(fs_size, -1),
            grad_gain_two.reshape(fs_size, -1),
            grad_br.reshape(fs_size, -1),
        ],
        axis=1,
    ).astype(BF)
    own = jnp.concatenate(
        [grad_b_qkv, grad_sink, lax.dynamic_slice_in_dim(grad_bo, my_fs * shard, shard)]
    ).astype(BF)
    cols = q_cols + 2 * kv_cols
    slab_rows, slab_part = 768, 128
    wide_part = 144
    own = jnp.where(jnp.arange(fs_size)[:, None] == my_fs, own, jnp.zeros((), BF))
    by_shard = jnp.concatenate([by_shard, own], axis=1)
    small_n = by_shard.shape[1]
    small_rows = -(-small_n // q_cols)
    by_shard = jnp.pad(by_shard, ((0, 0), (0, small_rows * q_cols - small_n)))
    norm_pad = jnp.pad(
        norm_attn.reshape(many, fs_size, shard), ((0, 0), (0, 0), (0, slab_rows - shard))
    ).reshape(many, fs_size * slab_rows)
    gq = left_dot(norm_pad, qkv_grad).astype(BF).reshape(fs_size, slab_rows, cols)
    gq = gq.at[:, shard : shard + small_rows, :q_cols].set(
        by_shard.reshape(fs_size, small_rows, q_cols)
    )
    gq = gq.reshape(fs_size, 2, slab_rows // (2 * slab_part), slab_part, cols)
    gw = left_dot(branch_grad, mixed).astype(BF)
    gw = gw.reshape(2, width // (2 * wide_part), wide_part, q_cols)
    tw, tq, tk, tv = reduce_parts(gw, gq, (q_cols, kv_cols, kv_cols), 3)
    sum_wo = jnp.swapaxes(tw.reshape(width, q_cols).astype(F32), 0, 1)
    sum_wq = tq[:shard].astype(F32)
    sum_wk = tk[:shard].astype(F32)
    sum_wv = tv[:shard].astype(F32)
    by_shard = jnp.sum(
        tq[shard : shard + small_rows].astype(F32).reshape(small_rows, fs_size, q_cols), axis=1
    ).reshape(-1)
    sum_wr = by_shard[: shard * expert_count].reshape(shard, expert_count)
    rest = by_shard[shard * expert_count : small_n - own.shape[1]]
    own = by_shard[small_n - own.shape[1] : small_n]
    sum_b = own[:cols]
    return (
        block_out.astype(jnp.bfloat16),
        grad_tokens,
        rest[:shard],
        sum_wq,
        sum_b[:q_cols],
        sum_wk,
        sum_b[q_cols : q_cols + kv_cols],
        sum_wv,
        sum_b[q_cols + kv_cols :],
        own[q_cols + 2 * kv_cols : q_cols + 2 * kv_cols + heads],
        sum_wo,
        own[q_cols + 2 * kv_cols + heads :],
        rest[shard : 2 * shard],
        sum_wr,
        rest[2 * shard :],
        grad_w_gate,
        grad_b_gate,
        grad_w_up,
        grad_b_up,
        grad_w_down,
        grad_b_down,
    )


def any_slice(
    tokens,
    seq_lengths,
    routes,
    attn_gain,
    w_query,
    b_query,
    w_key,
    b_key,
    w_value,
    b_value,
    sinks,
    w_out,
    b_out,
    ffn_gain,
    w_router,
    b_router,
    w_gate,
    b_gate,
    w_up,
    b_up,
    w_down,
    b_down,
    cotangent,
):
    rows, width = tokens.shape
    fs_size = lax.axis_size("fs")
    ep_size = lax.axis_size("ep")
    my_fs = lax.axis_index("fs")
    my_ep = lax.axis_index("ep")
    blocks = fs_size * ep_size
    expert_count = EXP_DEV * ep_size
    capacity = 3 * rows * TOP // (2 * expert_count)
    shard = w_query.shape[0]
    kv_heads = KEY_VALUE_HEADS // fs_size
    group = QUERY_HEADS // KEY_VALUE_HEADS
    q_cols = kv_heads * group * HEAD_SIZE
    kv_cols = kv_heads * HEAD_SIZE

    packed = jnp.concatenate(
        [attn_gain, ffn_gain, b_out, w_router.reshape(-1), b_router]
    )
    packed = lax.all_gather(packed, "fs", axis=0)
    gain_one = packed[:, :shard].reshape(-1).astype(jnp.float32)
    gain_two = packed[:, shard : 2 * shard].reshape(-1).astype(jnp.float32)
    bo = packed[:, 2 * shard : 3 * shard].reshape(-1).astype(jnp.float32)
    wr = packed[:, 3 * shard : (3 + expert_count) * shard].reshape(width, expert_count)
    br = packed[:, (3 + expert_count) * shard :].reshape(-1).astype(jnp.float32)
    whole_numbers = gather_all(
        jnp.concatenate([routes.reshape(-1), seq_lengths.reshape(-1)])[None]
    )
    routes_all = whole_numbers[:, : rows * TOP].reshape(blocks, rows, TOP)
    lengths_all = whole_numbers[:, rows * TOP :]
    lengths = lax.dynamic_index_in_dim(
        lengths_all.reshape(fs_size, ep_size, -1), my_ep, 1, keepdims=False
    )
    g_all = gather_all(cotangent)

    w_qkv = jnp.concatenate(
        [
            w_query.reshape(shard, fs_size, q_cols),
            w_key.reshape(shard, fs_size, kv_cols),
            w_value.reshape(shard, fs_size, kv_cols),
        ],
        axis=2,
    )
    w_qkv = lax.all_to_all(w_qkv, "fs", split_axis=1, concat_axis=0, tiled=True)
    w_qkv = w_qkv.reshape(width, q_cols + 2 * kv_cols)
    b_qkv = jnp.concatenate([b_query, b_key, b_value]).astype(jnp.float32)
    sink_score = sinks.astype(jnp.float32).reshape(1, kv_heads, group, 1)

    x_float = tokens.astype(jnp.float32)
    scale_one = norm_scale(x_float)
    norm_attn = gather_fs((x_float * scale_one * gain_one).astype(jnp.bfloat16))
    segment_ids, position = jax.vmap(lambda own: layout(own, rows))(lengths)
    cosine_table, sine_table = tables(position.reshape(-1), HEAD_SIZE // 2)
    qkv = jnp.dot(norm_attn, w_qkv, preferred_element_type=jnp.float32) + b_qkv
    many = fs_size * rows
    heads = kv_heads * group
    query = apply_rotation(
        qkv[:, :q_cols].reshape(many, heads, HEAD_SIZE), cosine_table, sine_table
    ).astype(jnp.bfloat16)
    query = query.reshape(fs_size, rows, kv_heads, group, HEAD_SIZE)
    key = apply_rotation(
        qkv[:, q_cols : q_cols + kv_cols].reshape(many, kv_heads, HEAD_SIZE),
        cosine_table,
        sine_table,
    ).astype(jnp.bfloat16)
    key = key.reshape(fs_size, rows, kv_heads, HEAD_SIZE)
    value = qkv[:, q_cols + kv_cols :].astype(jnp.bfloat16)
    value = value.reshape(fs_size, rows, kv_heads, HEAD_SIZE)
    places = jnp.arange(rows, dtype=jnp.int32)
    allowed = (segment_ids[:, :, None] == segment_ids[:, None, :]) & (
        places[:, None] >= places[None, :]
    )
    scores = mm("bqhgd,bkhd->bhgqk", query, key) * HEAD_SIZE ** (-0.5)
    masked = jnp.where(allowed[:, None, None], scores, MASKED_SCORE)
    top_score = jnp.maximum(jnp.max(masked, axis=-1), sink_score)
    exponent = jnp.exp(masked - top_score[..., None])
    sink_exp = jnp.exp(sink_score - top_score)
    denominator = jnp.sum(exponent, axis=-1) + sink_exp
    probs = exponent / denominator[..., None]
    sink_prob = sink_exp / denominator
    probs_b = probs.astype(jnp.bfloat16)
    mixed = mm("bhgqk,bkhd->bqhgd", probs_b, value).astype(jnp.bfloat16)
    mixed = mixed.reshape(many, q_cols)
    out_part = jnp.dot(mixed, w_out, preferred_element_type=jnp.float32)
    resid = x_float + scatter_fs(out_part.astype(jnp.bfloat16)).astype(jnp.float32) + bo
    scale_two = norm_scale(resid)
    norm_ffn = (resid * scale_two * gain_two).astype(jnp.bfloat16)

    n_all = gather_all(norm_ffn)
    logits = jnp.dot(n_all, wr, preferred_element_type=jnp.float32) + br
    logits = logits.reshape(blocks, rows, expert_count)
    one_hot = (
        routes_all[:, :, :, None] == jnp.arange(expert_count, dtype=jnp.int32)
    ).astype(jnp.float32)
    member = jnp.sum(one_hot, axis=2)
    peak = jnp.max(jnp.where(member > 0, logits, MASKED_SCORE), axis=-1, keepdims=True)
    gate_exp = jnp.where(member > 0, jnp.exp(logits - peak), 0.0)
    gates = gate_exp / jnp.sum(gate_exp, axis=-1, keepdims=True)
    own_member = lax.dynamic_slice_in_dim(member, my_ep * EXP_DEV, EXP_DEV, axis=2)
    own_gates = lax.dynamic_slice_in_dim(gates, my_ep * EXP_DEV, EXP_DEV, axis=2)
    rank = jnp.cumsum(own_member, axis=1) - own_member
    slots = jnp.arange(capacity, dtype=jnp.float32)
    pick = (rank.transpose(0, 2, 1)[:, :, None, :] == slots[:, None]) & (
        own_member.transpose(0, 2, 1)[:, :, None, :] > 0
    )
    pick_b = pick.astype(jnp.bfloat16)
    slot_gate = jnp.sum(
        jnp.where(pick, own_gates.transpose(0, 2, 1)[:, :, None, :], 0.0), axis=-1
    )
    slot_gate = slot_gate.transpose(1, 0, 2).reshape(EXP_DEV, blocks * capacity, 1)

    def spread(full):
        parts = mm("bekt,btd->ebkd", pick_b, full.reshape(blocks, rows, -1))
        return parts.astype(jnp.bfloat16).reshape(EXP_DEV, blocks * capacity, -1)

    def combine(parts):
        parts = parts.reshape(EXP_DEV, blocks, capacity, -1)
        return mm("bekt,ebkd->btd", pick_b, parts).reshape(blocks * rows, -1)

    x_slots = spread(n_all)
    g_slots = spread(g_all)
    gate_pre = mm("erd,edf->erf", x_slots, w_gate) + b_gate.astype(jnp.float32)[:, None]
    up_pre = mm("erd,edf->erf", x_slots, w_up) + b_up.astype(jnp.float32)[:, None]
    gate_soft = CLAMP_LIMIT * jnp.tanh(gate_pre / CLAMP_LIMIT)
    up_soft = CLAMP_LIMIT * jnp.tanh(up_pre / CLAMP_LIMIT)
    gate_sig = jax.nn.sigmoid(SWIGLU_ALPHA * gate_soft)
    glu_part = gate_soft * gate_sig
    middle = ((up_soft + 1.0) * glu_part).astype(jnp.bfloat16)
    first = (my_fs == 0).astype(jnp.float32)
    down_bias = b_down.astype(jnp.float32) * first
    expert_out = mm("erf,efd->erd", middle, w_down) + down_bias[:, None]
    expert_sum = scatter_all(
        combine((expert_out * slot_gate).astype(jnp.bfloat16)).astype(jnp.bfloat16)
    )
    block_out = resid + expert_sum.astype(jnp.float32)

    expert_grad = (g_slots.astype(jnp.float32) * slot_gate).astype(jnp.bfloat16)
    plain_grad = mm("erd,efd->erf", g_slots, w_down)
    middle_grad = plain_grad * slot_gate
    gate_dot = jnp.sum(plain_grad * middle.astype(jnp.float32), axis=-1) + jnp.sum(
        g_slots.astype(jnp.float32) * down_bias[:, None], axis=-1
    )
    grad_w_down = mm("erf,erd->efd", middle, expert_grad)
    grad_b_down = jnp.sum(expert_grad, axis=1, dtype=jnp.float32)
    up_grad = (middle_grad * glu_part * (1.0 - (up_soft / CLAMP_LIMIT) ** 2)).astype(jnp.bfloat16)
    gate_grad_pre = (
        middle_grad
        * (up_soft + 1.0)
        * (gate_sig + SWIGLU_ALPHA * gate_soft * gate_sig * (1.0 - gate_sig))
        * (1.0 - (gate_soft / CLAMP_LIMIT) ** 2)
    ).astype(jnp.bfloat16)
    grad_w_gate = mm("erd,erf->edf", x_slots, gate_grad_pre)
    grad_b_gate = jnp.sum(gate_grad_pre, axis=1, dtype=jnp.float32)
    grad_w_up = mm("erd,erf->edf", x_slots, up_grad)
    grad_b_up = jnp.sum(up_grad, axis=1, dtype=jnp.float32)
    row_part = mm("erf,edf->erd", gate_grad_pre, w_gate) + mm("erf,edf->erd", up_grad, w_up)
    row_sum = combine(row_part.astype(jnp.bfloat16))
    own_dot = jnp.sum(
        jnp.where(pick, gate_dot.reshape(EXP_DEV, blocks, capacity).transpose(1, 0, 2)[..., None], 0.0),
        axis=2,
    )
    dots = jnp.sum(
        own_dot[..., None]
        * (
            (my_ep * EXP_DEV + jnp.arange(EXP_DEV))[:, None] == jnp.arange(expert_count)[None]
        ).astype(jnp.float32)[None, :, None, :],
        axis=1,
    ).reshape(blocks * rows, expert_count)
    row_sum = scatter_all(jnp.concatenate([row_sum, dots], axis=1).astype(jnp.bfloat16))
    row_sum = row_sum.astype(jnp.float32)
    gate_grad = row_sum[:, width:]
    mine = my_fs * ep_size + my_ep
    gates_here = lax.dynamic_index_in_dim(gates, mine, 0, keepdims=False)
    logit_grad = gates_here * (
        gate_grad - jnp.sum(gates_here * gate_grad, axis=-1, keepdims=True)
    )
    logit_grad = logit_grad.astype(jnp.bfloat16)
    grad_br = jnp.sum(logit_grad, axis=0, dtype=jnp.float32)
    grad_wr = left_dot(norm_ffn, logit_grad)
    norm_ffn_grad = row_sum[:, :width] + jnp.dot(
        logit_grad, wr.T, preferred_element_type=jnp.float32
    )
    resid_norm_grad, grad_gain_two = norm_back(resid, scale_two, gain_two, norm_ffn_grad)
    resid_grad = cotangent.astype(jnp.float32) + resid_norm_grad

    branch_grad = gather_fs(resid_grad.astype(jnp.bfloat16))
    grad_bo = jnp.sum(branch_grad, axis=0, dtype=jnp.float32)
    mixed_grad = mm("td,fd->tf", branch_grad, w_out).astype(jnp.bfloat16)
    mixed_grad = mixed_grad.reshape(fs_size, rows, kv_heads, group, HEAD_SIZE)
    grad_wo = left_dot(mixed, branch_grad)
    grad_probs = mm("bqhgd,bkhd->bhgqk", mixed_grad, value)
    value_grad = mm("bhgqk,bqhgd->bkhd", probs_b, mixed_grad)
    row_delta = jnp.sum(probs * grad_probs, axis=-1)
    score_grad = (probs * (grad_probs - row_delta[..., None])).astype(jnp.bfloat16)
    query_grad = mm("bhgqk,bkhd->bqhgd", score_grad, key) * HEAD_SIZE ** (-0.5)
    key_grad = mm("bhgqk,bqhgd->bkhd", score_grad, query) * HEAD_SIZE ** (-0.5)
    grad_sink = -jnp.sum(sink_prob * row_delta, axis=(0, 3)).reshape(-1)
    query_pre_grad = undo_rotation(
        query_grad.reshape(many, heads, HEAD_SIZE), cosine_table, sine_table
    ).reshape(many, q_cols)
    key_pre_grad = undo_rotation(
        key_grad.reshape(many, kv_heads, HEAD_SIZE), cosine_table, sine_table
    ).reshape(many, kv_cols)
    qkv_grad = jnp.concatenate(
        [query_pre_grad, key_pre_grad, value_grad.reshape(many, kv_cols)], axis=1
    ).astype(jnp.bfloat16)
    grad_b_qkv = jnp.sum(qkv_grad, axis=0, dtype=jnp.float32)
    norm_attn_grad = scatter_fs(
        mm("tf,df->td", qkv_grad, w_qkv).astype(jnp.bfloat16)
    ).astype(jnp.float32)
    input_norm_grad, grad_gain_one = norm_back(x_float, scale_one, gain_one, norm_attn_grad)
    grad_tokens = resid_grad + input_norm_grad
    grad_qkv = left_dot(norm_attn, qkv_grad).astype(jnp.bfloat16)
    if shard % ep_size == 0:
        grad_qkv = grad_qkv.reshape(fs_size, ep_size, shard // ep_size, q_cols + 2 * kv_cols)
        grad_qkv = lax.psum_scatter(grad_qkv, "ep", scatter_dimension=1, tiled=False)
        grad_qkv = lax.all_to_all(grad_qkv, "fs", split_axis=0, concat_axis=1, tiled=False)
        grad_qkv = lax.all_gather(grad_qkv, "ep", axis=0, tiled=True).astype(jnp.float32)
    else:
        grad_qkv = lax.psum(grad_qkv.reshape(fs_size, shard, q_cols + 2 * kv_cols), "ep")
        grad_qkv = lax.all_to_all(grad_qkv, "fs", split_axis=0, concat_axis=1, tiled=False)
        grad_qkv = grad_qkv.astype(jnp.float32)
    sum_wq = grad_qkv[:, :, :q_cols].reshape(shard, -1)
    sum_wk = grad_qkv[:, :, q_cols : q_cols + kv_cols].reshape(shard, -1)
    sum_wv = grad_qkv[:, :, q_cols + kv_cols :].reshape(shard, -1)
    sum_wo = lax.psum(grad_wo.astype(jnp.bfloat16), "ep").astype(jnp.float32)
    by_shard = jnp.concatenate(
        [
            grad_wr.reshape(fs_size, -1),
            grad_gain_one.reshape(fs_size, -1),
            grad_gain_two.reshape(fs_size, -1),
            grad_br.reshape(fs_size, -1),
        ],
        axis=1,
    )
    by_shard = lax.psum(by_shard, ("fs", "ep"))
    by_shard = lax.dynamic_index_in_dim(by_shard, my_fs, 0, keepdims=False)
    sum_wr = by_shard[: shard * expert_count].reshape(shard, expert_count)
    rest = by_shard[shard * expert_count :]
    own = jnp.concatenate(
        [
            grad_b_qkv,
            grad_sink,
            lax.dynamic_slice_in_dim(grad_bo, my_fs * shard, shard),
        ]
    )
    own = lax.psum(own, "ep")
    sum_b = own[: q_cols + 2 * kv_cols]
    return (
        block_out.astype(jnp.bfloat16),
        grad_tokens,
        rest[:shard],
        sum_wq,
        sum_b[:q_cols],
        sum_wk,
        sum_b[q_cols : q_cols + kv_cols],
        sum_wv,
        sum_b[q_cols + kv_cols :],
        own[q_cols + 2 * kv_cols : q_cols + 2 * kv_cols + heads],
        sum_wo,
        own[q_cols + 2 * kv_cols + heads :],
        rest[shard : 2 * shard],
        sum_wr,
        rest[2 * shard :],
        grad_w_gate,
        grad_b_gate,
        grad_w_up,
        grad_b_up,
        grad_w_down,
        grad_b_down,
    )


def solution(mesh):
    in_specs = (
        P(("fs", "ep"), None),
        P(("fs", "ep"), None),
        P(("fs", "ep"), None),
        P("fs"),
        P("fs", None),
        P("fs"),
        P("fs", None),
        P("fs"),
        P("fs", None),
        P("fs"),
        P("fs"),
        P("fs", None),
        P("fs"),
        P("fs"),
        P("fs", None),
        P("fs"),
        P("ep", None, "fs"),
        P("ep", "fs"),
        P("ep", None, "fs"),
        P("ep", "fs"),
        P("ep", "fs", None),
        P("ep", None),
        P(("fs", "ep"), None),
    )
    out_specs = (
        P(("fs", "ep"), None),
        P(("fs", "ep"), None),
        P("fs"),
        P("fs", None),
        P("fs"),
        P("fs", None),
        P("fs"),
        P("fs", None),
        P("fs"),
        P("fs"),
        P("fs", None),
        P("fs"),
        P("fs"),
        P("fs", None),
        P("fs"),
        P("ep", None, "fs"),
        P("ep", "fs"),
        P("ep", None, "fs"),
        P("ep", "fs"),
        P("ep", "fs", None),
        P("ep", None),
    )
    run = this_slice if (mesh.shape["fs"], mesh.shape["ep"]) == (4, 8) else any_slice
    return jax.shard_map(
        run, mesh=mesh, in_specs=in_specs, out_specs=out_specs, check_vma=False
    )
```

```python
from functools import partial

import jax
import jax.numpy as jnp
from jax import lax
from jax.experimental import pallas as pl
from jax.experimental.pallas import tpu as pltpu
from jax.sharding import PartitionSpec as P

QUERY_HEADS = 64
KEY_VALUE_HEADS = 8
HEAD_SIZE = 64
TOP = 4
EXP_DEV = 2


EPSILON = 1e-05
ROPE_BASE = 150000.0
SWIGLU_ALPHA = 1.702
CLAMP_LIMIT = 7.0
MASKED_SCORE = -1e30


F32 = jnp.float32
BF = jnp.bfloat16
MESH = pl.DeviceIdType.MESH


def layout(lengths, card_rows):
    seq_ends = jnp.cumsum(lengths)
    places = jnp.arange(card_rows, dtype=jnp.int32)
    past_end = (places[:, None] >= seq_ends[None, :]).astype(jnp.int32)
    segment_ids = jnp.sum(past_end, axis=1)
    position = places - jnp.sum(past_end * lengths[None, :], axis=1)
    return (segment_ids, position)


def tables(position, half_dim):
    inv_freq = jnp.exp(-jnp.log(ROPE_BASE) * jnp.arange(half_dim, dtype=jnp.float32) / half_dim)
    angles = position.astype(jnp.float32)[:, None] * inv_freq[None, :]
    return (jnp.cos(angles)[:, None, :], jnp.sin(angles)[:, None, :])


def apply_rotation(value_matrix, cosine_table, sine_table):
    half_dim = value_matrix.shape[-1] // 2
    lower_half = value_matrix[..., :half_dim]
    upper_half = value_matrix[..., half_dim:]
    return jnp.concatenate(
        [
            lower_half * cosine_table - upper_half * sine_table,
            upper_half * cosine_table + lower_half * sine_table,
        ],
        axis=-1,
    )


def undo_rotation(value_matrix, cosine_table, sine_table):
    half_dim = value_matrix.shape[-1] // 2
    lower_half = value_matrix[..., :half_dim]
    upper_half = value_matrix[..., half_dim:]
    return jnp.concatenate(
        [
            lower_half * cosine_table + upper_half * sine_table,
            upper_half * cosine_table - lower_half * sine_table,
        ],
        axis=-1,
    )


def norm_scale(value_matrix):
    return lax.rsqrt(jnp.mean(value_matrix * value_matrix, axis=-1, keepdims=True) + EPSILON)


def norm_back(value_matrix, inv_scale, gain, grad_norm):
    weighted = grad_norm * gain
    grad_values = inv_scale * weighted - value_matrix * inv_scale**3 * jnp.mean(
        weighted * value_matrix, axis=-1, keepdims=True
    )
    grad_gain = jnp.sum(grad_norm * value_matrix * inv_scale, axis=0)
    return (grad_values, grad_gain)


def left_dot(left, right):
    return jnp.dot(left.T, right, preferred_element_type=jnp.float32)


def mm(spec, left, right):
    return jnp.einsum(spec, left, right, preferred_element_type=jnp.float32)


def gather_all(value):
    return lax.all_gather(value, ("fs", "ep"), axis=0, tiled=True)


def scatter_all(value):
    return lax.psum_scatter(value, ("fs", "ep"), scatter_dimension=0, tiled=True)


def gather_fs(value):
    return lax.all_gather(value, "fs", axis=0, tiled=True)


def scatter_fs(value):
    return lax.psum_scatter(value, "fs", scatter_dimension=0, tiled=True)


def spot():
    fs=lax.axis_index("fs"); ep=lax.axis_index("ep")
    return fs, ep, fs//2, fs%2, ep//2, ep%2

def greet(fs, ep, z, more=0):
    y, x, c = fs//2, fs%2, ep%2
    bar=pltpu.get_barrier_semaphore()
    def hi(f,e): pl.semaphore_signal(bar,inc=1,device_id=(f,e),device_id_type=MESH)
    hi(fs+1-2*x,ep); hi(fs+2-4*y,ep); hi(fs,ep+1-2*c)
    if more: hi(3-fs,ep)
    @pl.when(z>0)
    def _(): hi(fs,ep-2)
    @pl.when(z<3)
    def _(): hi(fs,ep+2)
    @pl.when((z>0)&(z<3))
    def _(): pl.semaphore_wait(bar,5+more)
    @pl.when((z==0)|(z==3))
    def _(): pl.semaphore_wait(bar,4+more)

def scatter_kernel(na, parts, *refs):
    ps=refs[:na]; out=refs[na]; far=refs[na+1]
    q,v1,v2,vu,vd,stg,load,s0,r0,gsem,s1,r1,s2,r2,su,ru,sd,rd,osem = refs[na+2:]
    fs,ep,y,x,z,c = spot()
    rows=ps[0].shape[2]; pr=rows//parts; half=pr//2
    items=na*4*parts
    xn=(fs+1-2*x,ep); yn=(fs+2-4*y,ep); cn=(fs,ep+1-2*c)
    A=pl.ds(0,half); B=pl.ds(half,half)
    def rem(src,dst,s,r,dev): return pltpu.make_async_remote_copy(src,dst,s,r,device_id=dev,device_id_type=MESH)
    def where(i):
        a=i//(4*parts); j=i%(4*parts); k=j//parts; part=j%parts
        zz=(k%2)*(k//2)+(1-k%2)*(3-k//2)
        return a,part,zz
    def block(i,par):
        a,part,zz=where(i)
        return a,zz*2+par,pl.ds(part*pr,pr)
    def on_array(i,f):
        if na==1: f(ps[0])
        else:
            a=i//(4*parts)
            for n in range(na):
                @pl.when(a==n)
                def _(): f(ps[n])
    def give(i,p):
        _,e,r=block(i,1-c)
        return rem(p.at[:,e,r],far.at[i],s0.at[i],r0.at[i],cn)
    def mine(i,p):
        _,e,r=block(i,c)
        return pltpu.make_async_copy(p.at[:,e,r],q.at[i],load.at[i])
    def fetch(i):
        return pltpu.make_async_copy(far.at[i],stg.at[i%2],gsem.at[i%2])
    def one(i):
        return ([rem(q.at[i,2*j+1-x,A],v1.at[i,0,j],s1.at[i,j],r1.at[i,j],xn) for j in range(2)],
                rem(q.at[i,pl.ds((1-y)*2,2),B],v1.at[i,1],s1.at[i,2],r1.at[i,2],yn))
    def two(i):
        return (rem(q.at[i,(1-y)*2+x,A],v2.at[i,0],s2.at[i,0],r2.at[i,0],yn),
                rem(q.at[i,y*2+1-x,B],v2.at[i,1],s2.at[i,1],r2.at[i,1],xn))
    def up(i): return rem(q.at[i,fs],vu.at[i],su.at[i],ru.at[i],(fs,ep+2))
    def down(i): return rem(q.at[i,fs],vd.at[i],sd.at[i],rd.at[i],(fs,ep-2))
    greet(fs,ep,z)
    @pl.loop(0,items)
    def _(i):
        on_array(i,lambda p: give(i,p).start())
        on_array(i,lambda p: mine(i,p).start())
    def valid(i): return (i>=0)&(i<items)
    def add(dst,src,n):
        for lo in range(0,n,16):
            s=pl.ds(lo,16)
            dst(s,src(s))
    def getfar(i):
        on_array(i,lambda p: give(i,p).wait_recv())
        fetch(i).start()
    getfar(0)
    @pl.loop(0,items+6)
    def _(t):
        @pl.when(t<items)
        def _():
            i=t
            @pl.when(i+1<items)
            def _(): getfar(i+1)
            fetch(i).wait()
            on_array(i,lambda p: mine(i,p).wait())
            for g in range(4):
                q[i,g]=q[i,g]+stg[i%2,g]
            a,b=one(i)
            for k in a: k.start()
            b.start()
        i=t-1
        @pl.when(valid(i))
        def _():
            a,b=one(i)
            for k in a: k.wait_recv()
            for j in range(2):
                q[i,2*j+x,A]=q[i,2*j+x,A]+v1[i,0,j]
            ta,tb=two(i)
            ta.start()
            b.wait_recv()
            for j in range(2):
                q[i,2*y+j,B]=q[i,2*y+j,B]+v1[i,1,j]
            tb.start()
        i2=t-2
        @pl.when(valid(i2))
        def _():
            ta,tb=two(i2)
            ta.wait_recv()
            q[i2,fs,A]=q[i2,fs,A]+v2[i2,0]
            tb.wait_recv()
            q[i2,fs,B]=q[i2,fs,B]+v2[i2,1]
        iu=t-2-z
        @pl.when(valid(iu))
        def _():
            _,_,zz=where(iu)
            @pl.when(zz>=z)
            def _():
                @pl.when(z>0)
                def _():
                    up(iu).wait_recv()
                    q[iu,fs]=q[iu,fs]+vu[iu]
                @pl.when(zz>z)
                def _(): up(iu).start()
        idn=t-2-(3-z)
        @pl.when(valid(idn))
        def _():
            _,_,zz=where(idn)
            @pl.when(zz<=z)
            def _():
                @pl.when(z<3)
                def _():
                    down(idn).wait_recv()
                    q[idn,fs]=q[idn,fs]+vd[idn]
                @pl.when(zz<z)
                def _(): down(idn).start()
    @pl.loop(0,items)
    def _(i):
        a,part,zz=where(i)
        @pl.when(zz==z)
        def _():
            pltpu.make_async_copy(q.at[i,fs],out.at[a,pl.ds(part*pr,pr)],osem.at[i]).start()
    @pl.loop(0,items)
    def _(i):
        a,part,zz=where(i)
        on_array(i,lambda p: give(i,p).wait_send())
        a1,b1=one(i)
        for k in a1: k.wait_send()
        b1.wait_send()
        ta,tb=two(i); ta.wait_send(); tb.wait_send()
        @pl.when(zz>z)
        def _(): up(i).wait_send()
        @pl.when(zz<z)
        def _(): down(i).wait_send()
        @pl.when(zz==z)
        def _(): pltpu.make_async_copy(q.at[i,fs],out.at[a,pl.ds(part*pr,pr)],osem.at[i]).wait()

def scatter_blocks(arrays, cid, parts=2):
    na=len(arrays); rows,width=arrays[0].shape[-2:]
    arrays=[a.reshape(4,8,rows,width) for a in arrays]
    pr=rows//parts; items=na*4*parts; half=pr//2
    any_=pl.BlockSpec(memory_space=pl.ANY)
    D=pltpu.SemaphoreType.DMA
    V=lambda *s: pltpu.VMEM(s+(width,),BF)
    out,_=pl.pallas_call(partial(scatter_kernel,na,parts),
        out_shape=[jax.ShapeDtypeStruct((na,rows,width),BF),jax.ShapeDtypeStruct((items,4,pr,width),BF)],
        in_specs=[any_]*na,out_specs=[any_,any_],
        scratch_shapes=[V(items,4,pr),V(items,2,2,half),V(items,2,half),V(items,pr),V(items,pr),V(2,4,pr),
            D((items,)),D((items,)),D((items,)),D((2,)),D((items,3)),D((items,3)),D((items,2)),D((items,2)),
            D((items,)),D((items,)),D((items,)),D((items,)),D((items,))],
        compiler_params=pltpu.CompilerParams(collective_id=cid,has_side_effects=True,vmem_limit_bytes=63*1024*1024),
        name="scatter_blocks")(*arrays)
    return out


def reduce_kernel(
    wide_n, slab_n, splits, gw, gq, gs, tw, tq, tk, tv,
    own_w, own_q, all_q, far_w, far_q, pin_w, pin_q, pout_w, pout_q, din_w, din_q, dout_w, dout_q, tot_w, tot_q, mate_q,
    wload, qload, s0w, r0w, s0q, r0q, sa, ra, su, ru, sd, rd, keep, keep_q, keep_m, sc, rc,
):
    fs, ep, y, x, z, c = spot()
    mate = (fs, ep + 1 - 2 * c)
    rows_w, rows_q = own_w.shape[1], own_q.shape[1]
    parts = slab_n // 4
    items = wide_n + slab_n

    def rem(src, dst, s, r, dev):
        return pltpu.make_async_remote_copy(src, dst, s, r, device_id=dev, device_id_type=MESH)

    def source(s):
        return ((y + s // 2) % 2) * 2 + (x + s) % 2

    def give_w(i):
        return rem(gw.at[1 - c, i], far_w.at[i], s0w.at[i], r0w.at[i], mate)

    def load_w(i):
        return pltpu.make_async_copy(gw.at[c, i], own_w.at[i], wload.at[i])

    body = gq.shape[1] - (2 * parts - 1) * rows_q

    def pieces(s, core, dst):
        base = core * parts * rows_q
        out = []
        for p in range(parts):
            n = rows_q if p < parts - 1 else body
            at = pl.ds(pl.multiple_of(base + p * rows_q, 16), n)
            out.append((gq.at[source(s), at], dst.at[s, p, pl.ds(0, n)]))
        rest = dst.at[s, parts - 1, pl.ds(body, rows_q - body)]
        at = pl.ds((parts - 1) * rows_q + body, rows_q - body)
        return out + [(gq.at[source(s), at], rest)], (gs.at[source(s)], rest)

    def give_q(s, do):
        common, other = pieces(s, 1 - c, far_q)

        def move(n, pair):
            do(rem(*pair, s0q.at[s, n], r0q.at[s, n], mate))

        for n, pair in enumerate(common[:-1]):
            move(n, pair)

        @pl.when(c == 1)
        def _():
            move(parts, common[-1])

        @pl.when(c == 0)
        def _():
            move(parts, other)

    def load_q(s, do):
        common, other = pieces(s, c, all_q)

        def move(n, pair):
            do(pltpu.make_async_copy(*pair, qload.at[s, n]))

        for n, pair in enumerate(common[:-1]):
            move(n, pair)

        @pl.when(c == 0)
        def _():
            move(parts, common[-1])

        @pl.when(c == 1)
        def _():
            move(parts, other)

    def pass_q(s):
        dev = (source(s), ep)
        return rem(all_q.at[s], own_q.at[pl.ds(s * parts, parts)], sa.at[s], ra.at[s], dev)

    def on_item(i, f):
        @pl.when(i < wide_n)
        def _():
            f(own_w, pin_w, pout_w, din_w, dout_w, tot_w, i)

        @pl.when(i >= wide_n)
        def _():
            f(own_q, pin_q, pout_q, din_q, dout_q, tot_q, i - wide_n)

    def valid(i):
        return (i >= 0) & (i < items)

    def place(buf, sem, j, core):
        at = pl.ds(pl.multiple_of((core * parts + j % parts) * rows_q, 16), rows_q)
        lo, out = 0, []
        for n, (dst, size) in enumerate(zip((tq, tk, tv), splits)):
            to = pl.ds(pl.multiple_of(source(j // parts) * size, 128), size)
            out.append(
                pltpu.make_async_copy(buf.at[j, :, pl.ds(lo, size)], dst.at[at, to], sem.at[j, n])
            )
            lo += size
        return out

    def share_w(i):
        dst = tw.at[c, i]
        return (
            pltpu.make_async_copy(tot_w.at[i], dst, keep.at[i]),
            rem(tot_w.at[i], dst, sc.at[i], rc.at[i], mate),
        )

    def share_q(j):
        i = j + wide_n
        return rem(tot_q.at[j], mate_q.at[j], sc.at[i], rc.at[i], mate)

    greet(fs, ep, z, 1)

    @pl.loop(0, wide_n)
    def _(i):
        give_w(i).start()
        load_w(i).start()

    for s in (1, 2, 3, 0):
        give_q(s, lambda copy: copy.start())
        load_q(s, lambda copy: copy.start())

    @pl.loop(0, items + 4)
    def _(t):
        @pl.when(t < wide_n)
        def _():
            load_w(t).wait()
            give_w(t).wait_recv()
            own_w[t] = own_w[t] + far_w[t]

        for n, s in enumerate((1, 2, 3, 0)):

            @pl.when(t == n + 3)
            def _():
                load_q(s, lambda copy: copy.wait())
                give_q(s, lambda copy: copy.wait_recv())

                @pl.loop(0, parts)
                def _(j):
                    if s:
                        all_q[s, j] = all_q[s, j] + far_q[s, j]
                    else:
                        own_q[j] = all_q[0, j] + far_q[0, j]

                if s:
                    pass_q(s).start()

        for s in (1, 2, 3):

            @pl.when(t == wide_n + s * parts)
            def _():
                pass_q(s).wait_recv()

        iu = t - z

        @pl.when(valid(iu))
        def _():
            def go(own, pin, pout, din, dout, tot, i):
                @pl.when(z == 0)
                def _():
                    rem(own.at[i], pin.at[i], su.at[iu], ru.at[iu], (fs, ep + 2)).start()

                @pl.when(z > 0)
                def _():
                    rem(own.at[i], pin.at[i], su.at[iu], ru.at[iu], (fs, ep - 2)).wait_recv()

                @pl.when((z > 0) & (z < 3))
                def _():
                    pout[i] = pin[i] + own[i]
                    rem(pout.at[i], pin.at[i], su.at[iu], ru.at[iu], (fs, ep + 2)).start()

            on_item(iu, go)

        idn = t - 3 + z

        @pl.when(valid(idn))
        def _():
            def go(own, pin, pout, din, dout, tot, i):
                @pl.when(z == 3)
                def _():
                    rem(own.at[i], din.at[i], sd.at[idn], rd.at[idn], (fs, ep - 2)).start()

                @pl.when(z < 3)
                def _():
                    rem(own.at[i], din.at[i], sd.at[idn], rd.at[idn], (fs, ep + 2)).wait_recv()

                @pl.when((z > 0) & (z < 3))
                def _():
                    dout[i] = din[i] + own[i]
                    rem(dout.at[i], din.at[i], sd.at[idn], rd.at[idn], (fs, ep - 2)).start()

            on_item(idn, go)

        last = t - 3

        @pl.when(valid(last))
        def _():
            def go(own, pin, pout, din, dout, tot, i):
                @pl.when(z == 0)
                def _():
                    tot[i] = own[i] + din[i]

                @pl.when(z == 3)
                def _():
                    tot[i] = own[i] + pin[i]

                @pl.when((z == 1) | (z == 2))
                def _():
                    tot[i] = own[i] + pin[i] + din[i]

            on_item(last, go)

            @pl.when(last < wide_n)
            def _():
                for copy in share_w(last):
                    copy.start()

            @pl.when(last >= wide_n)
            def _():
                j = last - wide_n
                for copy in (share_q(j), *place(tot_q, keep_q, j, c)):
                    copy.start()

    @pl.loop(0, items)
    def _(i):
        @pl.when(i < wide_n)
        def _():
            for copy in share_w(i):
                copy.wait()

        @pl.when(i >= wide_n)
        def _():
            j = i - wide_n
            share_q(j).wait()
            for copy in place(mate_q, keep_m, j, 1 - c):
                copy.start()

        def go(own, pin, pout, din, dout, tot, j):
            @pl.when(z < 3)
            def _():
                rem(own.at[j], pin.at[j], su.at[i], ru.at[i], (fs, ep + 2)).wait_send()

            @pl.when(z > 0)
            def _():
                rem(own.at[j], din.at[j], sd.at[i], rd.at[i], (fs, ep - 2)).wait_send()

        on_item(i, go)

    @pl.loop(0, slab_n)
    def _(j):
        for copy in (*place(tot_q, keep_q, j, c), *place(mate_q, keep_m, j, 1 - c)):
            copy.wait()

    @pl.loop(0, wide_n)
    def _(i):
        give_w(i).wait_send()

    for s in range(4):
        give_q(s, lambda copy: copy.wait_send())
        if s:
            pass_q(s).wait_send()


def reduce_parts(gw, gq, gs, parts, splits, cid):
    wide_n = gw.shape[1]
    slab_rows = gq.shape[1] + gs.shape[1]
    rows_q, cols = slab_rows // (2 * parts), gq.shape[2]
    slab_n = 4 * parts
    free = pl.BlockSpec(memory_space=pl.ANY)
    D = pltpu.SemaphoreType.DMA
    W = pltpu.VMEM((wide_n,) + gw.shape[2:], BF)
    Q = pltpu.VMEM((slab_n, rows_q, cols), BF)
    Q4 = pltpu.VMEM((4, parts, rows_q, cols), BF)
    items = wide_n + slab_n
    return pl.pallas_call(
        partial(reduce_kernel, wide_n, slab_n, splits),
        out_shape=[jax.ShapeDtypeStruct(gw.shape, BF)]
        + [jax.ShapeDtypeStruct((slab_rows, 4 * size), BF) for size in splits],
        in_specs=[free] * 3,
        out_specs=[free] * 4,
        scratch_shapes=[W, Q, Q4, W, Q4] + [W, Q] * 5 + [Q]
        + [D((wide_n,)), D((4, parts + 1)), D((wide_n,)), D((wide_n,)), D((4, parts + 1)), D((4, parts + 1))]
        + [D((4,)), D((4,))]
        + [D((items,))] * 4 + [D((wide_n,)), D((slab_n, 3)), D((slab_n, 3)), D((items,)), D((items,))],
        compiler_params=pltpu.CompilerParams(
            collective_id=cid, has_side_effects=True, vmem_limit_bytes=63 * 1024 * 1024
        ),
        cost_estimate=pl.CostEstimate(flops=0, bytes_accessed=500_000_000, transcendentals=0),
        name="reduce_parts",
    )(gw, gq, gs)


def start_kernel(
    splits, own, few, wq, wk, wv, rows_out, few_out, w_out, own_cols,
    here, here_few, own_w, sx, rx, sf, rf, sw, rw, sm, rm,
):
    fs, ep, y, x, z, c = spot()
    mate = (fs, ep + 1 - 2 * c)
    shard = wq.shape[0]
    pair = (fs, ep + 2 - 4 * (z % 2))
    units = shard // 16
    edges = [16 * (units * n // 4) for n in range(5)]
    quarters = [(lo, hi - lo) for lo, hi in zip(edges, edges[1:])]
    half = own.shape[0] // 2
    bands = (pl.ds(0, half), pl.ds(half, half))

    def peer(s):
        return ((y + s // 2) % 2) * 2 + (x + s) % 2

    def rem(src, dst, s, r, dev):
        return pltpu.make_async_remote_copy(src, dst, s, r, device_id=dev, device_id_type=MESH)

    def columns(dev, at):
        lo, out = 0, []
        for src, size in zip((wq, wk, wv), splits):
            cols = pl.ds(pl.multiple_of(dev * size, 128), size)
            out.append((src.at[at, cols], pl.ds(lo, size)))
            lo += size
        return out

    def send(s, lo, n):
        at = pl.ds(lo, n)
        return [
            rem(src, w_out.at[fs, at, cols], sw.at[s, k], rw.at[s, k], (peer(s), ep))
            for k, (src, cols) in enumerate(columns(peer(s), at))
        ]

    def arrive(s, lo, n):
        at = pl.ds(lo, n)
        return [
            rem(w_out.at[peer(s), at, cols], w_out.at[peer(s), at, cols], sw.at[s, k], rw.at[s, k], mate)
            for k, (_, cols) in enumerate(columns(fs, at))
        ]

    def share(s, k, lo, n, dev):
        v = w_out.at[peer(s), pl.ds(lo, n)]
        return rem(v, v, sm.at[s, k], rm.at[s, k], dev)

    def give(s, band):
        v = rows_out.at[fs, bands[band]]
        return rem(v, v, sx.at[s, band], rx.at[s, band], (peer(s), ep))

    def pass_on(s, band):
        v = rows_out.at[peer(s), bands[band]]
        return rem(v, v, sx.at[3, band], rx.at[3, band], (peer(3 - s), ep))

    def give_few(s):
        return rem(few, few_out.at[fs], sf.at[s], rf.at[s], (peer(s), ep))

    keep = pltpu.make_async_copy(own, rows_out.at[fs], here)
    keep.start()
    keep_few = pltpu.make_async_copy(few, few_out.at[fs], here_few)
    keep_few.start()
    locals_ = []
    for k, (src, cols) in enumerate(columns(fs, pl.ds(0, shard))):
        locals_.append(pltpu.make_async_copy(src, own_cols.at[:, cols], own_w.at[k]))
    for copy in locals_:
        copy.start()
    greet(fs, ep, z, 1)
    keep.wait()
    for copy in locals_:
        copy.wait()
    own_slab = pltpu.make_async_copy(own_cols, w_out.at[fs], here)
    own_slab.start()
    for s in (1, 2, 3):
        give_few(s).start()
    for quarter in range(4):

        @pl.when((z % 2) * 2 + c == quarter)
        def _():
            mine, mates, pairs, last = (quarters[quarter ^ n] for n in (0, 1, 2, 3))
            for s in (3, 1, 2):
                for copy in send(s, *mine):
                    copy.start()
            for s, band in ((1, 0), (2, 1), (1, 1), (2, 0)):
                give(s, band).start()
            for s in (1, 2, 3):
                for copy in arrive(s, *mine):
                    copy.wait_recv()
                share(s, 0, *mine, pair).start()
                share(s, 1, *mine, mate).start()
            give(1, 0).wait_recv()
            pass_on(1, 0).start()
            give(2, 1).wait_recv()
            pass_on(2, 1).start()
            for s in (1, 2, 3):
                share(s, 0, *pairs, pair).wait_recv()
                share(s, 2, *pairs, mate).start()
            for s in (1, 2, 3):
                share(s, 1, *mates, mate).wait_recv()
                share(s, 2, *last, mate).wait_recv()
            for s in (1, 2, 3):
                for copy in send(s, *mine):
                    copy.wait_send()
                share(s, 0, *mine, pair).wait_send()
                share(s, 1, *mine, mate).wait_send()
                share(s, 2, *pairs, mate).wait_send()

    for s in (1, 2):
        give(s, 2 - s).wait_recv()
        for band in range(2):
            give(s, band).wait_send()
    for s, band in ((1, 0), (2, 1)):
        pass_on(s, band).wait()
    for s in (1, 2, 3):
        give_few(s).wait_send()
        rem(few, few_out.at[peer(s)], sf.at[s], rf.at[s], mate).wait_recv()
    own_slab.wait()
    keep_few.wait()


def start_exchange(own, few, wq, wk, wv, cid):
    shard = wq.shape[0]
    splits = tuple(w.shape[1] // 4 for w in (wq, wk, wv))
    free = pl.BlockSpec(memory_space=pl.ANY)
    D = pltpu.SemaphoreType.DMA
    return pl.pallas_call(
        partial(start_kernel, splits),
        out_shape=[
            jax.ShapeDtypeStruct((4,) + own.shape, BF),
            jax.ShapeDtypeStruct((4,) + few.shape, BF),
            jax.ShapeDtypeStruct((4, shard, sum(splits)), BF),
        ],
        in_specs=[pl.BlockSpec(memory_space=pltpu.VMEM)] * 2 + [free] * 3,
        out_specs=[free] * 3,
        scratch_shapes=[pltpu.VMEM((shard, sum(splits)), BF), D, D, D((3,)), D((4, 2)), D((4, 2)), D((4,)), D((4,)), D((4, 3)), D((4, 3)), D((4, 3)), D((4, 3))],
        compiler_params=pltpu.CompilerParams(collective_id=cid, has_side_effects=True),
        name="start_exchange",
    )(own, few, wq, wk, wv)


def nn(left, right):
    return lax.dot_general(left, right, (((1,), (0,)), ((), ())), preferred_element_type=F32)


def nt(left, right):
    return lax.dot_general(left, right, (((1,), (1,)), ((), ())), preferred_element_type=F32)


def tn(left, right):
    return lax.dot_general(left, right, (((0,), (0,)), ((), ())), preferred_element_type=F32)


def strips(total, size):
    return [(at, min(size, total - at)) for at in range(0, total, size)]


def remote(src, dst, send, recv, device):
    return pltpu.make_async_remote_copy(
        src, dst, send, recv, device_id=device, device_id_type=MESH
    )


def line_order(z, i):
    code = jnp.where(z == 0, 228, jnp.where(z == 1, 225, jnp.where(z == 2, 30, 27)))
    power = jnp.where(i == 0, 1, jnp.where(i == 1, 4, jnp.where(i == 2, 16, 64)))
    return (code // power) % 4


class Gather:
    def __init__(self, full, sems):
        self.full = full
        self.sz, self.rz, self.s1, self.r1, self.s2, self.r2, self.sc, self.rc = sems
        self.fs, self.ep, self.y, self.x, self.z, self.c = spot()
        half = full.shape[3] // 2
        self.upper, self.lower = pl.ds(0, half), pl.ds(half, half)
        self.xn = (self.fs + 1 - 2 * self.x, self.ep)
        self.yn = (self.fs + 2 - 4 * self.y, self.ep)
        self.mate = (self.fs, self.ep + 1 - 2 * self.c)

    def item(self, t):
        return t // 4, line_order(self.z, t % 4)

    def along(self, a, zz, up):
        view = self.full.at[a, self.fs, zz * 2 + self.c]
        other = (self.fs, self.ep + (2 if up else -2))
        return remote(view, view, self.sz.at[a, zz, up], self.rz.at[a, zz], other)

    def first(self, a, zz):
        e = zz * 2 + self.c
        v = self.full.at[a, self.fs, e, self.upper]
        w = self.full.at[a, self.fs, e, self.lower]
        s, r = self.s1.at[a, zz], self.r1.at[a, zz]
        return (
            remote(v, v, s.at[0], r.at[0], self.xn),
            remote(w, w, s.at[1], r.at[1], self.yn),
            remote(w, w, s.at[2], r.at[2], self.xn),
            remote(v, v, s.at[3], r.at[3], self.yn),
        )

    def second(self, a, zz):
        e = zz * 2 + self.c
        v = self.full.at[a, self.y * 2 + 1 - self.x, e, self.upper]
        w = self.full.at[a, (1 - self.y) * 2 + self.x, e, self.lower]
        s, r = self.s2.at[a, zz], self.r2.at[a, zz]
        return remote(v, v, s.at[0], r.at[0], self.yn), remote(w, w, s.at[1], r.at[1], self.xn)

    def across(self, a, zz, e):
        v = self.full.at[a, :, zz * 2 + e]
        return remote(v, v, self.sc.at[a, zz], self.rc.at[a, zz], self.mate)

    def step0(self, t):
        @pl.when(t < 8)
        def _():
            a, zz = self.item(t)

            @pl.when(zz != self.z)
            def _():
                self.along(a, zz, 0).wait_recv()

            @pl.when((zz <= self.z) & (self.z < 3))
            def _():
                self.along(a, zz, 1).start()

            @pl.when((zz >= self.z) & (self.z > 0))
            def _():
                self.along(a, zz, 0).start()

    def step0_if(self, t, inner):
        inside = (self.z == 1) | (self.z == 2)

        @pl.when(inside == inner)
        def _():
            self.step0(t)

    def step1(self, t):
        @pl.when(t < 8)
        def _():
            for copy in self.first(*self.item(t)):
                copy.start()

    def step2(self, t):
        @pl.when(t < 8)
        def _():
            a, zz = self.item(t)
            from_x, from_y, _, _ = self.first(a, zz)
            to_y, to_x = self.second(a, zz)
            from_x.wait_recv()
            to_y.start()
            from_y.wait_recv()
            to_x.start()

    def step3(self, t):
        @pl.when(t < 8)
        def _():
            a, zz = self.item(t)
            for copy in (*self.first(a, zz)[2:], *self.second(a, zz)):
                copy.wait_recv()
            self.across(a, zz, self.c).start()

    def step4(self, t):
        a, zz = self.item(t)
        self.across(a, zz, 1 - self.c).wait_recv()

    def finish(self):
        @pl.loop(0, 8)
        def _(t):
            a, zz = self.item(t)
            self.across(a, zz, self.c).wait_send()
            for copy in (*self.first(a, zz), *self.second(a, zz)):
                copy.wait_send()

            @pl.when((zz <= self.z) & (self.z < 3))
            def _():
                self.along(a, zz, 1).wait_send()

            @pl.when((zz >= self.z) & (self.z > 0))
            def _():
                self.along(a, zz, 0).wait_send()


def experts_kernel(
    cap, width,
    n_own, g_own, wg_hbm, wu_hbm, wd_hbm, bg_ref, bu_ref, bd_ref,
    full, out_hbm, row_hbm, xs_hbm, eg_hbm, mid_hbm, ug_hbm, gg_hbm, cu_hbm, cg_hbm,
    sum_g, sum_u, sum_d,
    wg_ref, wu_ref, wd_ref, bin_, meta, pmat, pmat_t, gates, xs, res, mid, cub, cgb, dots, stage,
    w_sem, own_sem, in_sem, st_sem, save_sem,
    *sems,
):
    gather = Gather(full, sems)
    fs, ep, z = gather.fs, gather.ep, gather.z
    card_rows, wpad = bin_.shape[2:]
    tail = wpad - 128
    off = width - tail
    first = jnp.where(fs == 0, 1.0, 0.0).astype(F32)
    nb = 8
    rows = nb * cap
    weights = [
        pltpu.make_async_copy(src, dst, w_sem.at[n])
        for n, (src, dst) in enumerate(((wg_hbm, wg_ref), (wu_hbm, wu_ref), (wd_hbm, wd_ref)))
    ]
    keep = [
        pltpu.make_async_copy(src, full.at[a, fs, ep], own_sem.at[a])
        for a, src in enumerate((n_own, g_own))
    ]
    for copy in keep + weights:
        copy.start()
    greet(fs, ep, z)
    for copy in keep:
        copy.wait()
    gather.step0(0)
    gather.step1(0)
    gather.step0(1)
    gather.step2(0)
    gather.step1(1)
    gather.step3(0)
    gather.step0(2)

    def load(t):
        a, zz = gather.item(t)
        return pltpu.make_async_copy(full.at[a, :, pl.ds(zz * 2, 2)], bin_, in_sem)

    def save(src, dst, k, i, n):
        return pltpu.make_async_copy(src.at[k], dst.at[k, i], save_sem.at[n, k])

    def save_rows(dst, k, i):
        return pltpu.make_async_copy(xs.at[:, k], dst.at[k, i], save_sem.at[0, k])

    def fetch(src, dst, k, i, n):
        return pltpu.make_async_copy(src.at[k, i], dst.at[k], save_sem.at[n, k])

    def rows_of(ref, k, lo=0, n=width):
        return ref[:, k, :, lo : lo + n].reshape(rows, n)

    def next_load(t):
        @pl.when(t < 8)
        def _():
            gather.step4(t)
            load(t).start()

    def spread(i, prepare):
        @pl.loop(0, nb)
        def _(b):
            j, c = b // 2, b % 2
            if prepare:
                meta[...] = jnp.transpose(bin_[j, c, :, tail:].astype(F32))
                at = pl.ds(pl.multiple_of(b * cap, 16), cap)
                hits = []
                for k in range(2):
                    e = ep * 2 + k
                    place = meta[pl.ds(off + e, 1), :]
                    gate = meta[pl.ds(off + 16 + e, 1), :] + meta[pl.ds(off + 32 + e, 1), :]
                    hit = lax.broadcasted_iota(jnp.int32, (cap, card_rows), 0).astype(F32) == place
                    gates[i, k, at, :] = jnp.sum(jnp.where(hit, gate, 0.0), axis=1, keepdims=True)
                    hits.append(jnp.where(hit, 1.0, 0.0))
                hits.append(jnp.zeros((card_rows - 2 * cap, card_rows), F32))
                hits = jnp.concatenate(hits, axis=0)
                pmat[i, b] = hits[: 2 * cap].astype(BF)
                pmat_t[i, b] = jnp.transpose(hits).astype(BF)
            pick = pmat[i, b]
            for lo, n in strips(width, 768):
                got = nn(pick, bin_[j, c, :, lo : lo + n]).astype(BF)
                xs[b, :, :, lo : lo + n] = got.reshape(2, cap, n)

    def group_store(dst, zz):
        return pltpu.make_async_copy(stage, dst.at[:, pl.ds(zz * 2, 2)], st_sem)

    def combine(i, with_dots):
        column = lax.broadcasted_iota(jnp.int32, (cap, wpad - width), 1)

        @pl.loop(0, nb)
        def _(b):
            j, c = b // 2, b % 2
            pick = pmat_t[i, b, :, : 2 * cap]
            for lo, n in strips(width, 768):
                both = res[b, :, :, lo : lo + n].reshape(2 * cap, n)
                stage[j, c, :, lo : lo + n] = nn(pick, both).astype(BF)
            if with_dots:
                at = pl.ds(pl.multiple_of(b * cap, 16), cap)
                own_dots = jnp.concatenate(
                    [
                        jnp.where(column == ep * 2 + k, dots[k, at, :], 0.0).astype(BF)
                        for k in range(2)
                    ],
                    axis=0,
                )
                stage[j, c, :, width:] = nn(pick, own_dots).astype(BF)
            else:
                stage[j, c, :, width:] = jnp.zeros((card_rows, wpad - width), BF)

    next_load(0)
    for copy in weights:
        copy.wait()

    @pl.loop(0, 4)
    def _(i):
        zz = line_order(z, i)
        gather.step2(i + 1)
        gather.step1(i + 2)
        gather.step0_if(i + 3, True)
        load(i).wait()
        spread(i, True)
        for k in range(2):
            save_rows(xs_hbm, k, i).start()

        @pl.loop(0, 2)
        def _(k):
            @pl.when(k == 1)
            def _():
                gather.step3(i + 1)

            x = rows_of(xs, k)
            gate_soft = CLAMP_LIMIT * jnp.tanh((nt(x, wg_ref[k]) + bg_ref[k]) * (1.0 / CLAMP_LIMIT))
            up_soft = CLAMP_LIMIT * jnp.tanh((nt(x, wu_ref[k]) + bu_ref[k]) * (1.0 / CLAMP_LIMIT))
            sig = jax.nn.sigmoid(SWIGLU_ALPHA * gate_soft)
            glu = gate_soft * sig
            mid[k] = ((up_soft + 1.0) * glu).astype(BF)
            cub[k] = (glu * (1.0 - (up_soft * (1.0 / CLAMP_LIMIT)) ** 2)).astype(BF)
            cgb[k] = (
                (up_soft + 1.0)
                * (sig + SWIGLU_ALPHA * glu * (1.0 - sig))
                * (1.0 - (gate_soft * (1.0 / CLAMP_LIMIT)) ** 2)
            ).astype(BF)
            save(mid, mid_hbm, k, i, 1).start()
            save(cub, cu_hbm, k, i, 2).start()
            save(cgb, cg_hbm, k, i, 3).start()
            for lo, n in strips(width, 768):
                part = nn(mid[k], wd_ref[k, :, lo : lo + n]) + first * bd_ref[k, :, lo : lo + n]
                res[:, k, :, lo : lo + n] = (part * gates[i, k]).astype(BF).reshape(nb, cap, n)

        gather.step0_if(i + 3, False)
        next_load(i + 1)

        @pl.when(i > 0)
        def _():
            group_store(out_hbm, line_order(z, i - 1)).wait()

        combine(i, False)
        group_store(out_hbm, zz).start()
        for k in range(2):
            save_rows(xs_hbm, k, i).wait()
            save(mid, mid_hbm, k, i, 1).wait()
            save(cub, cu_hbm, k, i, 2).wait()
            save(cgb, cg_hbm, k, i, 3).wait()

    group_store(out_hbm, line_order(z, 3)).wait()
    sum_g[...] = jnp.zeros_like(sum_g)
    sum_u[...] = jnp.zeros_like(sum_u)
    sum_d[...] = jnp.zeros_like(sum_d)

    @pl.loop(0, 4)
    def _(i):
        zz = line_order(z, i)
        for k in range(2):
            fetch(mid_hbm, mid, k, i, 1).start()
            fetch(cu_hbm, cub, k, i, 2).start()
            fetch(cg_hbm, cgb, k, i, 3).start()
        gather.step2(i + 5)
        gather.step1(i + 6)
        gather.step0_if(i + 7, True)
        load(i + 4).wait()
        spread(i, False)

        @pl.loop(0, 2)
        def _(k):
            @pl.when(k == 1)
            def _():
                gather.step3(i + 5)

            fetch(mid_hbm, mid, k, i, 1).wait()
            fetch(cu_hbm, cub, k, i, 2).wait()
            fetch(cg_hbm, cgb, k, i, 3).wait()
            g_rows = rows_of(xs, k)
            plain = nt(g_rows, wd_ref[k])
            gate = gates[i, k]
            grad = plain * gate
            g_rows = g_rows.astype(F32)
            dots[k] = jnp.sum(plain * mid[k].astype(F32), axis=1, keepdims=True) + first * jnp.sum(
                g_rows * bd_ref[k], axis=1, keepdims=True
            )
            up_grad = (grad * cub[k].astype(F32)).astype(BF)
            cub[k] = up_grad
            sum_u[k] += jnp.sum(up_grad.astype(F32), axis=0, keepdims=True)
            gate_grad = (grad * cgb[k].astype(F32)).astype(BF)
            cgb[k] = gate_grad
            sum_g[k] += jnp.sum(gate_grad.astype(F32), axis=0, keepdims=True)
            scaled = (g_rows * gate).astype(BF)
            xs[:, k] = scaled.reshape(nb, cap, width)
            sum_d[k] += jnp.sum(scaled.astype(F32), axis=0, keepdims=True)
            save_rows(eg_hbm, k, i).start()
            save(cub, ug_hbm, k, i, 4).start()
            save(cgb, gg_hbm, k, i, 5).start()
            for lo, n in strips(width, 768):
                part = nn(cgb[k], wg_ref[k, :, lo : lo + n]) + nn(cub[k], wu_ref[k, :, lo : lo + n])
                res[:, k, :, lo : lo + n] = part.astype(BF).reshape(nb, cap, n)

        gather.step0_if(i + 7, False)
        next_load(i + 5)

        @pl.when(i > 0)
        def _():
            group_store(row_hbm, line_order(z, i - 1)).wait()

        combine(i, True)
        group_store(row_hbm, zz).start()
        for k in range(2):
            save_rows(eg_hbm, k, i).wait()
            save(cub, ug_hbm, k, i, 4).wait()
            save(cgb, gg_hbm, k, i, 5).wait()

    group_store(row_hbm, line_order(z, 3)).wait()
    gather.finish()


def experts(n_own, g_own, wg_t, b_gate, wu_t, b_up, w_down, b_down, cap, cid):
    rows, wpad = n_own.shape
    ff, width = w_down.shape[1:]
    n, m = 32 * cap, 8 * cap
    free = pl.BlockSpec(memory_space=pl.ANY)
    near = pl.BlockSpec(memory_space=pltpu.VMEM)
    shape = jax.ShapeDtypeStruct
    V = pltpu.VMEM
    D = pltpu.SemaphoreType.DMA
    biases = [b.astype(F32)[:, None] for b in (b_gate, b_up, b_down)]
    out = pl.pallas_call(
        partial(experts_kernel, cap, width),
        out_shape=[shape((2, 4, 8, rows, wpad), BF)]
        + [shape((4, 8, rows, wpad), BF)] * 2
        + [shape((2, 4, 8, cap, width), BF)] * 2
        + [shape((2, 4, m, ff), BF)] * 5
        + [shape((2, 1, ff), F32)] * 2
        + [shape((2, 1, width), F32)],
        in_specs=[near] * 2 + [free] * 3 + [near] * 3,
        out_specs=[free] * 10 + [near] * 3,
        scratch_shapes=[
            V((2, ff, width), BF), V((2, ff, width), BF), V((2, ff, width), BF),
            V((4, 2, rows, wpad), BF), V((128, rows), F32),
            V((4, 8, 2 * cap, rows), BF), V((4, 8, rows, rows), BF), V((4, 2, m, 1), F32),
            V((8, 2, cap, width), BF), V((8, 2, cap, width), BF),
            V((2, m, ff), BF), V((2, m, ff), BF), V((2, m, ff), BF),
            V((2, m, 1), F32), V((4, 2, rows, wpad), BF),
            D((3,)), D((2,)), D, D, D((6, 2)),
            D((2, 4, 2)), D((2, 4)), D((2, 4, 4)), D((2, 4, 4)), D((2, 4, 2)), D((2, 4, 2)), D((2, 4)), D((2, 4)),
        ],
        compiler_params=pltpu.CompilerParams(
            collective_id=cid, has_side_effects=True, vmem_limit_bytes=63 * 1024 * 1024
        ),
        cost_estimate=pl.CostEstimate(
            flops=24 * n * width * ff, bytes_accessed=300_000_000, transcendentals=6 * n * ff
        ),
        name="experts",
    )(n_own, g_own, wg_t, wu_t, w_down, *biases)
    saved = [v.reshape(2, n, -1) for v in out[3:8]]
    return (*out[1:3], *saved, *(total[:, 0] for total in out[10:]))


def group_sum_kernel(parts, p_ref, out_ref, q, v1, v2, s1, r1, s2, r2):
    fs, ep, y, x, z, c = spot()
    rows = p_ref.shape[1]
    step = rows // (2 * parts)
    xn, yn = (fs + 1 - 2 * x, ep), (fs + 2 - 4 * y, ep)

    def rem(src, dst, s, r, dev):
        return pltpu.make_async_remote_copy(src, dst, s, r, device_id=dev, device_id_type=MESH)

    def band(n, half):
        return pl.ds((2 * n + half) * step, step)

    def one(n):
        a, b = band(n, 0), band(n, 1)
        out = [
            (rem(p_ref.at[2 * j + 1 - x, a], v1.at[n, 0, j], s1.at[n, 0, j], r1.at[n, 0, j], xn))
            for j in range(2)
        ]
        return out + [
            rem(p_ref.at[2 * (1 - y) + j, b], v1.at[n, 1, j], s1.at[n, 1, j], r1.at[n, 1, j], yn)
            for j in range(2)
        ]

    def two(n):
        return (
            rem(q.at[n, 0], v2.at[n, 0], s2.at[n, 0], r2.at[n, 0], yn),
            rem(q.at[n, 1], v2.at[n, 1], s2.at[n, 1], r2.at[n, 1], xn),
        )

    greet(fs, ep, z)
    for n in range(parts):
        for copy in one(n):
            copy.start()
    for n in range(parts):
        a, b = band(n, 0), band(n, 1)
        copies = one(n)
        for copy in copies[:2]:
            copy.wait_recv()
        q[n, 0] = p_ref[2 * (1 - y) + x, a] + v1[n, 0, 1 - y]
        two(n)[0].start()
        for copy in copies[2:]:
            copy.wait_recv()
        q[n, 1] = p_ref[2 * y + 1 - x, b] + v1[n, 1, 1 - x]
        two(n)[1].start()
        out_ref[a, :] = p_ref[fs, a].astype(F32) + v1[n, 0, y].astype(F32)
        out_ref[b, :] = p_ref[fs, b].astype(F32) + v1[n, 1, x].astype(F32)
    for n in range(parts):
        for half in range(2):
            at = band(n, half)
            two(n)[half].wait_recv()
            out_ref[at, :] += v2[n, half].astype(F32)
    for n in range(parts):
        for copy in (*one(n), *two(n)):
            copy.wait_send()


def group_sum(part, cid, parts=2):
    _, rows, width = part.shape
    near = pl.BlockSpec(memory_space=pltpu.VMEM)
    D = pltpu.SemaphoreType.DMA
    step = rows // (2 * parts)
    V = pltpu.VMEM
    return pl.pallas_call(
        partial(group_sum_kernel, parts),
        out_shape=jax.ShapeDtypeStruct((rows, width), F32),
        in_specs=[near],
        out_specs=near,
        scratch_shapes=[
            V((parts, 2, step, width), BF), V((parts, 2, 2, step, width), BF), V((parts, 2, step, width), BF),
            D((parts, 2, 2)), D((parts, 2, 2)), D((parts, 2)), D((parts, 2)),
        ],
        compiler_params=pltpu.CompilerParams(
            collective_id=cid, has_side_effects=True, vmem_limit_bytes=32 * 1024 * 1024
        ),
        name="group_sum",
    )(part)


def weight_grads_kernel(xs, eg, mid, ug, gg, down, gate, up, rows, left, out, r_sem, l_sem, o_sem):
    width = xs.shape[2]
    jobs = [(k, w) for k in range(2) for w in range(3)]
    lefts, outs = (mid, gg, ug), (down, gate, up)

    def load_rows(n):
        return pltpu.make_async_copy((eg, xs)[n % 2].at[n // 2], rows.at[n % 2], r_sem.at[n % 2])

    def load_left(j):
        k, w = jobs[j]
        return pltpu.make_async_copy(lefts[w].at[k], left.at[j % 2], l_sem.at[j % 2])

    def store(j):
        k, w = jobs[j]
        return pltpu.make_async_copy(out.at[j % 2], outs[w].at[k], o_sem.at[j % 2])

    load_rows(0).start()
    load_left(0).start()
    load_rows(1).start()
    for j, (k, w) in enumerate(jobs):
        if j + 1 < len(jobs):
            load_left(j + 1).start()
        load_left(j).wait()
        if w < 2:
            load_rows(2 * k + w).wait()
        if j >= 2:
            store(j - 2).wait()
        right = rows.at[min(w, 1)]
        for lo, n in strips(width, 768):
            out[j % 2, :, lo : lo + n] = tn(left[j % 2], right[:, lo : lo + n])
        store(j).start()
        if k == 0 and w in (0, 2):
            load_rows(2 + (w > 0)).start()
    for j in (len(jobs) - 2, len(jobs) - 1):
        store(j).wait()


def weight_grads(xs, eg, mid, ug, gg):
    _, n, width = xs.shape
    ff = mid.shape[2]
    free = pl.BlockSpec(memory_space=pl.ANY)
    D = pltpu.SemaphoreType.DMA
    return pl.pallas_call(
        weight_grads_kernel,
        out_shape=[jax.ShapeDtypeStruct((2, ff, width), F32)] * 3,
        in_specs=[free] * 5,
        out_specs=[free] * 3,
        scratch_shapes=[
            pltpu.VMEM((2, n, width), BF), pltpu.VMEM((2, n, ff), BF), pltpu.VMEM((2, ff, width), F32),
            D((2,)), D((2,)), D((2,)),
        ],
        compiler_params=pltpu.CompilerParams(vmem_limit_bytes=60 * 1024 * 1024),
        cost_estimate=pl.CostEstimate(
            flops=12 * n * ff * width, bytes_accessed=100_000_000, transcendentals=0
        ),
        name="weight_grads",
    )(xs, eg, mid, ug, gg)


def this_slice(
    tokens,
    seq_lengths,
    routes,
    attn_gain,
    w_query,
    b_query,
    w_key,
    b_key,
    w_value,
    b_value,
    sinks,
    w_out,
    b_out,
    ffn_gain,
    w_router,
    b_router,
    w_gate,
    b_gate,
    w_up,
    b_up,
    w_down,
    b_down,
    cotangent,
):
    rows, width = tokens.shape
    fs_size = lax.axis_size("fs")
    ep_size = lax.axis_size("ep")
    my_fs = lax.axis_index("fs")
    my_ep = lax.axis_index("ep")
    blocks = fs_size * ep_size
    expert_count = EXP_DEV * ep_size
    capacity = 3 * rows * TOP // (2 * expert_count)
    shard = w_query.shape[0]
    kv_heads = KEY_VALUE_HEADS // fs_size
    group = QUERY_HEADS // KEY_VALUE_HEADS
    q_cols = kv_heads * group * HEAD_SIZE
    kv_cols = kv_heads * HEAD_SIZE

    spare = (-width) % 128
    small = jnp.concatenate(
        [attn_gain, ffn_gain, b_out, w_router.reshape(-1), b_router, seq_lengths[0].astype(BF)]
    )
    extra = -(-small.shape[0] // (16 * width)) * 16
    small = jnp.pad(small, (0, extra * width - small.shape[0])).reshape(extra, width)
    x_group, small, w_qkv = start_exchange(tokens, small, w_query, w_key, w_value, 4)
    x_group = x_group.reshape(fs_size * rows, width).astype(F32)
    small = small.reshape(fs_size, -1)
    gain_one = small[:, :shard].reshape(-1).astype(F32)
    gain_two = small[:, shard : 2 * shard].reshape(-1).astype(F32)
    bo = small[:, 2 * shard : 3 * shard].reshape(-1).astype(F32)
    at = (3 + expert_count) * shard
    wr = small[:, 3 * shard : at].reshape(width, expert_count)
    br = small[:, at : at + b_router.shape[0]].reshape(-1).astype(F32)
    at += b_router.shape[0]
    lengths = small[:, at : at + seq_lengths.shape[1]].astype(jnp.int32)

    w_qkv = w_qkv.reshape(width, q_cols + 2 * kv_cols)
    b_qkv = jnp.concatenate([b_query, b_key, b_value]).astype(jnp.float32)
    sink_score = sinks.astype(jnp.float32).reshape(1, kv_heads, group, 1)

    x_float = tokens.astype(jnp.float32)
    scale_one = norm_scale(x_float)
    scale_group = norm_scale(x_group)
    norm_attn = (x_group * scale_group * gain_one).astype(jnp.bfloat16)
    segment_ids, position = jax.vmap(lambda own: layout(own, rows))(lengths)
    cosine_table, sine_table = tables(position.reshape(-1), HEAD_SIZE // 2)
    qkv = jnp.dot(norm_attn, w_qkv, preferred_element_type=jnp.float32) + b_qkv
    many = fs_size * rows
    heads = kv_heads * group
    query = apply_rotation(
        qkv[:, :q_cols].reshape(many, heads, HEAD_SIZE), cosine_table, sine_table
    ).astype(jnp.bfloat16)
    query = query.reshape(fs_size, rows, kv_heads, group, HEAD_SIZE)
    key = apply_rotation(
        qkv[:, q_cols : q_cols + kv_cols].reshape(many, kv_heads, HEAD_SIZE),
        cosine_table,
        sine_table,
    ).astype(jnp.bfloat16)
    key = key.reshape(fs_size, rows, kv_heads, HEAD_SIZE)
    value = qkv[:, q_cols + kv_cols :].astype(jnp.bfloat16)
    value = value.reshape(fs_size, rows, kv_heads, HEAD_SIZE)
    places = jnp.arange(rows, dtype=jnp.int32)
    allowed = (segment_ids[:, :, None] == segment_ids[:, None, :]) & (
        places[:, None] >= places[None, :]
    )
    scores = mm("bqhgd,bkhd->bhgqk", query, key) * HEAD_SIZE ** (-0.5)
    masked = jnp.where(allowed[:, None, None], scores, MASKED_SCORE)
    top_score = jnp.maximum(jnp.max(masked, axis=-1), sink_score)
    exponent = jnp.exp(masked - top_score[..., None])
    sink_exp = jnp.exp(sink_score - top_score)
    denominator = jnp.sum(exponent, axis=-1) + sink_exp
    probs = exponent / denominator[..., None]
    sink_prob = sink_exp / denominator
    probs_b = probs.astype(jnp.bfloat16)
    mixed = mm("bhgqk,bkhd->bqhgd", probs_b, value).astype(jnp.bfloat16)
    mixed = mixed.reshape(many, q_cols)
    out_part = jnp.dot(mixed, w_out, preferred_element_type=jnp.float32)
    out_part = out_part.astype(BF).reshape(fs_size, rows, width)
    resid = x_float + group_sum(out_part, 5) + bo
    scale_two = norm_scale(resid)
    norm_ffn = (resid * scale_two * gain_two).astype(jnp.bfloat16)

    logits = jnp.dot(norm_ffn, wr, preferred_element_type=F32) + br
    one_hot = (routes[:, :, None] == jnp.arange(expert_count, dtype=jnp.int32)).astype(F32)
    member = jnp.sum(one_hot, axis=1)
    peak = jnp.max(jnp.where(member > 0, logits, MASKED_SCORE), axis=-1, keepdims=True)
    gate_exp = jnp.where(member > 0, jnp.exp(logits - peak), 0.0)
    gates_here = gate_exp / jnp.sum(gate_exp, axis=-1, keepdims=True)
    place = jnp.where(member > 0, jnp.cumsum(member, axis=0) - member, -1.0)
    gate_high = lax.reduce_precision(gates_here, 8, 7)
    block = jnp.concatenate(
        [norm_ffn]
        + [v.astype(BF) for v in (place, gate_high, gates_here - gate_high)]
        + [jnp.zeros((rows, spare - 3 * expert_count), BF)],
        axis=1,
    )
    wg_t = jnp.swapaxes(w_gate, 1, 2)
    wu_t = jnp.swapaxes(w_up, 1, 2)
    (
        out_part,
        row_part,
        x_slots,
        expert_grad,
        middle,
        up_grad,
        gate_grad_pre,
        grad_b_gate,
        grad_b_up,
        grad_b_down,
    ) = experts(
        block,
        jnp.pad(cotangent, ((0, 0), (0, spare))),
        wg_t,
        b_gate,
        wu_t,
        b_up,
        w_down,
        b_down,
        capacity,
        1,
    )
    sums = scatter_blocks([out_part, row_part], 2)
    block_out = resid + sums[0, :, :width].astype(F32)
    grad_w_down, gate_t, up_t = weight_grads(
        x_slots, expert_grad, middle, up_grad, gate_grad_pre
    )
    grad_w_gate = jnp.swapaxes(gate_t, 1, 2)
    grad_w_up = jnp.swapaxes(up_t, 1, 2)
    row_sum = sums[1].astype(F32)
    gate_grad = row_sum[:, width : width + expert_count]
    logit_grad = gates_here * (
        gate_grad - jnp.sum(gates_here * gate_grad, axis=-1, keepdims=True)
    )
    logit_grad = logit_grad.astype(jnp.bfloat16)
    grad_br = jnp.sum(logit_grad, axis=0, dtype=jnp.float32)
    grad_wr = left_dot(norm_ffn, logit_grad)
    norm_ffn_grad = row_sum[:, :width] + jnp.dot(
        logit_grad, wr.T, preferred_element_type=jnp.float32
    )
    resid_norm_grad, grad_gain_two = norm_back(resid, scale_two, gain_two, norm_ffn_grad)
    resid_grad = cotangent.astype(jnp.float32) + resid_norm_grad

    branch_grad = gather_fs(resid_grad.astype(jnp.bfloat16))
    grad_bo = jnp.sum(branch_grad, axis=0, dtype=jnp.float32)
    mixed_grad = mm("td,fd->tf", branch_grad, w_out).astype(jnp.bfloat16)
    mixed_grad = mixed_grad.reshape(fs_size, rows, kv_heads, group, HEAD_SIZE)
    grad_probs = mm("bqhgd,bkhd->bhgqk", mixed_grad, value)
    value_grad = mm("bhgqk,bqhgd->bkhd", probs_b, mixed_grad)
    row_delta = jnp.sum(probs * grad_probs, axis=-1)
    score_grad = (probs * (grad_probs - row_delta[..., None])).astype(jnp.bfloat16)
    query_grad = mm("bhgqk,bkhd->bqhgd", score_grad, key) * HEAD_SIZE ** (-0.5)
    key_grad = mm("bhgqk,bqhgd->bkhd", score_grad, query) * HEAD_SIZE ** (-0.5)
    grad_sink = -jnp.sum(sink_prob * row_delta, axis=(0, 3)).reshape(-1)
    query_pre_grad = undo_rotation(
        query_grad.reshape(many, heads, HEAD_SIZE), cosine_table, sine_table
    ).reshape(many, q_cols)
    key_pre_grad = undo_rotation(
        key_grad.reshape(many, kv_heads, HEAD_SIZE), cosine_table, sine_table
    ).reshape(many, kv_cols)
    qkv_grad = jnp.concatenate(
        [query_pre_grad, key_pre_grad, value_grad.reshape(many, kv_cols)], axis=1
    ).astype(jnp.bfloat16)
    grad_b_qkv = jnp.sum(qkv_grad, axis=0, dtype=jnp.float32)
    part = mm("tf,df->td", qkv_grad, w_qkv)
    grad_gain_one = jnp.sum(part * (x_group * scale_group), axis=0)
    norm_attn_grad = scatter_fs(part.astype(BF)).astype(F32)
    input_norm_grad, _ = norm_back(x_float, scale_one, gain_one, norm_attn_grad)
    grad_tokens = resid_grad + input_norm_grad
    by_shard = jnp.concatenate(
        [
            grad_wr.reshape(fs_size, -1),
            grad_gain_one.reshape(fs_size, -1),
            grad_gain_two.reshape(fs_size, -1),
            grad_br.reshape(fs_size, -1),
        ],
        axis=1,
    ).astype(BF)
    own = jnp.concatenate(
        [grad_b_qkv, grad_sink, lax.dynamic_slice_in_dim(grad_bo, my_fs * shard, shard)]
    ).astype(BF)
    cols = q_cols + 2 * kv_cols
    slab_rows = 768
    wide_part = 144
    own = jnp.where(jnp.arange(fs_size)[:, None] == my_fs, own, jnp.zeros((), BF))
    by_shard = jnp.concatenate([by_shard, own], axis=1)
    small_n = by_shard.shape[1]
    small_rows = -(-small_n // q_cols)
    by_shard = jnp.pad(by_shard, ((0, 0), (0, small_rows * q_cols - small_n)))
    by_shard = jnp.pad(
        by_shard.reshape(fs_size, small_rows, q_cols),
        ((0, 0), (0, slab_rows - shard - small_rows), (0, cols - q_cols)),
    )
    gq = left_dot(norm_attn, qkv_grad).astype(BF).reshape(fs_size, shard, cols)
    gw = left_dot(branch_grad, mixed).astype(BF)
    gw = gw.reshape(2, width // (2 * wide_part), wide_part, q_cols)
    tw, tq, tk, tv = reduce_parts(gw, gq, by_shard, 3, (q_cols, kv_cols, kv_cols), 3)
    sum_wo = jnp.swapaxes(tw.reshape(width, q_cols).astype(F32), 0, 1)
    sum_wq = tq[:shard].astype(F32)
    sum_wk = tk[:shard].astype(F32)
    sum_wv = tv[:shard].astype(F32)
    by_shard = jnp.sum(
        tq[shard : shard + small_rows].astype(F32).reshape(small_rows, fs_size, q_cols), axis=1
    ).reshape(-1)
    sum_wr = by_shard[: shard * expert_count].reshape(shard, expert_count)
    rest = by_shard[shard * expert_count : small_n - own.shape[1]]
    own = by_shard[small_n - own.shape[1] : small_n]
    sum_b = own[:cols]
    return (
        block_out.astype(jnp.bfloat16),
        grad_tokens,
        rest[:shard],
        sum_wq,
        sum_b[:q_cols],
        sum_wk,
        sum_b[q_cols : q_cols + kv_cols],
        sum_wv,
        sum_b[q_cols + kv_cols :],
        own[q_cols + 2 * kv_cols : q_cols + 2 * kv_cols + heads],
        sum_wo,
        own[q_cols + 2 * kv_cols + heads :],
        rest[shard : 2 * shard],
        sum_wr,
        rest[2 * shard :],
        grad_w_gate,
        grad_b_gate,
        grad_w_up,
        grad_b_up,
        grad_w_down,
        grad_b_down,
    )


def any_slice(
    tokens,
    seq_lengths,
    routes,
    attn_gain,
    w_query,
    b_query,
    w_key,
    b_key,
    w_value,
    b_value,
    sinks,
    w_out,
    b_out,
    ffn_gain,
    w_router,
    b_router,
    w_gate,
    b_gate,
    w_up,
    b_up,
    w_down,
    b_down,
    cotangent,
):
    rows, width = tokens.shape
    fs_size = lax.axis_size("fs")
    ep_size = lax.axis_size("ep")
    my_fs = lax.axis_index("fs")
    my_ep = lax.axis_index("ep")
    blocks = fs_size * ep_size
    expert_count = EXP_DEV * ep_size
    capacity = 3 * rows * TOP // (2 * expert_count)
    shard = w_query.shape[0]
    kv_heads = KEY_VALUE_HEADS // fs_size
    group = QUERY_HEADS // KEY_VALUE_HEADS
    q_cols = kv_heads * group * HEAD_SIZE
    kv_cols = kv_heads * HEAD_SIZE

    packed = jnp.concatenate(
        [attn_gain, ffn_gain, b_out, w_router.reshape(-1), b_router]
    )
    packed = lax.all_gather(packed, "fs", axis=0)
    gain_one = packed[:, :shard].reshape(-1).astype(jnp.float32)
    gain_two = packed[:, shard : 2 * shard].reshape(-1).astype(jnp.float32)
    bo = packed[:, 2 * shard : 3 * shard].reshape(-1).astype(jnp.float32)
    wr = packed[:, 3 * shard : (3 + expert_count) * shard].reshape(width, expert_count)
    br = packed[:, (3 + expert_count) * shard :].reshape(-1).astype(jnp.float32)
    whole_numbers = gather_all(
        jnp.concatenate([routes.reshape(-1), seq_lengths.reshape(-1)])[None]
    )
    routes_all = whole_numbers[:, : rows * TOP].reshape(blocks, rows, TOP)
    lengths_all = whole_numbers[:, rows * TOP :]
    lengths = lax.dynamic_index_in_dim(
        lengths_all.reshape(fs_size, ep_size, -1), my_ep, 1, keepdims=False
    )
    g_all = gather_all(cotangent)

    w_qkv = jnp.concatenate(
        [
            w_query.reshape(shard, fs_size, q_cols),
            w_key.reshape(shard, fs_size, kv_cols),
            w_value.reshape(shard, fs_size, kv_cols),
        ],
        axis=2,
    )
    w_qkv = lax.all_to_all(w_qkv, "fs", split_axis=1, concat_axis=0, tiled=True)
    w_qkv = w_qkv.reshape(width, q_cols + 2 * kv_cols)
    b_qkv = jnp.concatenate([b_query, b_key, b_value]).astype(jnp.float32)
    sink_score = sinks.astype(jnp.float32).reshape(1, kv_heads, group, 1)

    x_float = tokens.astype(jnp.float32)
    scale_one = norm_scale(x_float)
    norm_attn = gather_fs((x_float * scale_one * gain_one).astype(jnp.bfloat16))
    segment_ids, position = jax.vmap(lambda own: layout(own, rows))(lengths)
    cosine_table, sine_table = tables(position.reshape(-1), HEAD_SIZE // 2)
    qkv = jnp.dot(norm_attn, w_qkv, preferred_element_type=jnp.float32) + b_qkv
    many = fs_size * rows
    heads = kv_heads * group
    query = apply_rotation(
        qkv[:, :q_cols].reshape(many, heads, HEAD_SIZE), cosine_table, sine_table
    ).astype(jnp.bfloat16)
    query = query.reshape(fs_size, rows, kv_heads, group, HEAD_SIZE)
    key = apply_rotation(
        qkv[:, q_cols : q_cols + kv_cols].reshape(many, kv_heads, HEAD_SIZE),
        cosine_table,
        sine_table,
    ).astype(jnp.bfloat16)
    key = key.reshape(fs_size, rows, kv_heads, HEAD_SIZE)
    value = qkv[:, q_cols + kv_cols :].astype(jnp.bfloat16)
    value = value.reshape(fs_size, rows, kv_heads, HEAD_SIZE)
    places = jnp.arange(rows, dtype=jnp.int32)
    allowed = (segment_ids[:, :, None] == segment_ids[:, None, :]) & (
        places[:, None] >= places[None, :]
    )
    scores = mm("bqhgd,bkhd->bhgqk", query, key) * HEAD_SIZE ** (-0.5)
    masked = jnp.where(allowed[:, None, None], scores, MASKED_SCORE)
    top_score = jnp.maximum(jnp.max(masked, axis=-1), sink_score)
    exponent = jnp.exp(masked - top_score[..., None])
    sink_exp = jnp.exp(sink_score - top_score)
    denominator = jnp.sum(exponent, axis=-1) + sink_exp
    probs = exponent / denominator[..., None]
    sink_prob = sink_exp / denominator
    probs_b = probs.astype(jnp.bfloat16)
    mixed = mm("bhgqk,bkhd->bqhgd", probs_b, value).astype(jnp.bfloat16)
    mixed = mixed.reshape(many, q_cols)
    out_part = jnp.dot(mixed, w_out, preferred_element_type=jnp.float32)
    resid = x_float + scatter_fs(out_part.astype(jnp.bfloat16)).astype(jnp.float32) + bo
    scale_two = norm_scale(resid)
    norm_ffn = (resid * scale_two * gain_two).astype(jnp.bfloat16)

    n_all = gather_all(norm_ffn)
    logits = jnp.dot(n_all, wr, preferred_element_type=jnp.float32) + br
    logits = logits.reshape(blocks, rows, expert_count)
    one_hot = (
        routes_all[:, :, :, None] == jnp.arange(expert_count, dtype=jnp.int32)
    ).astype(jnp.float32)
    member = jnp.sum(one_hot, axis=2)
    peak = jnp.max(jnp.where(member > 0, logits, MASKED_SCORE), axis=-1, keepdims=True)
    gate_exp = jnp.where(member > 0, jnp.exp(logits - peak), 0.0)
    gates = gate_exp / jnp.sum(gate_exp, axis=-1, keepdims=True)
    own_member = lax.dynamic_slice_in_dim(member, my_ep * EXP_DEV, EXP_DEV, axis=2)
    own_gates = lax.dynamic_slice_in_dim(gates, my_ep * EXP_DEV, EXP_DEV, axis=2)
    rank = jnp.cumsum(own_member, axis=1) - own_member
    slots = jnp.arange(capacity, dtype=jnp.float32)
    pick = (rank.transpose(0, 2, 1)[:, :, None, :] == slots[:, None]) & (
        own_member.transpose(0, 2, 1)[:, :, None, :] > 0
    )
    pick_b = pick.astype(jnp.bfloat16)
    slot_gate = jnp.sum(
        jnp.where(pick, own_gates.transpose(0, 2, 1)[:, :, None, :], 0.0), axis=-1
    )
    slot_gate = slot_gate.transpose(1, 0, 2).reshape(EXP_DEV, blocks * capacity, 1)

    def spread(full):
        parts = mm("bekt,btd->ebkd", pick_b, full.reshape(blocks, rows, -1))
        return parts.astype(jnp.bfloat16).reshape(EXP_DEV, blocks * capacity, -1)

    def combine(parts):
        parts = parts.reshape(EXP_DEV, blocks, capacity, -1)
        return mm("bekt,ebkd->btd", pick_b, parts).reshape(blocks * rows, -1)

    x_slots = spread(n_all)
    g_slots = spread(g_all)
    gate_pre = mm("erd,edf->erf", x_slots, w_gate) + b_gate.astype(jnp.float32)[:, None]
    up_pre = mm("erd,edf->erf", x_slots, w_up) + b_up.astype(jnp.float32)[:, None]
    gate_soft = CLAMP_LIMIT * jnp.tanh(gate_pre / CLAMP_LIMIT)
    up_soft = CLAMP_LIMIT * jnp.tanh(up_pre / CLAMP_LIMIT)
    gate_sig = jax.nn.sigmoid(SWIGLU_ALPHA * gate_soft)
    glu_part = gate_soft * gate_sig
    middle = ((up_soft + 1.0) * glu_part).astype(jnp.bfloat16)
    first = (my_fs == 0).astype(jnp.float32)
    down_bias = b_down.astype(jnp.float32) * first
    expert_out = mm("erf,efd->erd", middle, w_down) + down_bias[:, None]
    expert_sum = scatter_all(
        combine((expert_out * slot_gate).astype(jnp.bfloat16)).astype(jnp.bfloat16)
    )
    block_out = resid + expert_sum.astype(jnp.float32)

    expert_grad = (g_slots.astype(jnp.float32) * slot_gate).astype(jnp.bfloat16)
    plain_grad = mm("erd,efd->erf", g_slots, w_down)
    middle_grad = plain_grad * slot_gate
    gate_dot = jnp.sum(plain_grad * middle.astype(jnp.float32), axis=-1) + jnp.sum(
        g_slots.astype(jnp.float32) * down_bias[:, None], axis=-1
    )
    grad_w_down = mm("erf,erd->efd", middle, expert_grad)
    grad_b_down = jnp.sum(expert_grad, axis=1, dtype=jnp.float32)
    up_grad = (middle_grad * glu_part * (1.0 - (up_soft / CLAMP_LIMIT) ** 2)).astype(jnp.bfloat16)
    gate_grad_pre = (
        middle_grad
        * (up_soft + 1.0)
        * (gate_sig + SWIGLU_ALPHA * gate_soft * gate_sig * (1.0 - gate_sig))
        * (1.0 - (gate_soft / CLAMP_LIMIT) ** 2)
    ).astype(jnp.bfloat16)
    grad_w_gate = mm("erd,erf->edf", x_slots, gate_grad_pre)
    grad_b_gate = jnp.sum(gate_grad_pre, axis=1, dtype=jnp.float32)
    grad_w_up = mm("erd,erf->edf", x_slots, up_grad)
    grad_b_up = jnp.sum(up_grad, axis=1, dtype=jnp.float32)
    row_part = mm("erf,edf->erd", gate_grad_pre, w_gate) + mm("erf,edf->erd", up_grad, w_up)
    row_sum = combine(row_part.astype(jnp.bfloat16))
    own_dot = jnp.sum(
        jnp.where(pick, gate_dot.reshape(EXP_DEV, blocks, capacity).transpose(1, 0, 2)[..., None], 0.0),
        axis=2,
    )
    dots = jnp.sum(
        own_dot[..., None]
        * (
            (my_ep * EXP_DEV + jnp.arange(EXP_DEV))[:, None] == jnp.arange(expert_count)[None]
        ).astype(jnp.float32)[None, :, None, :],
        axis=1,
    ).reshape(blocks * rows, expert_count)
    row_sum = scatter_all(jnp.concatenate([row_sum, dots], axis=1).astype(jnp.bfloat16))
    row_sum = row_sum.astype(jnp.float32)
    gate_grad = row_sum[:, width:]
    mine = my_fs * ep_size + my_ep
    gates_here = lax.dynamic_index_in_dim(gates, mine, 0, keepdims=False)
    logit_grad = gates_here * (
        gate_grad - jnp.sum(gates_here * gate_grad, axis=-1, keepdims=True)
    )
    logit_grad = logit_grad.astype(jnp.bfloat16)
    grad_br = jnp.sum(logit_grad, axis=0, dtype=jnp.float32)
    grad_wr = left_dot(norm_ffn, logit_grad)
    norm_ffn_grad = row_sum[:, :width] + jnp.dot(
        logit_grad, wr.T, preferred_element_type=jnp.float32
    )
    resid_norm_grad, grad_gain_two = norm_back(resid, scale_two, gain_two, norm_ffn_grad)
    resid_grad = cotangent.astype(jnp.float32) + resid_norm_grad

    branch_grad = gather_fs(resid_grad.astype(jnp.bfloat16))
    grad_bo = jnp.sum(branch_grad, axis=0, dtype=jnp.float32)
    mixed_grad = mm("td,fd->tf", branch_grad, w_out).astype(jnp.bfloat16)
    mixed_grad = mixed_grad.reshape(fs_size, rows, kv_heads, group, HEAD_SIZE)
    grad_wo = left_dot(mixed, branch_grad)
    grad_probs = mm("bqhgd,bkhd->bhgqk", mixed_grad, value)
    value_grad = mm("bhgqk,bqhgd->bkhd", probs_b, mixed_grad)
    row_delta = jnp.sum(probs * grad_probs, axis=-1)
    score_grad = (probs * (grad_probs - row_delta[..., None])).astype(jnp.bfloat16)
    query_grad = mm("bhgqk,bkhd->bqhgd", score_grad, key) * HEAD_SIZE ** (-0.5)
    key_grad = mm("bhgqk,bqhgd->bkhd", score_grad, query) * HEAD_SIZE ** (-0.5)
    grad_sink = -jnp.sum(sink_prob * row_delta, axis=(0, 3)).reshape(-1)
    query_pre_grad = undo_rotation(
        query_grad.reshape(many, heads, HEAD_SIZE), cosine_table, sine_table
    ).reshape(many, q_cols)
    key_pre_grad = undo_rotation(
        key_grad.reshape(many, kv_heads, HEAD_SIZE), cosine_table, sine_table
    ).reshape(many, kv_cols)
    qkv_grad = jnp.concatenate(
        [query_pre_grad, key_pre_grad, value_grad.reshape(many, kv_cols)], axis=1
    ).astype(jnp.bfloat16)
    grad_b_qkv = jnp.sum(qkv_grad, axis=0, dtype=jnp.float32)
    norm_attn_grad = scatter_fs(
        mm("tf,df->td", qkv_grad, w_qkv).astype(jnp.bfloat16)
    ).astype(jnp.float32)
    input_norm_grad, grad_gain_one = norm_back(x_float, scale_one, gain_one, norm_attn_grad)
    grad_tokens = resid_grad + input_norm_grad
    grad_qkv = left_dot(norm_attn, qkv_grad).astype(jnp.bfloat16)
    if shard % ep_size == 0:
        grad_qkv = grad_qkv.reshape(fs_size, ep_size, shard // ep_size, q_cols + 2 * kv_cols)
        grad_qkv = lax.psum_scatter(grad_qkv, "ep", scatter_dimension=1, tiled=False)
        grad_qkv = lax.all_to_all(grad_qkv, "fs", split_axis=0, concat_axis=1, tiled=False)
        grad_qkv = lax.all_gather(grad_qkv, "ep", axis=0, tiled=True).astype(jnp.float32)
    else:
        grad_qkv = lax.psum(grad_qkv.reshape(fs_size, shard, q_cols + 2 * kv_cols), "ep")
        grad_qkv = lax.all_to_all(grad_qkv, "fs", split_axis=0, concat_axis=1, tiled=False)
        grad_qkv = grad_qkv.astype(jnp.float32)
    sum_wq = grad_qkv[:, :, :q_cols].reshape(shard, -1)
    sum_wk = grad_qkv[:, :, q_cols : q_cols + kv_cols].reshape(shard, -1)
    sum_wv = grad_qkv[:, :, q_cols + kv_cols :].reshape(shard, -1)
    sum_wo = lax.psum(grad_wo.astype(jnp.bfloat16), "ep").astype(jnp.float32)
    by_shard = jnp.concatenate(
        [
            grad_wr.reshape(fs_size, -1),
            grad_gain_one.reshape(fs_size, -1),
            grad_gain_two.reshape(fs_size, -1),
            grad_br.reshape(fs_size, -1),
        ],
        axis=1,
    )
    by_shard = lax.psum(by_shard, ("fs", "ep"))
    by_shard = lax.dynamic_index_in_dim(by_shard, my_fs, 0, keepdims=False)
    sum_wr = by_shard[: shard * expert_count].reshape(shard, expert_count)
    rest = by_shard[shard * expert_count :]
    own = jnp.concatenate(
        [
            grad_b_qkv,
            grad_sink,
            lax.dynamic_slice_in_dim(grad_bo, my_fs * shard, shard),
        ]
    )
    own = lax.psum(own, "ep")
    sum_b = own[: q_cols + 2 * kv_cols]
    return (
        block_out.astype(jnp.bfloat16),
        grad_tokens,
        rest[:shard],
        sum_wq,
        sum_b[:q_cols],
        sum_wk,
        sum_b[q_cols : q_cols + kv_cols],
        sum_wv,
        sum_b[q_cols + kv_cols :],
        own[q_cols + 2 * kv_cols : q_cols + 2 * kv_cols + heads],
        sum_wo,
        own[q_cols + 2 * kv_cols + heads :],
        rest[shard : 2 * shard],
        sum_wr,
        rest[2 * shard :],
        grad_w_gate,
        grad_b_gate,
        grad_w_up,
        grad_b_up,
        grad_w_down,
        grad_b_down,
    )


def solution(mesh):
    in_specs = (
        P(("fs", "ep"), None),
        P(("fs", "ep"), None),
        P(("fs", "ep"), None),
        P("fs"),
        P("fs", None),
        P("fs"),
        P("fs", None),
        P("fs"),
        P("fs", None),
        P("fs"),
        P("fs"),
        P("fs", None),
        P("fs"),
        P("fs"),
        P("fs", None),
        P("fs"),
        P("ep", None, "fs"),
        P("ep", "fs"),
        P("ep", None, "fs"),
        P("ep", "fs"),
        P("ep", "fs", None),
        P("ep", None),
        P(("fs", "ep"), None),
    )
    out_specs = (
        P(("fs", "ep"), None),
        P(("fs", "ep"), None),
        P("fs"),
        P("fs", None),
        P("fs"),
        P("fs", None),
        P("fs"),
        P("fs", None),
        P("fs"),
        P("fs"),
        P("fs", None),
        P("fs"),
        P("fs"),
        P("fs", None),
        P("fs"),
        P("ep", None, "fs"),
        P("ep", "fs"),
        P("ep", None, "fs"),
        P("ep", "fs"),
        P("ep", "fs", None),
        P("ep", None),
    )
    run = this_slice if (mesh.shape["fs"], mesh.shape["ep"]) == (4, 8) else any_slice
    return jax.shard_map(
        run, mesh=mesh, in_specs=in_specs, out_specs=out_specs, check_vma=False
    )
```

```python
from functools import partial

import jax
import jax.numpy as jnp
from jax import lax
from jax.experimental import pallas as pl
from jax.experimental.pallas import tpu as pltpu
from jax.sharding import PartitionSpec as P

QUERY_HEADS = 64
KEY_VALUE_HEADS = 8
HEAD_SIZE = 64
TOP = 4
EXP_DEV = 2


EPSILON = 1e-05
ROPE_BASE = 150000.0
SWIGLU_ALPHA = 1.702
CLAMP_LIMIT = 7.0
MASKED_SCORE = -1e30


F32 = jnp.float32
BF = jnp.bfloat16
MESH = pl.DeviceIdType.MESH


def layout(lengths, card_rows):
    seq_ends = jnp.cumsum(lengths)
    places = jnp.arange(card_rows, dtype=jnp.int32)
    past_end = (places[:, None] >= seq_ends[None, :]).astype(jnp.int32)
    segment_ids = jnp.sum(past_end, axis=1)
    position = places - jnp.sum(past_end * lengths[None, :], axis=1)
    return (segment_ids, position)


def tables(position, half_dim):
    inv_freq = jnp.exp(-jnp.log(ROPE_BASE) * jnp.arange(half_dim, dtype=jnp.float32) / half_dim)
    angles = position.astype(jnp.float32)[:, None] * inv_freq[None, :]
    return (jnp.cos(angles)[:, None, :], jnp.sin(angles)[:, None, :])


def apply_rotation(value_matrix, cosine_table, sine_table):
    half_dim = value_matrix.shape[-1] // 2
    lower_half = value_matrix[..., :half_dim]
    upper_half = value_matrix[..., half_dim:]
    return jnp.concatenate(
        [
            lower_half * cosine_table - upper_half * sine_table,
            upper_half * cosine_table + lower_half * sine_table,
        ],
        axis=-1,
    )


def undo_rotation(value_matrix, cosine_table, sine_table):
    half_dim = value_matrix.shape[-1] // 2
    lower_half = value_matrix[..., :half_dim]
    upper_half = value_matrix[..., half_dim:]
    return jnp.concatenate(
        [
            lower_half * cosine_table + upper_half * sine_table,
            upper_half * cosine_table - lower_half * sine_table,
        ],
        axis=-1,
    )


def norm_scale(value_matrix):
    return lax.rsqrt(jnp.mean(value_matrix * value_matrix, axis=-1, keepdims=True) + EPSILON)


def norm_back(value_matrix, inv_scale, gain, grad_norm):
    weighted = grad_norm * gain
    grad_values = inv_scale * weighted - value_matrix * inv_scale**3 * jnp.mean(
        weighted * value_matrix, axis=-1, keepdims=True
    )
    grad_gain = jnp.sum(grad_norm * value_matrix * inv_scale, axis=0)
    return (grad_values, grad_gain)


def left_dot(left, right):
    return jnp.dot(left.T, right, preferred_element_type=jnp.float32)


def mm(spec, left, right):
    return jnp.einsum(spec, left, right, preferred_element_type=jnp.float32)


def gather_all(value):
    return lax.all_gather(value, ("fs", "ep"), axis=0, tiled=True)


def scatter_all(value):
    return lax.psum_scatter(value, ("fs", "ep"), scatter_dimension=0, tiled=True)


def gather_fs(value):
    return lax.all_gather(value, "fs", axis=0, tiled=True)


def scatter_fs(value):
    return lax.psum_scatter(value, "fs", scatter_dimension=0, tiled=True)


def spot():
    fs=lax.axis_index("fs"); ep=lax.axis_index("ep")
    return fs, ep, fs//2, fs%2, ep//2, ep%2

def greet(fs, ep, z, more=0):
    y, x, c = fs//2, fs%2, ep%2
    bar=pltpu.get_barrier_semaphore()
    def hi(f,e): pl.semaphore_signal(bar,inc=1,device_id=(f,e),device_id_type=MESH)
    hi(fs+1-2*x,ep); hi(fs+2-4*y,ep); hi(fs,ep+1-2*c)
    if more: hi(3-fs,ep)
    @pl.when(z>0)
    def _(): hi(fs,ep-2)
    @pl.when(z<3)
    def _(): hi(fs,ep+2)
    @pl.when((z>0)&(z<3))
    def _(): pl.semaphore_wait(bar,5+more)
    @pl.when((z==0)|(z==3))
    def _(): pl.semaphore_wait(bar,4+more)

def scatter_kernel(na, parts, *refs):
    ps=refs[:na]; out=refs[na]; far=refs[na+1]
    q,v1,v2,vu,vd,stg,load,s0,r0,gsem,s1,r1,s2,r2,su,ru,sd,rd,osem = refs[na+2:]
    fs,ep,y,x,z,c = spot()
    rows=ps[0].shape[2]; pr=rows//parts; half=pr//2
    items=na*4*parts
    xn=(fs+1-2*x,ep); yn=(fs+2-4*y,ep); cn=(fs,ep+1-2*c)
    A=pl.ds(0,half); B=pl.ds(half,half)
    def rem(src,dst,s,r,dev): return pltpu.make_async_remote_copy(src,dst,s,r,device_id=dev,device_id_type=MESH)
    def where(i):
        a=i//(4*parts); j=i%(4*parts); k=j//parts; part=j%parts
        zz=(k%2)*(k//2)+(1-k%2)*(3-k//2)
        return a,part,zz
    def block(i,par):
        a,part,zz=where(i)
        return a,zz*2+par,pl.ds(part*pr,pr)
    def on_array(i,f):
        if na==1: f(ps[0])
        else:
            a=i//(4*parts)
            for n in range(na):
                @pl.when(a==n)
                def _(): f(ps[n])
    def give(i,p):
        _,e,r=block(i,1-c)
        return rem(p.at[:,e,r],far.at[i],s0.at[i],r0.at[i],cn)
    def mine(i,p):
        _,e,r=block(i,c)
        return pltpu.make_async_copy(p.at[:,e,r],q.at[i],load.at[i])
    def fetch(i):
        return pltpu.make_async_copy(far.at[i],stg.at[i%2],gsem.at[i%2])
    def one(i):
        return ([rem(q.at[i,2*j+1-x,A],v1.at[i,0,j],s1.at[i,j],r1.at[i,j],xn) for j in range(2)],
                rem(q.at[i,pl.ds((1-y)*2,2),B],v1.at[i,1],s1.at[i,2],r1.at[i,2],yn))
    def two(i):
        return (rem(q.at[i,(1-y)*2+x,A],v2.at[i,0],s2.at[i,0],r2.at[i,0],yn),
                rem(q.at[i,y*2+1-x,B],v2.at[i,1],s2.at[i,1],r2.at[i,1],xn))
    def up(i): return rem(q.at[i,fs],vu.at[i],su.at[i],ru.at[i],(fs,ep+2))
    def down(i): return rem(q.at[i,fs],vd.at[i],sd.at[i],rd.at[i],(fs,ep-2))
    greet(fs,ep,z)
    @pl.loop(0,items)
    def _(i):
        on_array(i,lambda p: give(i,p).start())
        on_array(i,lambda p: mine(i,p).start())
    def valid(i): return (i>=0)&(i<items)
    def add(dst,src,n):
        for lo in range(0,n,16):
            s=pl.ds(lo,16)
            dst(s,src(s))
    def getfar(i):
        on_array(i,lambda p: give(i,p).wait_recv())
        fetch(i).start()
    getfar(0)
    @pl.loop(0,items+6)
    def _(t):
        @pl.when(t<items)
        def _():
            i=t
            @pl.when(i+1<items)
            def _(): getfar(i+1)
            fetch(i).wait()
            on_array(i,lambda p: mine(i,p).wait())
            for g in range(4):
                q[i,g]=q[i,g]+stg[i%2,g]
            a,b=one(i)
            for k in a: k.start()
            b.start()
        i=t-1
        @pl.when(valid(i))
        def _():
            a,b=one(i)
            for k in a: k.wait_recv()
            for j in range(2):
                q[i,2*j+x,A]=q[i,2*j+x,A]+v1[i,0,j]
            ta,tb=two(i)
            ta.start()
            b.wait_recv()
            for j in range(2):
                q[i,2*y+j,B]=q[i,2*y+j,B]+v1[i,1,j]
            tb.start()
        i2=t-2
        @pl.when(valid(i2))
        def _():
            ta,tb=two(i2)
            ta.wait_recv()
            q[i2,fs,A]=q[i2,fs,A]+v2[i2,0]
            tb.wait_recv()
            q[i2,fs,B]=q[i2,fs,B]+v2[i2,1]
        iu=t-2-z
        @pl.when(valid(iu))
        def _():
            _,_,zz=where(iu)
            @pl.when(zz>=z)
            def _():
                @pl.when(z>0)
                def _():
                    up(iu).wait_recv()
                    q[iu,fs]=q[iu,fs]+vu[iu]
                @pl.when(zz>z)
                def _(): up(iu).start()
        idn=t-2-(3-z)
        @pl.when(valid(idn))
        def _():
            _,_,zz=where(idn)
            @pl.when(zz<=z)
            def _():
                @pl.when(z<3)
                def _():
                    down(idn).wait_recv()
                    q[idn,fs]=q[idn,fs]+vd[idn]
                @pl.when(zz<z)
                def _(): down(idn).start()
    @pl.loop(0,items)
    def _(i):
        a,part,zz=where(i)
        @pl.when(zz==z)
        def _():
            pltpu.make_async_copy(q.at[i,fs],out.at[a,pl.ds(part*pr,pr)],osem.at[i]).start()
    @pl.loop(0,items)
    def _(i):
        a,part,zz=where(i)
        on_array(i,lambda p: give(i,p).wait_send())
        a1,b1=one(i)
        for k in a1: k.wait_send()
        b1.wait_send()
        ta,tb=two(i); ta.wait_send(); tb.wait_send()
        @pl.when(zz>z)
        def _(): up(i).wait_send()
        @pl.when(zz<z)
        def _(): down(i).wait_send()
        @pl.when(zz==z)
        def _(): pltpu.make_async_copy(q.at[i,fs],out.at[a,pl.ds(part*pr,pr)],osem.at[i]).wait()

def scatter_blocks(arrays, cid, parts=2):
    na=len(arrays); rows,width=arrays[0].shape[-2:]
    arrays=[a.reshape(4,8,rows,width) for a in arrays]
    pr=rows//parts; items=na*4*parts; half=pr//2
    any_=pl.BlockSpec(memory_space=pl.ANY)
    D=pltpu.SemaphoreType.DMA
    V=lambda *s: pltpu.VMEM(s+(width,),BF)
    out,_=pl.pallas_call(partial(scatter_kernel,na,parts),
        out_shape=[jax.ShapeDtypeStruct((na,rows,width),BF),jax.ShapeDtypeStruct((items,4,pr,width),BF)],
        in_specs=[any_]*na,out_specs=[any_,any_],
        scratch_shapes=[V(items,4,pr),V(items,2,2,half),V(items,2,half),V(items,pr),V(items,pr),V(2,4,pr),
            D((items,)),D((items,)),D((items,)),D((2,)),D((items,3)),D((items,3)),D((items,2)),D((items,2)),
            D((items,)),D((items,)),D((items,)),D((items,)),D((items,))],
        compiler_params=pltpu.CompilerParams(collective_id=cid,has_side_effects=True,vmem_limit_bytes=63*1024*1024),
        name="scatter_blocks")(*arrays)
    return out


def reduce_kernel(
    wide_n, slab_n, splits, gw, gq, gs, tw, tq, tk, tv,
    own_w, own_q, all_q, far_w, far_q, pin_w, pin_q, pout_w, pout_q, din_w, din_q, dout_w, dout_q, tot_w, tot_q, mate_q,
    wload, qload, s0w, r0w, s0q, r0q, sa, ra, su, ru, sd, rd, keep, keep_q, keep_m, sc, rc,
):
    fs, ep, y, x, z, c = spot()
    mate = (fs, ep + 1 - 2 * c)
    rows_w, rows_q = own_w.shape[1], own_q.shape[1]
    parts = slab_n // 4
    items = wide_n + slab_n

    def rem(src, dst, s, r, dev):
        return pltpu.make_async_remote_copy(src, dst, s, r, device_id=dev, device_id_type=MESH)

    def source(s):
        return ((y + s // 2) % 2) * 2 + (x + s) % 2

    def give_w(i):
        return rem(gw.at[1 - c, i], far_w.at[i], s0w.at[i], r0w.at[i], mate)

    def load_w(i):
        return pltpu.make_async_copy(gw.at[c, i], own_w.at[i], wload.at[i])

    body = gq.shape[1] - (2 * parts - 1) * rows_q

    def pieces(s, core, dst):
        base = core * parts * rows_q
        out = []
        for p in range(parts):
            n = rows_q if p < parts - 1 else body
            at = pl.ds(pl.multiple_of(base + p * rows_q, 16), n)
            out.append((gq.at[source(s), at], dst.at[s, p, pl.ds(0, n)]))
        rest = dst.at[s, parts - 1, pl.ds(body, rows_q - body)]
        at = pl.ds((parts - 1) * rows_q + body, rows_q - body)
        return out + [(gq.at[source(s), at], rest)], (gs.at[source(s)], rest)

    def give_q(s, do):
        common, other = pieces(s, 1 - c, far_q)

        def move(n, pair):
            do(rem(*pair, s0q.at[s, n], r0q.at[s, n], mate))

        for n, pair in enumerate(common[:-1]):
            move(n, pair)

        @pl.when(c == 1)
        def _():
            move(parts, common[-1])

        @pl.when(c == 0)
        def _():
            move(parts, other)

    def load_q(s, do):
        common, other = pieces(s, c, all_q)

        def move(n, pair):
            do(pltpu.make_async_copy(*pair, qload.at[s, n]))

        for n, pair in enumerate(common[:-1]):
            move(n, pair)

        @pl.when(c == 0)
        def _():
            move(parts, common[-1])

        @pl.when(c == 1)
        def _():
            move(parts, other)

    def pass_q(s):
        dev = (source(s), ep)
        return rem(all_q.at[s], own_q.at[pl.ds(s * parts, parts)], sa.at[s], ra.at[s], dev)

    def on_item(i, f):
        @pl.when(i < wide_n)
        def _():
            f(own_w, pin_w, pout_w, din_w, dout_w, tot_w, i)

        @pl.when(i >= wide_n)
        def _():
            f(own_q, pin_q, pout_q, din_q, dout_q, tot_q, i - wide_n)

    def valid(i):
        return (i >= 0) & (i < items)

    def place(buf, sem, j, core):
        at = pl.ds(pl.multiple_of((core * parts + j % parts) * rows_q, 16), rows_q)
        lo, out = 0, []
        for n, (dst, size) in enumerate(zip((tq, tk, tv), splits)):
            to = pl.ds(pl.multiple_of(source(j // parts) * size, 128), size)
            out.append(
                pltpu.make_async_copy(buf.at[j, :, pl.ds(lo, size)], dst.at[at, to], sem.at[j, n])
            )
            lo += size
        return out

    def share_w(i):
        dst = tw.at[c, i]
        return (
            pltpu.make_async_copy(tot_w.at[i], dst, keep.at[i]),
            rem(tot_w.at[i], dst, sc.at[i], rc.at[i], mate),
        )

    def share_q(j):
        i = j + wide_n
        return rem(tot_q.at[j], mate_q.at[j], sc.at[i], rc.at[i], mate)

    greet(fs, ep, z, 1)

    @pl.loop(0, wide_n)
    def _(i):
        give_w(i).start()
        load_w(i).start()

    for s in (1, 2, 3, 0):
        give_q(s, lambda copy: copy.start())
        load_q(s, lambda copy: copy.start())

    @pl.loop(0, items + 4)
    def _(t):
        @pl.when(t < wide_n)
        def _():
            load_w(t).wait()
            give_w(t).wait_recv()
            own_w[t] = own_w[t] + far_w[t]

        for n, s in enumerate((1, 2, 3, 0)):

            @pl.when(t == n + 3)
            def _():
                load_q(s, lambda copy: copy.wait())
                give_q(s, lambda copy: copy.wait_recv())

                @pl.loop(0, parts)
                def _(j):
                    if s:
                        all_q[s, j] = all_q[s, j] + far_q[s, j]
                    else:
                        own_q[j] = all_q[0, j] + far_q[0, j]

                if s:
                    pass_q(s).start()

        for s in (1, 2, 3):

            @pl.when(t == wide_n + s * parts)
            def _():
                pass_q(s).wait_recv()

        iu = t - z

        @pl.when(valid(iu))
        def _():
            def go(own, pin, pout, din, dout, tot, i):
                @pl.when(z == 0)
                def _():
                    rem(own.at[i], pin.at[i], su.at[iu], ru.at[iu], (fs, ep + 2)).start()

                @pl.when(z > 0)
                def _():
                    rem(own.at[i], pin.at[i], su.at[iu], ru.at[iu], (fs, ep - 2)).wait_recv()

                @pl.when((z > 0) & (z < 3))
                def _():
                    pout[i] = pin[i] + own[i]
                    rem(pout.at[i], pin.at[i], su.at[iu], ru.at[iu], (fs, ep + 2)).start()

            on_item(iu, go)

        idn = t - 3 + z

        @pl.when(valid(idn))
        def _():
            def go(own, pin, pout, din, dout, tot, i):
                @pl.when(z == 3)
                def _():
                    rem(own.at[i], din.at[i], sd.at[idn], rd.at[idn], (fs, ep - 2)).start()

                @pl.when(z < 3)
                def _():
                    rem(own.at[i], din.at[i], sd.at[idn], rd.at[idn], (fs, ep + 2)).wait_recv()

                @pl.when((z > 0) & (z < 3))
                def _():
                    dout[i] = din[i] + own[i]
                    rem(dout.at[i], din.at[i], sd.at[idn], rd.at[idn], (fs, ep - 2)).start()

            on_item(idn, go)

        last = t - 3

        @pl.when(valid(last))
        def _():
            def go(own, pin, pout, din, dout, tot, i):
                @pl.when(z == 0)
                def _():
                    tot[i] = own[i] + din[i]

                @pl.when(z == 3)
                def _():
                    tot[i] = own[i] + pin[i]

                @pl.when((z == 1) | (z == 2))
                def _():
                    tot[i] = own[i] + pin[i] + din[i]

            on_item(last, go)

            @pl.when(last < wide_n)
            def _():
                for copy in share_w(last):
                    copy.start()

            @pl.when(last >= wide_n)
            def _():
                j = last - wide_n
                for copy in (share_q(j), *place(tot_q, keep_q, j, c)):
                    copy.start()

    @pl.loop(0, items)
    def _(i):
        @pl.when(i < wide_n)
        def _():
            for copy in share_w(i):
                copy.wait()

        @pl.when(i >= wide_n)
        def _():
            j = i - wide_n
            share_q(j).wait()
            for copy in place(mate_q, keep_m, j, 1 - c):
                copy.start()

        def go(own, pin, pout, din, dout, tot, j):
            @pl.when(z < 3)
            def _():
                rem(own.at[j], pin.at[j], su.at[i], ru.at[i], (fs, ep + 2)).wait_send()

            @pl.when(z > 0)
            def _():
                rem(own.at[j], din.at[j], sd.at[i], rd.at[i], (fs, ep - 2)).wait_send()

        on_item(i, go)

    @pl.loop(0, slab_n)
    def _(j):
        for copy in (*place(tot_q, keep_q, j, c), *place(mate_q, keep_m, j, 1 - c)):
            copy.wait()

    @pl.loop(0, wide_n)
    def _(i):
        give_w(i).wait_send()

    for s in range(4):
        give_q(s, lambda copy: copy.wait_send())
        if s:
            pass_q(s).wait_send()


def reduce_parts(gw, gq, gs, parts, splits, cid):
    wide_n = gw.shape[1]
    slab_rows = gq.shape[1] + gs.shape[1]
    rows_q, cols = slab_rows // (2 * parts), gq.shape[2]
    slab_n = 4 * parts
    free = pl.BlockSpec(memory_space=pl.ANY)
    D = pltpu.SemaphoreType.DMA
    W = pltpu.VMEM((wide_n,) + gw.shape[2:], BF)
    Q = pltpu.VMEM((slab_n, rows_q, cols), BF)
    Q4 = pltpu.VMEM((4, parts, rows_q, cols), BF)
    items = wide_n + slab_n
    return pl.pallas_call(
        partial(reduce_kernel, wide_n, slab_n, splits),
        out_shape=[jax.ShapeDtypeStruct(gw.shape, BF)]
        + [jax.ShapeDtypeStruct((slab_rows, 4 * size), BF) for size in splits],
        in_specs=[free] * 3,
        out_specs=[free] * 4,
        scratch_shapes=[W, Q, Q4, W, Q4] + [W, Q] * 5 + [Q]
        + [D((wide_n,)), D((4, parts + 1)), D((wide_n,)), D((wide_n,)), D((4, parts + 1)), D((4, parts + 1))]
        + [D((4,)), D((4,))]
        + [D((items,))] * 4 + [D((wide_n,)), D((slab_n, 3)), D((slab_n, 3)), D((items,)), D((items,))],
        compiler_params=pltpu.CompilerParams(
            collective_id=cid, has_side_effects=True, vmem_limit_bytes=63 * 1024 * 1024
        ),
        cost_estimate=pl.CostEstimate(flops=0, bytes_accessed=500_000_000, transcendentals=0),
        name="reduce_parts",
    )(gw, gq, gs)


def start_kernel(
    splits, own, few, wq, wk, wv, rows_out, few_out, w_out, own_cols,
    here, here_few, own_w, sx, rx, sf, rf, sw, rw, sm, rm,
):
    fs, ep, y, x, z, c = spot()
    mate = (fs, ep + 1 - 2 * c)
    shard = wq.shape[0]
    pair = (fs, ep + 2 - 4 * (z % 2))
    units = shard // 16
    edges = [16 * (units * n // 4) for n in range(5)]
    quarters = [(lo, hi - lo) for lo, hi in zip(edges, edges[1:])]
    half = own.shape[0] // 2
    bands = (pl.ds(0, half), pl.ds(half, half))

    def peer(s):
        return ((y + s // 2) % 2) * 2 + (x + s) % 2

    def rem(src, dst, s, r, dev):
        return pltpu.make_async_remote_copy(src, dst, s, r, device_id=dev, device_id_type=MESH)

    def columns(dev, at):
        lo, out = 0, []
        for src, size in zip((wq, wk, wv), splits):
            cols = pl.ds(pl.multiple_of(dev * size, 128), size)
            out.append((src.at[at, cols], pl.ds(lo, size)))
            lo += size
        return out

    def send(s, lo, n):
        at = pl.ds(lo, n)
        return [
            rem(src, w_out.at[fs, at, cols], sw.at[s, k], rw.at[s, k], (peer(s), ep))
            for k, (src, cols) in enumerate(columns(peer(s), at))
        ]

    def arrive(s, lo, n):
        at = pl.ds(lo, n)
        return [
            rem(w_out.at[peer(s), at, cols], w_out.at[peer(s), at, cols], sw.at[s, k], rw.at[s, k], mate)
            for k, (_, cols) in enumerate(columns(fs, at))
        ]

    def share(s, k, lo, n, dev):
        v = w_out.at[peer(s), pl.ds(lo, n)]
        return rem(v, v, sm.at[s, k], rm.at[s, k], dev)

    def give(s, band):
        v = rows_out.at[fs, bands[band]]
        return rem(v, v, sx.at[s, band], rx.at[s, band], (peer(s), ep))

    def pass_on(s, band):
        v = rows_out.at[peer(s), bands[band]]
        return rem(v, v, sx.at[3, band], rx.at[3, band], (peer(3 - s), ep))

    def give_few(s):
        return rem(few, few_out.at[fs], sf.at[s], rf.at[s], (peer(s), ep))

    keep = pltpu.make_async_copy(own, rows_out.at[fs], here)
    keep.start()
    keep_few = pltpu.make_async_copy(few, few_out.at[fs], here_few)
    keep_few.start()
    locals_ = []
    for k, (src, cols) in enumerate(columns(fs, pl.ds(0, shard))):
        locals_.append(pltpu.make_async_copy(src, own_cols.at[:, cols], own_w.at[k]))
    for copy in locals_:
        copy.start()
    greet(fs, ep, z, 1)
    keep.wait()
    for copy in locals_:
        copy.wait()
    own_slab = pltpu.make_async_copy(own_cols, w_out.at[fs], here)
    own_slab.start()
    for s in (1, 2, 3):
        give_few(s).start()
    for quarter in range(4):

        @pl.when((z % 2) * 2 + c == quarter)
        def _():
            mine, mates, pairs, last = (quarters[quarter ^ n] for n in (0, 1, 2, 3))
            for s in (3, 1, 2):
                for copy in send(s, *mine):
                    copy.start()
            for s, band in ((1, 0), (2, 1), (1, 1), (2, 0)):
                give(s, band).start()
            for s in (1, 2, 3):
                for copy in arrive(s, *mine):
                    copy.wait_recv()
                share(s, 0, *mine, pair).start()
                share(s, 1, *mine, mate).start()
            give(1, 0).wait_recv()
            pass_on(1, 0).start()
            give(2, 1).wait_recv()
            pass_on(2, 1).start()
            for s in (1, 2, 3):
                share(s, 0, *pairs, pair).wait_recv()
                share(s, 2, *pairs, mate).start()
            for s in (1, 2, 3):
                share(s, 1, *mates, mate).wait_recv()
                share(s, 2, *last, mate).wait_recv()
            for s in (1, 2, 3):
                for copy in send(s, *mine):
                    copy.wait_send()
                share(s, 0, *mine, pair).wait_send()
                share(s, 1, *mine, mate).wait_send()
                share(s, 2, *pairs, mate).wait_send()

    for s in (1, 2):
        give(s, 2 - s).wait_recv()
        for band in range(2):
            give(s, band).wait_send()
    for s, band in ((1, 0), (2, 1)):
        pass_on(s, band).wait()
    for s in (1, 2, 3):
        give_few(s).wait_send()
        rem(few, few_out.at[peer(s)], sf.at[s], rf.at[s], mate).wait_recv()
    own_slab.wait()
    keep_few.wait()


def start_exchange(own, few, wq, wk, wv, cid):
    shard = wq.shape[0]
    splits = tuple(w.shape[1] // 4 for w in (wq, wk, wv))
    free = pl.BlockSpec(memory_space=pl.ANY)
    D = pltpu.SemaphoreType.DMA
    return pl.pallas_call(
        partial(start_kernel, splits),
        out_shape=[
            jax.ShapeDtypeStruct((4,) + own.shape, BF),
            jax.ShapeDtypeStruct((4,) + few.shape, BF),
            jax.ShapeDtypeStruct((4, shard, sum(splits)), BF),
        ],
        in_specs=[pl.BlockSpec(memory_space=pltpu.VMEM)] * 2 + [free] * 3,
        out_specs=[free] * 3,
        scratch_shapes=[pltpu.VMEM((shard, sum(splits)), BF), D, D, D((3,)), D((4, 2)), D((4, 2)), D((4,)), D((4,)), D((4, 3)), D((4, 3)), D((4, 3)), D((4, 3))],
        compiler_params=pltpu.CompilerParams(collective_id=cid, has_side_effects=True),
        name="start_exchange",
    )(own, few, wq, wk, wv)


def nn(left, right):
    return lax.dot_general(left, right, (((1,), (0,)), ((), ())), preferred_element_type=F32)


def nt(left, right):
    return lax.dot_general(left, right, (((1,), (1,)), ((), ())), preferred_element_type=F32)


def tn(left, right):
    return lax.dot_general(left, right, (((0,), (0,)), ((), ())), preferred_element_type=F32)


def strips(total, size):
    return [(at, min(size, total - at)) for at in range(0, total, size)]


def remote(src, dst, send, recv, device):
    return pltpu.make_async_remote_copy(
        src, dst, send, recv, device_id=device, device_id_type=MESH
    )


def line_order(z, i):
    code = jnp.where(z == 0, 228, jnp.where(z == 1, 225, jnp.where(z == 2, 30, 27)))
    power = jnp.where(i == 0, 1, jnp.where(i == 1, 4, jnp.where(i == 2, 16, 64)))
    return (code // power) % 4


class Gather:
    def __init__(self, full, sems):
        self.full = full
        self.sz, self.rz, self.s1, self.r1, self.s2, self.r2, self.sc, self.rc = sems
        self.fs, self.ep, self.y, self.x, self.z, self.c = spot()
        half = full.shape[3] // 2
        self.upper, self.lower = pl.ds(0, half), pl.ds(half, half)
        self.xn = (self.fs + 1 - 2 * self.x, self.ep)
        self.yn = (self.fs + 2 - 4 * self.y, self.ep)
        self.mate = (self.fs, self.ep + 1 - 2 * self.c)

    def item(self, t):
        return t // 4, line_order(self.z, t % 4)

    def along(self, a, zz, up):
        view = self.full.at[a, self.fs, zz * 2 + self.c]
        other = (self.fs, self.ep + (2 if up else -2))
        return remote(view, view, self.sz.at[a, zz, up], self.rz.at[a, zz], other)

    def first(self, a, zz):
        e = zz * 2 + self.c
        v = self.full.at[a, self.fs, e, self.upper]
        w = self.full.at[a, self.fs, e, self.lower]
        s, r = self.s1.at[a, zz], self.r1.at[a, zz]
        return (
            remote(v, v, s.at[0], r.at[0], self.xn),
            remote(w, w, s.at[1], r.at[1], self.yn),
            remote(w, w, s.at[2], r.at[2], self.xn),
            remote(v, v, s.at[3], r.at[3], self.yn),
        )

    def second(self, a, zz):
        e = zz * 2 + self.c
        v = self.full.at[a, self.y * 2 + 1 - self.x, e, self.upper]
        w = self.full.at[a, (1 - self.y) * 2 + self.x, e, self.lower]
        s, r = self.s2.at[a, zz], self.r2.at[a, zz]
        return remote(v, v, s.at[0], r.at[0], self.yn), remote(w, w, s.at[1], r.at[1], self.xn)

    def across(self, a, zz, e):
        v = self.full.at[a, :, zz * 2 + e]
        return remote(v, v, self.sc.at[a, zz], self.rc.at[a, zz], self.mate)

    def step0(self, t):
        @pl.when(t < 8)
        def _():
            a, zz = self.item(t)

            @pl.when(zz != self.z)
            def _():
                self.along(a, zz, 0).wait_recv()

            @pl.when((zz <= self.z) & (self.z < 3))
            def _():
                self.along(a, zz, 1).start()

            @pl.when((zz >= self.z) & (self.z > 0))
            def _():
                self.along(a, zz, 0).start()

    def step0_if(self, t, inner):
        inside = (self.z == 1) | (self.z == 2)

        @pl.when(inside == inner)
        def _():
            self.step0(t)

    def step1(self, t):
        @pl.when(t < 8)
        def _():
            for copy in self.first(*self.item(t)):
                copy.start()

    def step2(self, t):
        @pl.when(t < 8)
        def _():
            a, zz = self.item(t)
            from_x, from_y, _, _ = self.first(a, zz)
            to_y, to_x = self.second(a, zz)
            from_x.wait_recv()
            to_y.start()
            from_y.wait_recv()
            to_x.start()

    def step3(self, t):
        @pl.when(t < 8)
        def _():
            a, zz = self.item(t)
            for copy in (*self.first(a, zz)[2:], *self.second(a, zz)):
                copy.wait_recv()
            self.across(a, zz, self.c).start()

    def step4(self, t):
        a, zz = self.item(t)
        self.across(a, zz, 1 - self.c).wait_recv()

    def finish(self):
        @pl.loop(0, 8)
        def _(t):
            a, zz = self.item(t)
            self.across(a, zz, self.c).wait_send()
            for copy in (*self.first(a, zz), *self.second(a, zz)):
                copy.wait_send()

            @pl.when((zz <= self.z) & (self.z < 3))
            def _():
                self.along(a, zz, 1).wait_send()

            @pl.when((zz >= self.z) & (self.z > 0))
            def _():
                self.along(a, zz, 0).wait_send()


def experts_kernel(
    cap, width,
    n_own, g_own, wg_hbm, wu_hbm, wd_hbm, bg_ref, bu_ref, bd_ref,
    full, out_hbm, row_hbm, xs_hbm, eg_hbm, mid_hbm, ug_hbm, gg_hbm, cu_hbm, cg_hbm,
    sum_g, sum_u, sum_d,
    wg_ref, wu_ref, wd_ref, bin_, meta, pmat, pmat_t, gates, xs, res, mid, cub, cgb, dots, stage,
    w_sem, own_sem, in_sem, st_sem, save_sem,
    *sems,
):
    gather = Gather(full, sems)
    fs, ep, z = gather.fs, gather.ep, gather.z
    card_rows, wpad = bin_.shape[2:]
    tail = wpad - 128
    off = width - tail
    first = jnp.where(fs == 0, 1.0, 0.0).astype(F32)
    nb = 8
    rows = nb * cap
    weights = [
        pltpu.make_async_copy(src, dst, w_sem.at[n])
        for n, (src, dst) in enumerate(((wg_hbm, wg_ref), (wu_hbm, wu_ref), (wd_hbm, wd_ref)))
    ]
    keep = [
        pltpu.make_async_copy(src, full.at[a, fs, ep], own_sem.at[a])
        for a, src in enumerate((n_own, g_own))
    ]
    for copy in keep + weights:
        copy.start()
    greet(fs, ep, z)
    for copy in keep:
        copy.wait()
    gather.step0(0)
    gather.step1(0)
    gather.step0(1)
    gather.step2(0)
    gather.step1(1)
    gather.step3(0)
    gather.step0(2)

    def load(t):
        a, zz = gather.item(t)
        return pltpu.make_async_copy(full.at[a, :, pl.ds(zz * 2, 2)], bin_, in_sem)

    def save(src, dst, k, i, n):
        return pltpu.make_async_copy(src.at[k], dst.at[k, i], save_sem.at[n, k])

    def save_rows(dst, k, i):
        return pltpu.make_async_copy(xs.at[:, k], dst.at[k, i], save_sem.at[0, k])

    def fetch(src, dst, k, i, n):
        return pltpu.make_async_copy(src.at[k, i], dst.at[k], save_sem.at[n, k])

    def rows_of(ref, k, lo=0, n=width):
        return ref[:, k, :, lo : lo + n].reshape(rows, n)

    def next_load(t):
        @pl.when(t < 8)
        def _():
            gather.step4(t)
            load(t).start()

    def spread(i, prepare):
        @pl.loop(0, nb)
        def _(b):
            j, c = b // 2, b % 2
            if prepare:
                meta[...] = jnp.transpose(bin_[j, c, :, tail:].astype(F32))
                at = pl.ds(pl.multiple_of(b * cap, 16), cap)
                hits = []
                for k in range(2):
                    e = ep * 2 + k
                    place = meta[pl.ds(off + e, 1), :]
                    gate = meta[pl.ds(off + 16 + e, 1), :] + meta[pl.ds(off + 32 + e, 1), :]
                    hit = lax.broadcasted_iota(jnp.int32, (cap, card_rows), 0).astype(F32) == place
                    gates[i, k, at, :] = jnp.sum(jnp.where(hit, gate, 0.0), axis=1, keepdims=True)
                    hits.append(jnp.where(hit, 1.0, 0.0))
                hits.append(jnp.zeros((card_rows - 2 * cap, card_rows), F32))
                hits = jnp.concatenate(hits, axis=0)
                pmat[i, b] = hits[: 2 * cap].astype(BF)
                pmat_t[i, b] = jnp.transpose(hits).astype(BF)
            pick = pmat[i, b]
            for lo, n in strips(width, 768):
                got = nn(pick, bin_[j, c, :, lo : lo + n]).astype(BF)
                xs[b, :, :, lo : lo + n] = got.reshape(2, cap, n)

    def group_store(dst, zz):
        return pltpu.make_async_copy(stage, dst.at[:, pl.ds(zz * 2, 2)], st_sem)

    def combine(i, with_dots):
        column = lax.broadcasted_iota(jnp.int32, (cap, wpad - width), 1)

        @pl.loop(0, nb)
        def _(b):
            j, c = b // 2, b % 2
            pick = pmat_t[i, b, :, : 2 * cap]
            for lo, n in strips(width, 768):
                both = res[b, :, :, lo : lo + n].reshape(2 * cap, n)
                stage[j, c, :, lo : lo + n] = nn(pick, both).astype(BF)
            if with_dots:
                at = pl.ds(pl.multiple_of(b * cap, 16), cap)
                own_dots = jnp.concatenate(
                    [
                        jnp.where(column == ep * 2 + k, dots[k, at, :], 0.0).astype(BF)
                        for k in range(2)
                    ],
                    axis=0,
                )
                stage[j, c, :, width:] = nn(pick, own_dots).astype(BF)
            else:
                stage[j, c, :, width:] = jnp.zeros((card_rows, wpad - width), BF)

    next_load(0)
    for copy in weights:
        copy.wait()

    @pl.loop(0, 4)
    def _(i):
        zz = line_order(z, i)
        gather.step2(i + 1)
        gather.step1(i + 2)
        gather.step0_if(i + 3, True)
        load(i).wait()
        spread(i, True)
        for k in range(2):
            save_rows(xs_hbm, k, i).start()

        @pl.loop(0, 2)
        def _(k):
            @pl.when(k == 1)
            def _():
                gather.step3(i + 1)

            x = rows_of(xs, k)
            gate_soft = CLAMP_LIMIT * jnp.tanh((nt(x, wg_ref[k]) + bg_ref[k]) * (1.0 / CLAMP_LIMIT))
            up_soft = CLAMP_LIMIT * jnp.tanh((nt(x, wu_ref[k]) + bu_ref[k]) * (1.0 / CLAMP_LIMIT))
            sig = jax.nn.sigmoid(SWIGLU_ALPHA * gate_soft)
            glu = gate_soft * sig
            mid[k] = ((up_soft + 1.0) * glu).astype(BF)
            cub[k] = (glu * (1.0 - (up_soft * (1.0 / CLAMP_LIMIT)) ** 2)).astype(BF)
            cgb[k] = (
                (up_soft + 1.0)
                * (sig + SWIGLU_ALPHA * glu * (1.0 - sig))
                * (1.0 - (gate_soft * (1.0 / CLAMP_LIMIT)) ** 2)
            ).astype(BF)
            save(mid, mid_hbm, k, i, 1).start()
            save(cub, cu_hbm, k, i, 2).start()
            save(cgb, cg_hbm, k, i, 3).start()
            for lo, n in strips(width, 768):
                part = nn(mid[k], wd_ref[k, :, lo : lo + n]) + first * bd_ref[k, :, lo : lo + n]
                res[:, k, :, lo : lo + n] = (part * gates[i, k]).astype(BF).reshape(nb, cap, n)

        gather.step0_if(i + 3, False)
        next_load(i + 1)

        @pl.when(i > 0)
        def _():
            group_store(out_hbm, line_order(z, i - 1)).wait()

        combine(i, False)
        group_store(out_hbm, zz).start()
        for k in range(2):
            save_rows(xs_hbm, k, i).wait()
            save(mid, mid_hbm, k, i, 1).wait()
            save(cub, cu_hbm, k, i, 2).wait()
            save(cgb, cg_hbm, k, i, 3).wait()

    group_store(out_hbm, line_order(z, 3)).wait()
    sum_g[...] = jnp.zeros_like(sum_g)
    sum_u[...] = jnp.zeros_like(sum_u)
    sum_d[...] = jnp.zeros_like(sum_d)

    @pl.loop(0, 4)
    def _(i):
        zz = line_order(z, i)
        for k in range(2):
            fetch(mid_hbm, mid, k, i, 1).start()
            fetch(cu_hbm, cub, k, i, 2).start()
            fetch(cg_hbm, cgb, k, i, 3).start()
        gather.step2(i + 5)
        gather.step1(i + 6)
        gather.step0_if(i + 7, True)
        load(i + 4).wait()
        spread(i, False)

        @pl.loop(0, 2)
        def _(k):
            @pl.when(k == 1)
            def _():
                gather.step3(i + 5)

            fetch(mid_hbm, mid, k, i, 1).wait()
            fetch(cu_hbm, cub, k, i, 2).wait()
            fetch(cg_hbm, cgb, k, i, 3).wait()
            g_rows = rows_of(xs, k)
            plain = nt(g_rows, wd_ref[k])
            gate = gates[i, k]
            grad = plain * gate
            g_rows = g_rows.astype(F32)
            dots[k] = jnp.sum(plain * mid[k].astype(F32), axis=1, keepdims=True) + first * jnp.sum(
                g_rows * bd_ref[k], axis=1, keepdims=True
            )
            up_grad = (grad * cub[k].astype(F32)).astype(BF)
            cub[k] = up_grad
            sum_u[k] += jnp.sum(up_grad.astype(F32), axis=0, keepdims=True)
            gate_grad = (grad * cgb[k].astype(F32)).astype(BF)
            cgb[k] = gate_grad
            sum_g[k] += jnp.sum(gate_grad.astype(F32), axis=0, keepdims=True)
            scaled = (g_rows * gate).astype(BF)
            xs[:, k] = scaled.reshape(nb, cap, width)
            sum_d[k] += jnp.sum(scaled.astype(F32), axis=0, keepdims=True)
            save_rows(eg_hbm, k, i).start()
            save(cub, ug_hbm, k, i, 4).start()
            save(cgb, gg_hbm, k, i, 5).start()
            for lo, n in strips(width, 768):
                part = nn(cgb[k], wg_ref[k, :, lo : lo + n]) + nn(cub[k], wu_ref[k, :, lo : lo + n])
                res[:, k, :, lo : lo + n] = part.astype(BF).reshape(nb, cap, n)

        gather.step0_if(i + 7, False)
        next_load(i + 5)

        @pl.when(i > 0)
        def _():
            group_store(row_hbm, line_order(z, i - 1)).wait()

        combine(i, True)
        group_store(row_hbm, zz).start()
        for k in range(2):
            save_rows(eg_hbm, k, i).wait()
            save(cub, ug_hbm, k, i, 4).wait()
            save(cgb, gg_hbm, k, i, 5).wait()

    group_store(row_hbm, line_order(z, 3)).wait()
    gather.finish()


def experts(n_own, g_own, wg_t, b_gate, wu_t, b_up, w_down, b_down, cap, cid):
    rows, wpad = n_own.shape
    ff, width = w_down.shape[1:]
    n, m = 32 * cap, 8 * cap
    free = pl.BlockSpec(memory_space=pl.ANY)
    near = pl.BlockSpec(memory_space=pltpu.VMEM)
    shape = jax.ShapeDtypeStruct
    V = pltpu.VMEM
    D = pltpu.SemaphoreType.DMA
    biases = [b.astype(F32)[:, None] for b in (b_gate, b_up, b_down)]
    out = pl.pallas_call(
        partial(experts_kernel, cap, width),
        out_shape=[shape((2, 4, 8, rows, wpad), BF)]
        + [shape((4, 8, rows, wpad), BF)] * 2
        + [shape((2, 4, 8, cap, width), BF)] * 2
        + [shape((2, 4, m, ff), BF)] * 5
        + [shape((2, 1, ff), F32)] * 2
        + [shape((2, 1, width), F32)],
        in_specs=[near] * 2 + [free] * 3 + [near] * 3,
        out_specs=[free] * 10 + [near] * 3,
        scratch_shapes=[
            V((2, ff, width), BF), V((2, ff, width), BF), V((2, ff, width), BF),
            V((4, 2, rows, wpad), BF), V((128, rows), F32),
            V((4, 8, 2 * cap, rows), BF), V((4, 8, rows, rows), BF), V((4, 2, m, 1), F32),
            V((8, 2, cap, width), BF), V((8, 2, cap, width), BF),
            V((2, m, ff), BF), V((2, m, ff), BF), V((2, m, ff), BF),
            V((2, m, 1), F32), V((4, 2, rows, wpad), BF),
            D((3,)), D((2,)), D, D, D((6, 2)),
            D((2, 4, 2)), D((2, 4)), D((2, 4, 4)), D((2, 4, 4)), D((2, 4, 2)), D((2, 4, 2)), D((2, 4)), D((2, 4)),
        ],
        compiler_params=pltpu.CompilerParams(
            collective_id=cid, has_side_effects=True, vmem_limit_bytes=63 * 1024 * 1024
        ),
        cost_estimate=pl.CostEstimate(
            flops=24 * n * width * ff, bytes_accessed=300_000_000, transcendentals=6 * n * ff
        ),
        name="experts",
    )(n_own, g_own, wg_t, wu_t, w_down, *biases)
    saved = [v.reshape(2, n, -1) for v in out[3:8]]
    return (*out[1:3], *saved, *(total[:, 0] for total in out[10:]))


def project_sum_kernel(parts, m_ref, w_ref, out_ref, p_ref, q, v1, v2, s1, r1, s2, r2):
    fs, ep, y, x, z, c = spot()
    rows = p_ref.shape[1]
    step = rows // (2 * parts)
    xn, yn = (fs + 1 - 2 * x, ep), (fs + 2 - 4 * y, ep)

    def rem(src, dst, s, r, dev):
        return pltpu.make_async_remote_copy(src, dst, s, r, device_id=dev, device_id_type=MESH)

    def band(n, half):
        return pl.ds((2 * n + half) * step, step)

    def one(n):
        a, b = band(n, 0), band(n, 1)
        out = [
            (rem(p_ref.at[2 * j + 1 - x, a], v1.at[n, 0, j], s1.at[n, 0, j], r1.at[n, 0, j], xn))
            for j in range(2)
        ]
        return out + [
            rem(p_ref.at[2 * (1 - y) + j, b], v1.at[n, 1, j], s1.at[n, 1, j], r1.at[n, 1, j], yn)
            for j in range(2)
        ]

    def two(n):
        return (
            rem(q.at[n, 0], v2.at[n, 0], s2.at[n, 0], r2.at[n, 0], yn),
            rem(q.at[n, 1], v2.at[n, 1], s2.at[n, 1], r2.at[n, 1], xn),
        )

    def project(dev):
        m = m_ref[dev]
        for lo, n in strips(w_ref.shape[0], 768):
            p_ref[dev, :, lo : lo + n] = nt(m, w_ref[lo : lo + n, :]).astype(BF)

    def send(dx, dy):
        for n in range(parts):
            copies = one(n)
            for j in range(2):
                if dx:

                    @pl.when(y == (j + dy) % 2)
                    def _():
                        copies[j].start()

                if dy:

                    @pl.when(x == (j + dx) % 2)
                    def _():
                        copies[2 + j].start()

    project(3 - fs)
    greet(fs, ep, z)
    send(1, 1)
    project(2 * y + 1 - x)
    send(1, 0)
    project(2 * (1 - y) + x)
    send(0, 1)
    project(fs)
    for n in range(parts):
        a, b = band(n, 0), band(n, 1)
        copies = one(n)
        for copy in copies[:2]:
            copy.wait_recv()
        q[n, 0] = p_ref[2 * (1 - y) + x, a] + v1[n, 0, 1 - y]
        two(n)[0].start()
        for copy in copies[2:]:
            copy.wait_recv()
        q[n, 1] = p_ref[2 * y + 1 - x, b] + v1[n, 1, 1 - x]
        two(n)[1].start()
        out_ref[a, :] = p_ref[fs, a].astype(F32) + v1[n, 0, y].astype(F32)
        out_ref[b, :] = p_ref[fs, b].astype(F32) + v1[n, 1, x].astype(F32)
    for n in range(parts):
        for half in range(2):
            at = band(n, half)
            two(n)[half].wait_recv()
            out_ref[at, :] += v2[n, half].astype(F32)
    for n in range(parts):
        for copy in (*one(n), *two(n)):
            copy.wait_send()


def project_sum(mixed, w_t, cid, parts=2):
    _, rows, features = mixed.shape
    width = w_t.shape[0]
    near = pl.BlockSpec(memory_space=pltpu.VMEM)
    D = pltpu.SemaphoreType.DMA
    step = rows // (2 * parts)
    V = pltpu.VMEM
    return pl.pallas_call(
        partial(project_sum_kernel, parts),
        out_shape=jax.ShapeDtypeStruct((rows, width), F32),
        in_specs=[near, near],
        out_specs=near,
        scratch_shapes=[
            V((4, rows, width), BF), V((parts, 2, step, width), BF),
            V((parts, 2, 2, step, width), BF), V((parts, 2, step, width), BF),
            D((parts, 2, 2)), D((parts, 2, 2)), D((parts, 2)), D((parts, 2)),
        ],
        compiler_params=pltpu.CompilerParams(
            collective_id=cid, has_side_effects=True, vmem_limit_bytes=40 * 1024 * 1024
        ),
        cost_estimate=pl.CostEstimate(
            flops=8 * rows * features * width, bytes_accessed=20_000_000, transcendentals=0
        ),
        name="project_sum",
    )(mixed, w_t)


def weight_grads_kernel(xs, eg, mid, ug, gg, down, gate, up, rows, left, out, r_sem, l_sem, o_sem):
    width = xs.shape[2]
    jobs = [(k, w) for k in range(2) for w in range(3)]
    lefts, outs = (mid, gg, ug), (down, gate, up)

    def load_rows(n):
        return pltpu.make_async_copy((eg, xs)[n % 2].at[n // 2], rows.at[n % 2], r_sem.at[n % 2])

    def load_left(j):
        k, w = jobs[j]
        return pltpu.make_async_copy(lefts[w].at[k], left.at[j % 2], l_sem.at[j % 2])

    def store(j):
        k, w = jobs[j]
        return pltpu.make_async_copy(out.at[j % 2], outs[w].at[k], o_sem.at[j % 2])

    load_rows(0).start()
    load_left(0).start()
    load_rows(1).start()
    for j, (k, w) in enumerate(jobs):
        if j + 1 < len(jobs):
            load_left(j + 1).start()
        load_left(j).wait()
        if w < 2:
            load_rows(2 * k + w).wait()
        if j >= 2:
            store(j - 2).wait()
        right = rows.at[min(w, 1)]
        for lo, n in strips(width, 768):
            out[j % 2, :, lo : lo + n] = tn(left[j % 2], right[:, lo : lo + n])
        store(j).start()
        if k == 0 and w in (0, 2):
            load_rows(2 + (w > 0)).start()
    for j in (len(jobs) - 2, len(jobs) - 1):
        store(j).wait()


def weight_grads(xs, eg, mid, ug, gg):
    _, n, width = xs.shape
    ff = mid.shape[2]
    free = pl.BlockSpec(memory_space=pl.ANY)
    D = pltpu.SemaphoreType.DMA
    return pl.pallas_call(
        weight_grads_kernel,
        out_shape=[jax.ShapeDtypeStruct((2, ff, width), F32)] * 3,
        in_specs=[free] * 5,
        out_specs=[free] * 3,
        scratch_shapes=[
            pltpu.VMEM((2, n, width), BF), pltpu.VMEM((2, n, ff), BF), pltpu.VMEM((2, ff, width), F32),
            D((2,)), D((2,)), D((2,)),
        ],
        compiler_params=pltpu.CompilerParams(vmem_limit_bytes=60 * 1024 * 1024),
        cost_estimate=pl.CostEstimate(
            flops=12 * n * ff * width, bytes_accessed=100_000_000, transcendentals=0
        ),
        name="weight_grads",
    )(xs, eg, mid, ug, gg)


def this_slice(
    tokens,
    seq_lengths,
    routes,
    attn_gain,
    w_query,
    b_query,
    w_key,
    b_key,
    w_value,
    b_value,
    sinks,
    w_out,
    b_out,
    ffn_gain,
    w_router,
    b_router,
    w_gate,
    b_gate,
    w_up,
    b_up,
    w_down,
    b_down,
    cotangent,
):
    rows, width = tokens.shape
    fs_size = lax.axis_size("fs")
    ep_size = lax.axis_size("ep")
    my_fs = lax.axis_index("fs")
    my_ep = lax.axis_index("ep")
    blocks = fs_size * ep_size
    expert_count = EXP_DEV * ep_size
    capacity = 3 * rows * TOP // (2 * expert_count)
    shard = w_query.shape[0]
    kv_heads = KEY_VALUE_HEADS // fs_size
    group = QUERY_HEADS // KEY_VALUE_HEADS
    q_cols = kv_heads * group * HEAD_SIZE
    kv_cols = kv_heads * HEAD_SIZE

    spare = (-width) % 128
    small = jnp.concatenate(
        [attn_gain, ffn_gain, b_out, w_router.reshape(-1), b_router, seq_lengths[0].astype(BF)]
    )
    extra = -(-small.shape[0] // (16 * width)) * 16
    small = jnp.pad(small, (0, extra * width - small.shape[0])).reshape(extra, width)
    x_group, small, w_qkv = start_exchange(tokens, small, w_query, w_key, w_value, 4)
    x_group = x_group.reshape(fs_size * rows, width).astype(F32)
    small = small.reshape(fs_size, -1)
    gain_one = small[:, :shard].reshape(-1).astype(F32)
    gain_two = small[:, shard : 2 * shard].reshape(-1).astype(F32)
    bo = small[:, 2 * shard : 3 * shard].reshape(-1).astype(F32)
    at = (3 + expert_count) * shard
    wr = small[:, 3 * shard : at].reshape(width, expert_count)
    br = small[:, at : at + b_router.shape[0]].reshape(-1).astype(F32)
    at += b_router.shape[0]
    lengths = small[:, at : at + seq_lengths.shape[1]].astype(jnp.int32)

    w_qkv = w_qkv.reshape(width, q_cols + 2 * kv_cols)
    b_qkv = jnp.concatenate([b_query, b_key, b_value]).astype(jnp.float32)
    sink_score = sinks.astype(jnp.float32).reshape(1, kv_heads, group, 1)

    x_float = tokens.astype(jnp.float32)
    scale_one = norm_scale(x_float)
    scale_group = norm_scale(x_group)
    norm_attn = (x_group * scale_group * gain_one).astype(jnp.bfloat16)
    segment_ids, position = jax.vmap(lambda own: layout(own, rows))(lengths)
    cosine_table, sine_table = tables(position.reshape(-1), HEAD_SIZE // 2)
    qkv = jnp.dot(norm_attn, w_qkv, preferred_element_type=jnp.float32) + b_qkv
    many = fs_size * rows
    heads = kv_heads * group
    query = apply_rotation(
        qkv[:, :q_cols].reshape(many, heads, HEAD_SIZE), cosine_table, sine_table
    ).astype(jnp.bfloat16)
    query = query.reshape(fs_size, rows, kv_heads, group, HEAD_SIZE)
    key = apply_rotation(
        qkv[:, q_cols : q_cols + kv_cols].reshape(many, kv_heads, HEAD_SIZE),
        cosine_table,
        sine_table,
    ).astype(jnp.bfloat16)
    key = key.reshape(fs_size, rows, kv_heads, HEAD_SIZE)
    value = qkv[:, q_cols + kv_cols :].astype(jnp.bfloat16)
    value = value.reshape(fs_size, rows, kv_heads, HEAD_SIZE)
    places = jnp.arange(rows, dtype=jnp.int32)
    allowed = (segment_ids[:, :, None] == segment_ids[:, None, :]) & (
        places[:, None] >= places[None, :]
    )
    scores = mm("bqhgd,bkhd->bhgqk", query, key) * HEAD_SIZE ** (-0.5)
    masked = jnp.where(allowed[:, None, None], scores, MASKED_SCORE)
    top_score = jnp.maximum(jnp.max(masked, axis=-1), sink_score)
    exponent = jnp.exp(masked - top_score[..., None])
    sink_exp = jnp.exp(sink_score - top_score)
    denominator = jnp.sum(exponent, axis=-1) + sink_exp
    probs = exponent / denominator[..., None]
    sink_prob = sink_exp / denominator
    probs_b = probs.astype(jnp.bfloat16)
    mixed = mm("bhgqk,bkhd->bqhgd", probs_b, value).astype(jnp.bfloat16)
    mixed = mixed.reshape(many, q_cols)
    projected = project_sum(
        mixed.reshape(fs_size, rows, q_cols), jnp.swapaxes(w_out, 0, 1), 5
    )
    resid = x_float + projected + bo
    scale_two = norm_scale(resid)
    norm_ffn = (resid * scale_two * gain_two).astype(jnp.bfloat16)

    logits = jnp.dot(norm_ffn, wr, preferred_element_type=F32) + br
    one_hot = (routes[:, :, None] == jnp.arange(expert_count, dtype=jnp.int32)).astype(F32)
    member = jnp.sum(one_hot, axis=1)
    peak = jnp.max(jnp.where(member > 0, logits, MASKED_SCORE), axis=-1, keepdims=True)
    gate_exp = jnp.where(member > 0, jnp.exp(logits - peak), 0.0)
    gates_here = gate_exp / jnp.sum(gate_exp, axis=-1, keepdims=True)
    place = jnp.where(member > 0, jnp.cumsum(member, axis=0) - member, -1.0)
    gate_high = lax.reduce_precision(gates_here, 8, 7)
    block = jnp.concatenate(
        [norm_ffn]
        + [v.astype(BF) for v in (place, gate_high, gates_here - gate_high)]
        + [jnp.zeros((rows, spare - 3 * expert_count), BF)],
        axis=1,
    )
    wg_t = jnp.swapaxes(w_gate, 1, 2)
    wu_t = jnp.swapaxes(w_up, 1, 2)
    (
        out_part,
        row_part,
        x_slots,
        expert_grad,
        middle,
        up_grad,
        gate_grad_pre,
        grad_b_gate,
        grad_b_up,
        grad_b_down,
    ) = experts(
        block,
        jnp.pad(cotangent, ((0, 0), (0, spare))),
        wg_t,
        b_gate,
        wu_t,
        b_up,
        w_down,
        b_down,
        capacity,
        1,
    )
    sums = scatter_blocks([out_part, row_part], 2)
    block_out = resid + sums[0, :, :width].astype(F32)
    grad_w_down, gate_t, up_t = weight_grads(
        x_slots, expert_grad, middle, up_grad, gate_grad_pre
    )
    grad_w_gate = jnp.swapaxes(gate_t, 1, 2)
    grad_w_up = jnp.swapaxes(up_t, 1, 2)
    row_sum = sums[1].astype(F32)
    gate_grad = row_sum[:, width : width + expert_count]
    logit_grad = gates_here * (
        gate_grad - jnp.sum(gates_here * gate_grad, axis=-1, keepdims=True)
    )
    logit_grad = logit_grad.astype(jnp.bfloat16)
    grad_br = jnp.sum(logit_grad, axis=0, dtype=jnp.float32)
    grad_wr = left_dot(norm_ffn, logit_grad)
    norm_ffn_grad = row_sum[:, :width] + jnp.dot(
        logit_grad, wr.T, preferred_element_type=jnp.float32
    )
    resid_norm_grad, grad_gain_two = norm_back(resid, scale_two, gain_two, norm_ffn_grad)
    resid_grad = cotangent.astype(jnp.float32) + resid_norm_grad

    branch_grad = gather_fs(resid_grad.astype(jnp.bfloat16))
    grad_bo = jnp.sum(branch_grad, axis=0, dtype=jnp.float32)
    mixed_grad = mm("td,fd->tf", branch_grad, w_out).astype(jnp.bfloat16)
    mixed_grad = mixed_grad.reshape(fs_size, rows, kv_heads, group, HEAD_SIZE)
    grad_probs = mm("bqhgd,bkhd->bhgqk", mixed_grad, value)
    value_grad = mm("bhgqk,bqhgd->bkhd", probs_b, mixed_grad)
    row_delta = jnp.sum(probs * grad_probs, axis=-1)
    score_grad = (probs * (grad_probs - row_delta[..., None])).astype(jnp.bfloat16)
    query_grad = mm("bhgqk,bkhd->bqhgd", score_grad, key) * HEAD_SIZE ** (-0.5)
    key_grad = mm("bhgqk,bqhgd->bkhd", score_grad, query) * HEAD_SIZE ** (-0.5)
    grad_sink = -jnp.sum(sink_prob * row_delta, axis=(0, 3)).reshape(-1)
    query_pre_grad = undo_rotation(
        query_grad.reshape(many, heads, HEAD_SIZE), cosine_table, sine_table
    ).reshape(many, q_cols)
    key_pre_grad = undo_rotation(
        key_grad.reshape(many, kv_heads, HEAD_SIZE), cosine_table, sine_table
    ).reshape(many, kv_cols)
    qkv_grad = jnp.concatenate(
        [query_pre_grad, key_pre_grad, value_grad.reshape(many, kv_cols)], axis=1
    ).astype(jnp.bfloat16)
    grad_b_qkv = jnp.sum(qkv_grad, axis=0, dtype=jnp.float32)
    part = mm("tf,df->td", qkv_grad, w_qkv)
    grad_gain_one = jnp.sum(part * (x_group * scale_group), axis=0)
    norm_attn_grad = scatter_fs(part.astype(BF)).astype(F32)
    input_norm_grad, _ = norm_back(x_float, scale_one, gain_one, norm_attn_grad)
    grad_tokens = resid_grad + input_norm_grad
    by_shard = jnp.concatenate(
        [
            grad_wr.reshape(fs_size, -1),
            grad_gain_one.reshape(fs_size, -1),
            grad_gain_two.reshape(fs_size, -1),
            grad_br.reshape(fs_size, -1),
        ],
        axis=1,
    ).astype(BF)
    own = jnp.concatenate(
        [grad_b_qkv, grad_sink, lax.dynamic_slice_in_dim(grad_bo, my_fs * shard, shard)]
    ).astype(BF)
    cols = q_cols + 2 * kv_cols
    slab_rows = 768
    wide_part = 144
    own = jnp.where(jnp.arange(fs_size)[:, None] == my_fs, own, jnp.zeros((), BF))
    by_shard = jnp.concatenate([by_shard, own], axis=1)
    small_n = by_shard.shape[1]
    small_rows = -(-small_n // q_cols)
    by_shard = jnp.pad(by_shard, ((0, 0), (0, small_rows * q_cols - small_n)))
    by_shard = jnp.pad(
        by_shard.reshape(fs_size, small_rows, q_cols),
        ((0, 0), (0, slab_rows - shard - small_rows), (0, cols - q_cols)),
    )
    gq = left_dot(norm_attn, qkv_grad).astype(BF).reshape(fs_size, shard, cols)
    gw = left_dot(branch_grad, mixed).astype(BF)
    gw = gw.reshape(2, width // (2 * wide_part), wide_part, q_cols)
    tw, tq, tk, tv = reduce_parts(gw, gq, by_shard, 3, (q_cols, kv_cols, kv_cols), 3)
    sum_wo = jnp.swapaxes(tw.reshape(width, q_cols).astype(F32), 0, 1)
    sum_wq = tq[:shard].astype(F32)
    sum_wk = tk[:shard].astype(F32)
    sum_wv = tv[:shard].astype(F32)
    by_shard = jnp.sum(
        tq[shard : shard + small_rows].astype(F32).reshape(small_rows, fs_size, q_cols), axis=1
    ).reshape(-1)
    sum_wr = by_shard[: shard * expert_count].reshape(shard, expert_count)
    rest = by_shard[shard * expert_count : small_n - own.shape[1]]
    own = by_shard[small_n - own.shape[1] : small_n]
    sum_b = own[:cols]
    return (
        block_out.astype(jnp.bfloat16),
        grad_tokens,
        rest[:shard],
        sum_wq,
        sum_b[:q_cols],
        sum_wk,
        sum_b[q_cols : q_cols + kv_cols],
        sum_wv,
        sum_b[q_cols + kv_cols :],
        own[q_cols + 2 * kv_cols : q_cols + 2 * kv_cols + heads],
        sum_wo,
        own[q_cols + 2 * kv_cols + heads :],
        rest[shard : 2 * shard],
        sum_wr,
        rest[2 * shard :],
        grad_w_gate,
        grad_b_gate,
        grad_w_up,
        grad_b_up,
        grad_w_down,
        grad_b_down,
    )


def any_slice(
    tokens,
    seq_lengths,
    routes,
    attn_gain,
    w_query,
    b_query,
    w_key,
    b_key,
    w_value,
    b_value,
    sinks,
    w_out,
    b_out,
    ffn_gain,
    w_router,
    b_router,
    w_gate,
    b_gate,
    w_up,
    b_up,
    w_down,
    b_down,
    cotangent,
):
    rows, width = tokens.shape
    fs_size = lax.axis_size("fs")
    ep_size = lax.axis_size("ep")
    my_fs = lax.axis_index("fs")
    my_ep = lax.axis_index("ep")
    blocks = fs_size * ep_size
    expert_count = EXP_DEV * ep_size
    capacity = 3 * rows * TOP // (2 * expert_count)
    shard = w_query.shape[0]
    kv_heads = KEY_VALUE_HEADS // fs_size
    group = QUERY_HEADS // KEY_VALUE_HEADS
    q_cols = kv_heads * group * HEAD_SIZE
    kv_cols = kv_heads * HEAD_SIZE

    packed = jnp.concatenate(
        [attn_gain, ffn_gain, b_out, w_router.reshape(-1), b_router]
    )
    packed = lax.all_gather(packed, "fs", axis=0)
    gain_one = packed[:, :shard].reshape(-1).astype(jnp.float32)
    gain_two = packed[:, shard : 2 * shard].reshape(-1).astype(jnp.float32)
    bo = packed[:, 2 * shard : 3 * shard].reshape(-1).astype(jnp.float32)
    wr = packed[:, 3 * shard : (3 + expert_count) * shard].reshape(width, expert_count)
    br = packed[:, (3 + expert_count) * shard :].reshape(-1).astype(jnp.float32)
    whole_numbers = gather_all(
        jnp.concatenate([routes.reshape(-1), seq_lengths.reshape(-1)])[None]
    )
    routes_all = whole_numbers[:, : rows * TOP].reshape(blocks, rows, TOP)
    lengths_all = whole_numbers[:, rows * TOP :]
    lengths = lax.dynamic_index_in_dim(
        lengths_all.reshape(fs_size, ep_size, -1), my_ep, 1, keepdims=False
    )
    g_all = gather_all(cotangent)

    w_qkv = jnp.concatenate(
        [
            w_query.reshape(shard, fs_size, q_cols),
            w_key.reshape(shard, fs_size, kv_cols),
            w_value.reshape(shard, fs_size, kv_cols),
        ],
        axis=2,
    )
    w_qkv = lax.all_to_all(w_qkv, "fs", split_axis=1, concat_axis=0, tiled=True)
    w_qkv = w_qkv.reshape(width, q_cols + 2 * kv_cols)
    b_qkv = jnp.concatenate([b_query, b_key, b_value]).astype(jnp.float32)
    sink_score = sinks.astype(jnp.float32).reshape(1, kv_heads, group, 1)

    x_float = tokens.astype(jnp.float32)
    scale_one = norm_scale(x_float)
    norm_attn = gather_fs((x_float * scale_one * gain_one).astype(jnp.bfloat16))
    segment_ids, position = jax.vmap(lambda own: layout(own, rows))(lengths)
    cosine_table, sine_table = tables(position.reshape(-1), HEAD_SIZE // 2)
    qkv = jnp.dot(norm_attn, w_qkv, preferred_element_type=jnp.float32) + b_qkv
    many = fs_size * rows
    heads = kv_heads * group
    query = apply_rotation(
        qkv[:, :q_cols].reshape(many, heads, HEAD_SIZE), cosine_table, sine_table
    ).astype(jnp.bfloat16)
    query = query.reshape(fs_size, rows, kv_heads, group, HEAD_SIZE)
    key = apply_rotation(
        qkv[:, q_cols : q_cols + kv_cols].reshape(many, kv_heads, HEAD_SIZE),
        cosine_table,
        sine_table,
    ).astype(jnp.bfloat16)
    key = key.reshape(fs_size, rows, kv_heads, HEAD_SIZE)
    value = qkv[:, q_cols + kv_cols :].astype(jnp.bfloat16)
    value = value.reshape(fs_size, rows, kv_heads, HEAD_SIZE)
    places = jnp.arange(rows, dtype=jnp.int32)
    allowed = (segment_ids[:, :, None] == segment_ids[:, None, :]) & (
        places[:, None] >= places[None, :]
    )
    scores = mm("bqhgd,bkhd->bhgqk", query, key) * HEAD_SIZE ** (-0.5)
    masked = jnp.where(allowed[:, None, None], scores, MASKED_SCORE)
    top_score = jnp.maximum(jnp.max(masked, axis=-1), sink_score)
    exponent = jnp.exp(masked - top_score[..., None])
    sink_exp = jnp.exp(sink_score - top_score)
    denominator = jnp.sum(exponent, axis=-1) + sink_exp
    probs = exponent / denominator[..., None]
    sink_prob = sink_exp / denominator
    probs_b = probs.astype(jnp.bfloat16)
    mixed = mm("bhgqk,bkhd->bqhgd", probs_b, value).astype(jnp.bfloat16)
    mixed = mixed.reshape(many, q_cols)
    out_part = jnp.dot(mixed, w_out, preferred_element_type=jnp.float32)
    resid = x_float + scatter_fs(out_part.astype(jnp.bfloat16)).astype(jnp.float32) + bo
    scale_two = norm_scale(resid)
    norm_ffn = (resid * scale_two * gain_two).astype(jnp.bfloat16)

    n_all = gather_all(norm_ffn)
    logits = jnp.dot(n_all, wr, preferred_element_type=jnp.float32) + br
    logits = logits.reshape(blocks, rows, expert_count)
    one_hot = (
        routes_all[:, :, :, None] == jnp.arange(expert_count, dtype=jnp.int32)
    ).astype(jnp.float32)
    member = jnp.sum(one_hot, axis=2)
    peak = jnp.max(jnp.where(member > 0, logits, MASKED_SCORE), axis=-1, keepdims=True)
    gate_exp = jnp.where(member > 0, jnp.exp(logits - peak), 0.0)
    gates = gate_exp / jnp.sum(gate_exp, axis=-1, keepdims=True)
    own_member = lax.dynamic_slice_in_dim(member, my_ep * EXP_DEV, EXP_DEV, axis=2)
    own_gates = lax.dynamic_slice_in_dim(gates, my_ep * EXP_DEV, EXP_DEV, axis=2)
    rank = jnp.cumsum(own_member, axis=1) - own_member
    slots = jnp.arange(capacity, dtype=jnp.float32)
    pick = (rank.transpose(0, 2, 1)[:, :, None, :] == slots[:, None]) & (
        own_member.transpose(0, 2, 1)[:, :, None, :] > 0
    )
    pick_b = pick.astype(jnp.bfloat16)
    slot_gate = jnp.sum(
        jnp.where(pick, own_gates.transpose(0, 2, 1)[:, :, None, :], 0.0), axis=-1
    )
    slot_gate = slot_gate.transpose(1, 0, 2).reshape(EXP_DEV, blocks * capacity, 1)

    def spread(full):
        parts = mm("bekt,btd->ebkd", pick_b, full.reshape(blocks, rows, -1))
        return parts.astype(jnp.bfloat16).reshape(EXP_DEV, blocks * capacity, -1)

    def combine(parts):
        parts = parts.reshape(EXP_DEV, blocks, capacity, -1)
        return mm("bekt,ebkd->btd", pick_b, parts).reshape(blocks * rows, -1)

    x_slots = spread(n_all)
    g_slots = spread(g_all)
    gate_pre = mm("erd,edf->erf", x_slots, w_gate) + b_gate.astype(jnp.float32)[:, None]
    up_pre = mm("erd,edf->erf", x_slots, w_up) + b_up.astype(jnp.float32)[:, None]
    gate_soft = CLAMP_LIMIT * jnp.tanh(gate_pre / CLAMP_LIMIT)
    up_soft = CLAMP_LIMIT * jnp.tanh(up_pre / CLAMP_LIMIT)
    gate_sig = jax.nn.sigmoid(SWIGLU_ALPHA * gate_soft)
    glu_part = gate_soft * gate_sig
    middle = ((up_soft + 1.0) * glu_part).astype(jnp.bfloat16)
    first = (my_fs == 0).astype(jnp.float32)
    down_bias = b_down.astype(jnp.float32) * first
    expert_out = mm("erf,efd->erd", middle, w_down) + down_bias[:, None]
    expert_sum = scatter_all(
        combine((expert_out * slot_gate).astype(jnp.bfloat16)).astype(jnp.bfloat16)
    )
    block_out = resid + expert_sum.astype(jnp.float32)

    expert_grad = (g_slots.astype(jnp.float32) * slot_gate).astype(jnp.bfloat16)
    plain_grad = mm("erd,efd->erf", g_slots, w_down)
    middle_grad = plain_grad * slot_gate
    gate_dot = jnp.sum(plain_grad * middle.astype(jnp.float32), axis=-1) + jnp.sum(
        g_slots.astype(jnp.float32) * down_bias[:, None], axis=-1
    )
    grad_w_down = mm("erf,erd->efd", middle, expert_grad)
    grad_b_down = jnp.sum(expert_grad, axis=1, dtype=jnp.float32)
    up_grad = (middle_grad * glu_part * (1.0 - (up_soft / CLAMP_LIMIT) ** 2)).astype(jnp.bfloat16)
    gate_grad_pre = (
        middle_grad
        * (up_soft + 1.0)
        * (gate_sig + SWIGLU_ALPHA * gate_soft * gate_sig * (1.0 - gate_sig))
        * (1.0 - (gate_soft / CLAMP_LIMIT) ** 2)
    ).astype(jnp.bfloat16)
    grad_w_gate = mm("erd,erf->edf", x_slots, gate_grad_pre)
    grad_b_gate = jnp.sum(gate_grad_pre, axis=1, dtype=jnp.float32)
    grad_w_up = mm("erd,erf->edf", x_slots, up_grad)
    grad_b_up = jnp.sum(up_grad, axis=1, dtype=jnp.float32)
    row_part = mm("erf,edf->erd", gate_grad_pre, w_gate) + mm("erf,edf->erd", up_grad, w_up)
    row_sum = combine(row_part.astype(jnp.bfloat16))
    own_dot = jnp.sum(
        jnp.where(pick, gate_dot.reshape(EXP_DEV, blocks, capacity).transpose(1, 0, 2)[..., None], 0.0),
        axis=2,
    )
    dots = jnp.sum(
        own_dot[..., None]
        * (
            (my_ep * EXP_DEV + jnp.arange(EXP_DEV))[:, None] == jnp.arange(expert_count)[None]
        ).astype(jnp.float32)[None, :, None, :],
        axis=1,
    ).reshape(blocks * rows, expert_count)
    row_sum = scatter_all(jnp.concatenate([row_sum, dots], axis=1).astype(jnp.bfloat16))
    row_sum = row_sum.astype(jnp.float32)
    gate_grad = row_sum[:, width:]
    mine = my_fs * ep_size + my_ep
    gates_here = lax.dynamic_index_in_dim(gates, mine, 0, keepdims=False)
    logit_grad = gates_here * (
        gate_grad - jnp.sum(gates_here * gate_grad, axis=-1, keepdims=True)
    )
    logit_grad = logit_grad.astype(jnp.bfloat16)
    grad_br = jnp.sum(logit_grad, axis=0, dtype=jnp.float32)
    grad_wr = left_dot(norm_ffn, logit_grad)
    norm_ffn_grad = row_sum[:, :width] + jnp.dot(
        logit_grad, wr.T, preferred_element_type=jnp.float32
    )
    resid_norm_grad, grad_gain_two = norm_back(resid, scale_two, gain_two, norm_ffn_grad)
    resid_grad = cotangent.astype(jnp.float32) + resid_norm_grad

    branch_grad = gather_fs(resid_grad.astype(jnp.bfloat16))
    grad_bo = jnp.sum(branch_grad, axis=0, dtype=jnp.float32)
    mixed_grad = mm("td,fd->tf", branch_grad, w_out).astype(jnp.bfloat16)
    mixed_grad = mixed_grad.reshape(fs_size, rows, kv_heads, group, HEAD_SIZE)
    grad_wo = left_dot(mixed, branch_grad)
    grad_probs = mm("bqhgd,bkhd->bhgqk", mixed_grad, value)
    value_grad = mm("bhgqk,bqhgd->bkhd", probs_b, mixed_grad)
    row_delta = jnp.sum(probs * grad_probs, axis=-1)
    score_grad = (probs * (grad_probs - row_delta[..., None])).astype(jnp.bfloat16)
    query_grad = mm("bhgqk,bkhd->bqhgd", score_grad, key) * HEAD_SIZE ** (-0.5)
    key_grad = mm("bhgqk,bqhgd->bkhd", score_grad, query) * HEAD_SIZE ** (-0.5)
    grad_sink = -jnp.sum(sink_prob * row_delta, axis=(0, 3)).reshape(-1)
    query_pre_grad = undo_rotation(
        query_grad.reshape(many, heads, HEAD_SIZE), cosine_table, sine_table
    ).reshape(many, q_cols)
    key_pre_grad = undo_rotation(
        key_grad.reshape(many, kv_heads, HEAD_SIZE), cosine_table, sine_table
    ).reshape(many, kv_cols)
    qkv_grad = jnp.concatenate(
        [query_pre_grad, key_pre_grad, value_grad.reshape(many, kv_cols)], axis=1
    ).astype(jnp.bfloat16)
    grad_b_qkv = jnp.sum(qkv_grad, axis=0, dtype=jnp.float32)
    norm_attn_grad = scatter_fs(
        mm("tf,df->td", qkv_grad, w_qkv).astype(jnp.bfloat16)
    ).astype(jnp.float32)
    input_norm_grad, grad_gain_one = norm_back(x_float, scale_one, gain_one, norm_attn_grad)
    grad_tokens = resid_grad + input_norm_grad
    grad_qkv = left_dot(norm_attn, qkv_grad).astype(jnp.bfloat16)
    if shard % ep_size == 0:
        grad_qkv = grad_qkv.reshape(fs_size, ep_size, shard // ep_size, q_cols + 2 * kv_cols)
        grad_qkv = lax.psum_scatter(grad_qkv, "ep", scatter_dimension=1, tiled=False)
        grad_qkv = lax.all_to_all(grad_qkv, "fs", split_axis=0, concat_axis=1, tiled=False)
        grad_qkv = lax.all_gather(grad_qkv, "ep", axis=0, tiled=True).astype(jnp.float32)
    else:
        grad_qkv = lax.psum(grad_qkv.reshape(fs_size, shard, q_cols + 2 * kv_cols), "ep")
        grad_qkv = lax.all_to_all(grad_qkv, "fs", split_axis=0, concat_axis=1, tiled=False)
        grad_qkv = grad_qkv.astype(jnp.float32)
    sum_wq = grad_qkv[:, :, :q_cols].reshape(shard, -1)
    sum_wk = grad_qkv[:, :, q_cols : q_cols + kv_cols].reshape(shard, -1)
    sum_wv = grad_qkv[:, :, q_cols + kv_cols :].reshape(shard, -1)
    sum_wo = lax.psum(grad_wo.astype(jnp.bfloat16), "ep").astype(jnp.float32)
    by_shard = jnp.concatenate(
        [
            grad_wr.reshape(fs_size, -1),
            grad_gain_one.reshape(fs_size, -1),
            grad_gain_two.reshape(fs_size, -1),
            grad_br.reshape(fs_size, -1),
        ],
        axis=1,
    )
    by_shard = lax.psum(by_shard, ("fs", "ep"))
    by_shard = lax.dynamic_index_in_dim(by_shard, my_fs, 0, keepdims=False)
    sum_wr = by_shard[: shard * expert_count].reshape(shard, expert_count)
    rest = by_shard[shard * expert_count :]
    own = jnp.concatenate(
        [
            grad_b_qkv,
            grad_sink,
            lax.dynamic_slice_in_dim(grad_bo, my_fs * shard, shard),
        ]
    )
    own = lax.psum(own, "ep")
    sum_b = own[: q_cols + 2 * kv_cols]
    return (
        block_out.astype(jnp.bfloat16),
        grad_tokens,
        rest[:shard],
        sum_wq,
        sum_b[:q_cols],
        sum_wk,
        sum_b[q_cols : q_cols + kv_cols],
        sum_wv,
        sum_b[q_cols + kv_cols :],
        own[q_cols + 2 * kv_cols : q_cols + 2 * kv_cols + heads],
        sum_wo,
        own[q_cols + 2 * kv_cols + heads :],
        rest[shard : 2 * shard],
        sum_wr,
        rest[2 * shard :],
        grad_w_gate,
        grad_b_gate,
        grad_w_up,
        grad_b_up,
        grad_w_down,
        grad_b_down,
    )


def solution(mesh):
    in_specs = (
        P(("fs", "ep"), None),
        P(("fs", "ep"), None),
        P(("fs", "ep"), None),
        P("fs"),
        P("fs", None),
        P("fs"),
        P("fs", None),
        P("fs"),
        P("fs", None),
        P("fs"),
        P("fs"),
        P("fs", None),
        P("fs"),
        P("fs"),
        P("fs", None),
        P("fs"),
        P("ep", None, "fs"),
        P("ep", "fs"),
        P("ep", None, "fs"),
        P("ep", "fs"),
        P("ep", "fs", None),
        P("ep", None),
        P(("fs", "ep"), None),
    )
    out_specs = (
        P(("fs", "ep"), None),
        P(("fs", "ep"), None),
        P("fs"),
        P("fs", None),
        P("fs"),
        P("fs", None),
        P("fs"),
        P("fs", None),
        P("fs"),
        P("fs"),
        P("fs", None),
        P("fs"),
        P("fs"),
        P("fs", None),
        P("fs"),
        P("ep", None, "fs"),
        P("ep", "fs"),
        P("ep", None, "fs"),
        P("ep", "fs"),
        P("ep", "fs", None),
        P("ep", None),
    )
    run = this_slice if (mesh.shape["fs"], mesh.shape["ep"]) == (4, 8) else any_slice
    return jax.shard_map(
        run, mesh=mesh, in_specs=in_specs, out_specs=out_specs, check_vma=False
    )
```

```python
from functools import partial

import jax
import jax.numpy as jnp
from jax import lax
from jax.experimental import pallas as pl
from jax.experimental.pallas import tpu as pltpu
from jax.sharding import PartitionSpec as P

QUERY_HEADS = 64
KEY_VALUE_HEADS = 8
HEAD_SIZE = 64
TOP = 4
EXP_DEV = 2


EPSILON = 1e-05
ROPE_BASE = 150000.0
SWIGLU_ALPHA = 1.702
CLAMP_LIMIT = 7.0
MASKED_SCORE = -1e30


F32 = jnp.float32
BF = jnp.bfloat16
MESH = pl.DeviceIdType.MESH


def layout(lengths, card_rows):
    seq_ends = jnp.cumsum(lengths)
    places = jnp.arange(card_rows, dtype=jnp.int32)
    past_end = (places[:, None] >= seq_ends[None, :]).astype(jnp.int32)
    segment_ids = jnp.sum(past_end, axis=1)
    position = places - jnp.sum(past_end * lengths[None, :], axis=1)
    return (segment_ids, position)


def tables(position, half_dim):
    inv_freq = jnp.exp(-jnp.log(ROPE_BASE) * jnp.arange(half_dim, dtype=jnp.float32) / half_dim)
    angles = position.astype(jnp.float32)[:, None] * inv_freq[None, :]
    return (jnp.cos(angles)[:, None, :], jnp.sin(angles)[:, None, :])


def apply_rotation(value_matrix, cosine_table, sine_table):
    half_dim = value_matrix.shape[-1] // 2
    lower_half = value_matrix[..., :half_dim]
    upper_half = value_matrix[..., half_dim:]
    return jnp.concatenate(
        [
            lower_half * cosine_table - upper_half * sine_table,
            upper_half * cosine_table + lower_half * sine_table,
        ],
        axis=-1,
    )


def undo_rotation(value_matrix, cosine_table, sine_table):
    half_dim = value_matrix.shape[-1] // 2
    lower_half = value_matrix[..., :half_dim]
    upper_half = value_matrix[..., half_dim:]
    return jnp.concatenate(
        [
            lower_half * cosine_table + upper_half * sine_table,
            upper_half * cosine_table - lower_half * sine_table,
        ],
        axis=-1,
    )


def norm_scale(value_matrix):
    return lax.rsqrt(jnp.mean(value_matrix * value_matrix, axis=-1, keepdims=True) + EPSILON)


def norm_back(value_matrix, inv_scale, gain, grad_norm):
    weighted = grad_norm * gain
    grad_values = inv_scale * weighted - value_matrix * inv_scale**3 * jnp.mean(
        weighted * value_matrix, axis=-1, keepdims=True
    )
    grad_gain = jnp.sum(grad_norm * value_matrix * inv_scale, axis=0)
    return (grad_values, grad_gain)


def left_dot(left, right):
    return jnp.dot(left.T, right, preferred_element_type=jnp.float32)


def mm(spec, left, right):
    return jnp.einsum(spec, left, right, preferred_element_type=jnp.float32)


def gather_all(value):
    return lax.all_gather(value, ("fs", "ep"), axis=0, tiled=True)


def scatter_all(value):
    return lax.psum_scatter(value, ("fs", "ep"), scatter_dimension=0, tiled=True)


def gather_fs(value):
    return lax.all_gather(value, "fs", axis=0, tiled=True)


def scatter_fs(value):
    return lax.psum_scatter(value, "fs", scatter_dimension=0, tiled=True)


def spot():
    fs=lax.axis_index("fs"); ep=lax.axis_index("ep")
    return fs, ep, fs//2, fs%2, ep//2, ep%2

def greet(fs, ep, z, more=0):
    y, x, c = fs//2, fs%2, ep%2
    bar=pltpu.get_barrier_semaphore()
    def hi(f,e): pl.semaphore_signal(bar,inc=1,device_id=(f,e),device_id_type=MESH)
    hi(fs+1-2*x,ep); hi(fs+2-4*y,ep); hi(fs,ep+1-2*c)
    if more: hi(3-fs,ep)
    @pl.when(z>0)
    def _(): hi(fs,ep-2)
    @pl.when(z<3)
    def _(): hi(fs,ep+2)
    @pl.when((z>0)&(z<3))
    def _(): pl.semaphore_wait(bar,5+more)
    @pl.when((z==0)|(z==3))
    def _(): pl.semaphore_wait(bar,4+more)

def scatter_kernel(na, parts, *refs):
    ps=refs[:na]; out=refs[na]; far=refs[na+1]
    q,v1,v2,vu,vd,stg,load,s0,r0,gsem,s1,r1,s2,r2,su,ru,sd,rd,osem = refs[na+2:]
    fs,ep,y,x,z,c = spot()
    rows=ps[0].shape[2]; pr=rows//parts; half=pr//2
    items=na*4*parts
    xn=(fs+1-2*x,ep); yn=(fs+2-4*y,ep); cn=(fs,ep+1-2*c)
    A=pl.ds(0,half); B=pl.ds(half,half)
    def rem(src,dst,s,r,dev): return pltpu.make_async_remote_copy(src,dst,s,r,device_id=dev,device_id_type=MESH)
    def where(i):
        a=i//(4*parts); j=i%(4*parts); k=j//parts; part=j%parts
        zz=(k%2)*(k//2)+(1-k%2)*(3-k//2)
        return a,part,zz
    def block(i,par):
        a,part,zz=where(i)
        return a,zz*2+par,pl.ds(part*pr,pr)
    def on_array(i,f):
        if na==1: f(ps[0])
        else:
            a=i//(4*parts)
            for n in range(na):
                @pl.when(a==n)
                def _(): f(ps[n])
    def give(i,p):
        _,e,r=block(i,1-c)
        return rem(p.at[:,e,r],far.at[i],s0.at[i],r0.at[i],cn)
    def mine(i,p):
        _,e,r=block(i,c)
        return pltpu.make_async_copy(p.at[:,e,r],q.at[i],load.at[i])
    def fetch(i):
        return pltpu.make_async_copy(far.at[i],stg.at[i%2],gsem.at[i%2])
    def one(i):
        return ([rem(q.at[i,2*j+1-x,A],v1.at[i,0,j],s1.at[i,j],r1.at[i,j],xn) for j in range(2)],
                rem(q.at[i,pl.ds((1-y)*2,2),B],v1.at[i,1],s1.at[i,2],r1.at[i,2],yn))
    def two(i):
        return (rem(q.at[i,(1-y)*2+x,A],v2.at[i,0],s2.at[i,0],r2.at[i,0],yn),
                rem(q.at[i,y*2+1-x,B],v2.at[i,1],s2.at[i,1],r2.at[i,1],xn))
    def up(i): return rem(q.at[i,fs],vu.at[i],su.at[i],ru.at[i],(fs,ep+2))
    def down(i): return rem(q.at[i,fs],vd.at[i],sd.at[i],rd.at[i],(fs,ep-2))
    def from_below(i): return rem(q.at[i,fs],vu.at[i],su.at[i],ru.at[i],(fs,ep-2))
    def from_above(i): return rem(q.at[i,fs],vd.at[i],sd.at[i],rd.at[i],(fs,ep+2))
    greet(fs,ep,z)
    @pl.loop(0,items)
    def _(i):
        on_array(i,lambda p: give(i,p).start())
        on_array(i,lambda p: mine(i,p).start())
    def valid(i): return (i>=0)&(i<items)
    def add(dst,src,n):
        for lo in range(0,n,16):
            s=pl.ds(lo,16)
            dst(s,src(s))
    def getfar(i):
        on_array(i,lambda p: give(i,p).wait_recv())
        fetch(i).start()
    getfar(0)
    @pl.loop(0,items+6)
    def _(t):
        @pl.when(t<items)
        def _():
            i=t
            @pl.when(i+1<items)
            def _(): getfar(i+1)
            fetch(i).wait()
            on_array(i,lambda p: mine(i,p).wait())
            for g in range(4):
                q[i,g]=q[i,g]+stg[i%2,g]
            a,b=one(i)
            for k in a: k.start()
            b.start()
        i=t-1
        @pl.when(valid(i))
        def _():
            a,b=one(i)
            for k in a: k.wait_recv()
            for j in range(2):
                q[i,2*j+x,A]=q[i,2*j+x,A]+v1[i,0,j]
            ta,tb=two(i)
            ta.start()
            b.wait_recv()
            for j in range(2):
                q[i,2*y+j,B]=q[i,2*y+j,B]+v1[i,1,j]
            tb.start()
        i2=t-2
        @pl.when(valid(i2))
        def _():
            ta,tb=two(i2)
            ta.wait_recv()
            q[i2,fs,A]=q[i2,fs,A]+v2[i2,0]
            tb.wait_recv()
            q[i2,fs,B]=q[i2,fs,B]+v2[i2,1]
        iu=t-2-z
        @pl.when(valid(iu))
        def _():
            _,_,zz=where(iu)
            @pl.when(zz>=z)
            def _():
                @pl.when(z>0)
                def _():
                    from_below(iu).wait_recv()
                    q[iu,fs]=q[iu,fs]+vu[iu]
                @pl.when(zz>z)
                def _(): up(iu).start()
        idn=t-2-(3-z)
        @pl.when(valid(idn))
        def _():
            _,_,zz=where(idn)
            @pl.when(zz<=z)
            def _():
                @pl.when(z<3)
                def _():
                    from_above(idn).wait_recv()
                    q[idn,fs]=q[idn,fs]+vd[idn]
                @pl.when(zz<z)
                def _(): down(idn).start()
    @pl.loop(0,items)
    def _(i):
        a,part,zz=where(i)
        @pl.when(zz==z)
        def _():
            pltpu.make_async_copy(q.at[i,fs],out.at[a,pl.ds(part*pr,pr)],osem.at[i]).start()
    @pl.loop(0,items)
    def _(i):
        a,part,zz=where(i)
        on_array(i,lambda p: give(i,p).wait_send())
        a1,b1=one(i)
        for k in a1: k.wait_send()
        b1.wait_send()
        ta,tb=two(i); ta.wait_send(); tb.wait_send()
        @pl.when(zz>z)
        def _(): up(i).wait_send()
        @pl.when(zz<z)
        def _(): down(i).wait_send()
        @pl.when(zz==z)
        def _(): pltpu.make_async_copy(q.at[i,fs],out.at[a,pl.ds(part*pr,pr)],osem.at[i]).wait()

def scatter_blocks(arrays, cid, parts=2):
    na=len(arrays); rows,width=arrays[0].shape[-2:]
    arrays=[a.reshape(4,8,rows,width) for a in arrays]
    pr=rows//parts; items=na*4*parts; half=pr//2
    any_=pl.BlockSpec(memory_space=pl.ANY)
    D=pltpu.SemaphoreType.DMA
    V=lambda *s: pltpu.VMEM(s+(width,),BF)
    out,_=pl.pallas_call(partial(scatter_kernel,na,parts),
        out_shape=[jax.ShapeDtypeStruct((na,rows,width),BF),jax.ShapeDtypeStruct((items,4,pr,width),BF)],
        in_specs=[any_]*na,out_specs=[any_,any_],
        scratch_shapes=[V(items,4,pr),V(items,2,2,half),V(items,2,half),V(items,pr),V(items,pr),V(2,4,pr),
            D((items,)),D((items,)),D((items,)),D((2,)),D((items,3)),D((items,3)),D((items,2)),D((items,2)),
            D((items,)),D((items,)),D((items,)),D((items,)),D((items,))],
        compiler_params=pltpu.CompilerParams(collective_id=cid,has_side_effects=True,vmem_limit_bytes=63*1024*1024),
        name="scatter_blocks")(*arrays)
    return out


def reduce_kernel(
    wide_n, slab_n, splits, gw, gq, gs, tw, tq, tk, tv,
    own_w, own_q, all_q, far_w, far_q, pin_w, pin_q, pout_w, pout_q, din_w, din_q, dout_w, dout_q, tot_w, tot_q, mate_q,
    wload, qload, s0w, r0w, s0q, r0q, sa, ra, su, ru, sd, rd, keep, keep_q, keep_m, sc, rc,
):
    fs, ep, y, x, z, c = spot()
    mate = (fs, ep + 1 - 2 * c)
    rows_w, rows_q = own_w.shape[1], own_q.shape[1]
    parts = slab_n // 4
    items = wide_n + slab_n

    def rem(src, dst, s, r, dev):
        return pltpu.make_async_remote_copy(src, dst, s, r, device_id=dev, device_id_type=MESH)

    def source(s):
        return ((y + s // 2) % 2) * 2 + (x + s) % 2

    def give_w(i):
        return rem(gw.at[1 - c, i], far_w.at[i], s0w.at[i], r0w.at[i], mate)

    def load_w(i):
        return pltpu.make_async_copy(gw.at[c, i], own_w.at[i], wload.at[i])

    body = gq.shape[1] - (2 * parts - 1) * rows_q

    def pieces(s, core, dst):
        base = core * parts * rows_q
        out = []
        for p in range(parts):
            n = rows_q if p < parts - 1 else body
            at = pl.ds(pl.multiple_of(base + p * rows_q, 16), n)
            out.append((gq.at[source(s), at], dst.at[s, p, pl.ds(0, n)]))
        rest = dst.at[s, parts - 1, pl.ds(body, rows_q - body)]
        at = pl.ds((parts - 1) * rows_q + body, rows_q - body)
        return out + [(gq.at[source(s), at], rest)], (gs.at[source(s)], rest)

    def give_q(s, do):
        common, other = pieces(s, 1 - c, far_q)

        def move(n, pair):
            do(rem(*pair, s0q.at[s, n], r0q.at[s, n], mate))

        for n, pair in enumerate(common[:-1]):
            move(n, pair)

        @pl.when(c == 1)
        def _():
            move(parts, common[-1])

        @pl.when(c == 0)
        def _():
            move(parts, other)

    def load_q(s, do):
        common, other = pieces(s, c, all_q)

        def move(n, pair):
            do(pltpu.make_async_copy(*pair, qload.at[s, n]))

        for n, pair in enumerate(common[:-1]):
            move(n, pair)

        @pl.when(c == 0)
        def _():
            move(parts, common[-1])

        @pl.when(c == 1)
        def _():
            move(parts, other)

    def pass_q(s):
        dev = (source(s), ep)
        return rem(all_q.at[s], own_q.at[pl.ds(s * parts, parts)], sa.at[s], ra.at[s], dev)

    def on_item(i, f):
        @pl.when(i < wide_n)
        def _():
            f(own_w, pin_w, pout_w, din_w, dout_w, tot_w, i)

        @pl.when(i >= wide_n)
        def _():
            f(own_q, pin_q, pout_q, din_q, dout_q, tot_q, i - wide_n)

    def valid(i):
        return (i >= 0) & (i < items)

    def place(buf, sem, j, core):
        at = pl.ds(pl.multiple_of((core * parts + j % parts) * rows_q, 16), rows_q)
        lo, out = 0, []
        for n, (dst, size) in enumerate(zip((tq, tk, tv), splits)):
            to = pl.ds(pl.multiple_of(source(j // parts) * size, 128), size)
            out.append(
                pltpu.make_async_copy(buf.at[j, :, pl.ds(lo, size)], dst.at[at, to], sem.at[j, n])
            )
            lo += size
        return out

    def share_w(i):
        dst = tw.at[c, i]
        return (
            pltpu.make_async_copy(tot_w.at[i], dst, keep.at[i]),
            rem(tot_w.at[i], dst, sc.at[i], rc.at[i], mate),
        )

    def share_q(j):
        i = j + wide_n
        return rem(tot_q.at[j], mate_q.at[j], sc.at[i], rc.at[i], mate)

    greet(fs, ep, z, 1)

    @pl.loop(0, wide_n)
    def _(i):
        give_w(i).start()
        load_w(i).start()

    for s in (1, 2, 3, 0):
        give_q(s, lambda copy: copy.start())
        load_q(s, lambda copy: copy.start())

    @pl.loop(0, items + 4)
    def _(t):
        @pl.when(t < wide_n)
        def _():
            load_w(t).wait()
            give_w(t).wait_recv()
            own_w[t] = own_w[t] + far_w[t]

        for n, s in enumerate((1, 2, 3, 0)):

            @pl.when(t == n + 3)
            def _():
                load_q(s, lambda copy: copy.wait())
                give_q(s, lambda copy: copy.wait_recv())

                @pl.loop(0, parts)
                def _(j):
                    if s:
                        all_q[s, j] = all_q[s, j] + far_q[s, j]
                    else:
                        own_q[j] = all_q[0, j] + far_q[0, j]

                if s:
                    pass_q(s).start()

        for s in (1, 2, 3):

            @pl.when(t == wide_n + s * parts)
            def _():
                pass_q(s).wait_recv()

        iu = t - z

        @pl.when(valid(iu))
        def _():
            def go(own, pin, pout, din, dout, tot, i):
                @pl.when(z == 0)
                def _():
                    rem(own.at[i], pin.at[i], su.at[iu], ru.at[iu], (fs, ep + 2)).start()

                @pl.when(z > 0)
                def _():
                    rem(own.at[i], pin.at[i], su.at[iu], ru.at[iu], (fs, ep - 2)).wait_recv()

                @pl.when((z > 0) & (z < 3))
                def _():
                    pout[i] = pin[i] + own[i]
                    rem(pout.at[i], pin.at[i], su.at[iu], ru.at[iu], (fs, ep + 2)).start()

            on_item(iu, go)

        idn = t - 3 + z

        @pl.when(valid(idn))
        def _():
            def go(own, pin, pout, din, dout, tot, i):
                @pl.when(z == 3)
                def _():
                    rem(own.at[i], din.at[i], sd.at[idn], rd.at[idn], (fs, ep - 2)).start()

                @pl.when(z < 3)
                def _():
                    rem(own.at[i], din.at[i], sd.at[idn], rd.at[idn], (fs, ep + 2)).wait_recv()

                @pl.when((z > 0) & (z < 3))
                def _():
                    dout[i] = din[i] + own[i]
                    rem(dout.at[i], din.at[i], sd.at[idn], rd.at[idn], (fs, ep - 2)).start()

            on_item(idn, go)

        last = t - 3

        @pl.when(valid(last))
        def _():
            def go(own, pin, pout, din, dout, tot, i):
                @pl.when(z == 0)
                def _():
                    tot[i] = own[i] + din[i]

                @pl.when(z == 3)
                def _():
                    tot[i] = own[i] + pin[i]

                @pl.when((z == 1) | (z == 2))
                def _():
                    tot[i] = own[i] + pin[i] + din[i]

            on_item(last, go)

            @pl.when(last < wide_n)
            def _():
                for copy in share_w(last):
                    copy.start()

            @pl.when(last >= wide_n)
            def _():
                j = last - wide_n
                for copy in (share_q(j), *place(tot_q, keep_q, j, c)):
                    copy.start()

    @pl.loop(0, items)
    def _(i):
        @pl.when(i < wide_n)
        def _():
            for copy in share_w(i):
                copy.wait()

        @pl.when(i >= wide_n)
        def _():
            j = i - wide_n
            share_q(j).wait()
            for copy in place(mate_q, keep_m, j, 1 - c):
                copy.start()

        def go(own, pin, pout, din, dout, tot, j):
            @pl.when(z < 3)
            def _():
                rem(own.at[j], pin.at[j], su.at[i], ru.at[i], (fs, ep + 2)).wait_send()

            @pl.when(z > 0)
            def _():
                rem(own.at[j], din.at[j], sd.at[i], rd.at[i], (fs, ep - 2)).wait_send()

        on_item(i, go)

    @pl.loop(0, slab_n)
    def _(j):
        for copy in (*place(tot_q, keep_q, j, c), *place(mate_q, keep_m, j, 1 - c)):
            copy.wait()

    @pl.loop(0, wide_n)
    def _(i):
        give_w(i).wait_send()

    for s in range(4):
        give_q(s, lambda copy: copy.wait_send())
        if s:
            pass_q(s).wait_send()


def reduce_parts(gw, gq, gs, parts, splits, cid):
    wide_n = gw.shape[1]
    slab_rows = gq.shape[1] + gs.shape[1]
    rows_q, cols = slab_rows // (2 * parts), gq.shape[2]
    slab_n = 4 * parts
    free = pl.BlockSpec(memory_space=pl.ANY)
    D = pltpu.SemaphoreType.DMA
    W = pltpu.VMEM((wide_n,) + gw.shape[2:], BF)
    Q = pltpu.VMEM((slab_n, rows_q, cols), BF)
    Q4 = pltpu.VMEM((4, parts, rows_q, cols), BF)
    items = wide_n + slab_n
    return pl.pallas_call(
        partial(reduce_kernel, wide_n, slab_n, splits),
        out_shape=[jax.ShapeDtypeStruct(gw.shape, BF)]
        + [jax.ShapeDtypeStruct((slab_rows, 4 * size), BF) for size in splits],
        in_specs=[free] * 3,
        out_specs=[free] * 4,
        scratch_shapes=[W, Q, Q4, W, Q4] + [W, Q] * 5 + [Q]
        + [D((wide_n,)), D((4, parts + 1)), D((wide_n,)), D((wide_n,)), D((4, parts + 1)), D((4, parts + 1))]
        + [D((4,)), D((4,))]
        + [D((items,))] * 4 + [D((wide_n,)), D((slab_n, 3)), D((slab_n, 3)), D((items,)), D((items,))],
        compiler_params=pltpu.CompilerParams(
            collective_id=cid, has_side_effects=True, vmem_limit_bytes=63 * 1024 * 1024
        ),
        cost_estimate=pl.CostEstimate(flops=0, bytes_accessed=500_000_000, transcendentals=0),
        name="reduce_parts",
    )(gw, gq, gs)


def start_kernel(
    splits, own, few, wq, wk, wv, rows_out, few_out, w_out, own_cols,
    here, here_few, own_w, sx, rx, sf, rf, sw, rw, sm, rm,
):
    fs, ep, y, x, z, c = spot()
    mate = (fs, ep + 1 - 2 * c)
    shard = wq.shape[0]
    pair = (fs, ep + 2 - 4 * (z % 2))
    units = shard // 16
    edges = [16 * (units * n // 4) for n in range(5)]
    quarters = [(lo, hi - lo) for lo, hi in zip(edges, edges[1:])]
    half = own.shape[0] // 2
    bands = (pl.ds(0, half), pl.ds(half, half))

    def peer(s):
        return ((y + s // 2) % 2) * 2 + (x + s) % 2

    def rem(src, dst, s, r, dev):
        return pltpu.make_async_remote_copy(src, dst, s, r, device_id=dev, device_id_type=MESH)

    def columns(dev, at):
        lo, out = 0, []
        for src, size in zip((wq, wk, wv), splits):
            cols = pl.ds(pl.multiple_of(dev * size, 128), size)
            out.append((src.at[at, cols], pl.ds(lo, size)))
            lo += size
        return out

    def send(s, lo, n):
        at = pl.ds(lo, n)
        return [
            rem(src, w_out.at[fs, at, cols], sw.at[s, k], rw.at[s, k], (peer(s), ep))
            for k, (src, cols) in enumerate(columns(peer(s), at))
        ]

    def arrive(s, lo, n):
        at = pl.ds(lo, n)
        return [
            rem(w_out.at[peer(s), at, cols], w_out.at[peer(s), at, cols], sw.at[s, k], rw.at[s, k], mate)
            for k, (_, cols) in enumerate(columns(fs, at))
        ]

    def share(s, k, lo, n, dev):
        v = w_out.at[peer(s), pl.ds(lo, n)]
        return rem(v, v, sm.at[s, k], rm.at[s, k], dev)

    def give(s, band):
        v = rows_out.at[fs, bands[band]]
        return rem(v, v, sx.at[s, band], rx.at[s, band], (peer(s), ep))

    def pass_on(s, band):
        v = rows_out.at[peer(s), bands[band]]
        return rem(v, v, sx.at[3, band], rx.at[3, band], (peer(3 - s), ep))

    def give_few(s):
        return rem(few, few_out.at[fs], sf.at[s], rf.at[s], (peer(s), ep))

    keep = pltpu.make_async_copy(own, rows_out.at[fs], here)
    keep.start()
    keep_few = pltpu.make_async_copy(few, few_out.at[fs], here_few)
    keep_few.start()
    locals_ = []
    for k, (src, cols) in enumerate(columns(fs, pl.ds(0, shard))):
        locals_.append(pltpu.make_async_copy(src, own_cols.at[:, cols], own_w.at[k]))
    for copy in locals_:
        copy.start()
    greet(fs, ep, z, 1)
    keep.wait()
    for copy in locals_:
        copy.wait()
    own_slab = pltpu.make_async_copy(own_cols, w_out.at[fs], here)
    own_slab.start()
    for s in (1, 2, 3):
        give_few(s).start()
    for quarter in range(4):

        @pl.when((z % 2) * 2 + c == quarter)
        def _():
            mine, mates, pairs, last = (quarters[quarter ^ n] for n in (0, 1, 2, 3))
            for s in (3, 1, 2):
                for copy in send(s, *mine):
                    copy.start()
            for s, band in ((1, 0), (2, 1), (1, 1), (2, 0)):
                give(s, band).start()
            for s in (1, 2, 3):
                for copy in arrive(s, *mine):
                    copy.wait_recv()
                share(s, 0, *mine, pair).start()
                share(s, 1, *mine, mate).start()
            give(1, 0).wait_recv()
            pass_on(1, 0).start()
            give(2, 1).wait_recv()
            pass_on(2, 1).start()
            for s in (1, 2, 3):
                share(s, 0, *pairs, pair).wait_recv()
                share(s, 2, *pairs, mate).start()
            for s in (1, 2, 3):
                share(s, 1, *mates, mate).wait_recv()
                share(s, 2, *last, mate).wait_recv()
            for s in (1, 2, 3):
                for copy in send(s, *mine):
                    copy.wait_send()
                share(s, 0, *mine, pair).wait_send()
                share(s, 1, *mine, mate).wait_send()
                share(s, 2, *pairs, mate).wait_send()

    for s in (1, 2):
        give(s, 2 - s).wait_recv()
        for band in range(2):
            give(s, band).wait_send()
    for s, band in ((1, 0), (2, 1)):
        pass_on(s, band).wait()
    for s in (1, 2, 3):
        give_few(s).wait_send()
        rem(few, few_out.at[peer(s)], sf.at[s], rf.at[s], mate).wait_recv()
    own_slab.wait()
    keep_few.wait()


def start_exchange(own, few, wq, wk, wv, cid):
    shard = wq.shape[0]
    splits = tuple(w.shape[1] // 4 for w in (wq, wk, wv))
    free = pl.BlockSpec(memory_space=pl.ANY)
    D = pltpu.SemaphoreType.DMA
    return pl.pallas_call(
        partial(start_kernel, splits),
        out_shape=[
            jax.ShapeDtypeStruct((4,) + own.shape, BF),
            jax.ShapeDtypeStruct((4,) + few.shape, BF),
            jax.ShapeDtypeStruct((4, shard, sum(splits)), BF),
        ],
        in_specs=[pl.BlockSpec(memory_space=pltpu.VMEM)] * 2 + [free] * 3,
        out_specs=[free] * 3,
        scratch_shapes=[pltpu.VMEM((shard, sum(splits)), BF), D, D, D((3,)), D((4, 2)), D((4, 2)), D((4,)), D((4,)), D((4, 3)), D((4, 3)), D((4, 3)), D((4, 3))],
        compiler_params=pltpu.CompilerParams(collective_id=cid, has_side_effects=True),
        name="start_exchange",
    )(own, few, wq, wk, wv)


def nn(left, right):
    return lax.dot_general(left, right, (((1,), (0,)), ((), ())), preferred_element_type=F32)


def nt(left, right):
    return lax.dot_general(left, right, (((1,), (1,)), ((), ())), preferred_element_type=F32)


def tn(left, right):
    return lax.dot_general(left, right, (((0,), (0,)), ((), ())), preferred_element_type=F32)


def strips(total, size):
    return [(at, min(size, total - at)) for at in range(0, total, size)]


def remote(src, dst, send, recv, device):
    return pltpu.make_async_remote_copy(
        src, dst, send, recv, device_id=device, device_id_type=MESH
    )


def line_order(z, i):
    code = jnp.where(z == 0, 228, jnp.where(z == 1, 225, jnp.where(z == 2, 30, 27)))
    power = jnp.where(i == 0, 1, jnp.where(i == 1, 4, jnp.where(i == 2, 16, 64)))
    return (code // power) % 4


class Gather:
    def __init__(self, full, sems):
        self.full = full
        self.sz, self.rz, self.s1, self.r1, self.s2, self.r2, self.sc, self.rc = sems
        self.fs, self.ep, self.y, self.x, self.z, self.c = spot()
        half = full.shape[3] // 2
        self.upper, self.lower = pl.ds(0, half), pl.ds(half, half)
        self.xn = (self.fs + 1 - 2 * self.x, self.ep)
        self.yn = (self.fs + 2 - 4 * self.y, self.ep)
        self.mate = (self.fs, self.ep + 1 - 2 * self.c)

    def item(self, t):
        return t // 4, line_order(self.z, t % 4)

    def along(self, a, zz, up):
        view = self.full.at[a, self.fs, zz * 2 + self.c]
        other = (self.fs, self.ep + (2 if up else -2))
        return remote(view, view, self.sz.at[a, zz, up], self.rz.at[a, zz], other)

    def arriving(self, a, zz):
        view = self.full.at[a, self.fs, zz * 2 + self.c]
        other = (self.fs, self.ep + jnp.where(self.z == 0, 2, -2))
        return remote(view, view, self.sz.at[a, zz, 0], self.rz.at[a, zz], other)

    def first(self, a, zz):
        e = zz * 2 + self.c
        v = self.full.at[a, self.fs, e, self.upper]
        w = self.full.at[a, self.fs, e, self.lower]
        s, r = self.s1.at[a, zz], self.r1.at[a, zz]
        return (
            remote(v, v, s.at[0], r.at[0], self.xn),
            remote(w, w, s.at[1], r.at[1], self.yn),
            remote(w, w, s.at[2], r.at[2], self.xn),
            remote(v, v, s.at[3], r.at[3], self.yn),
        )

    def second(self, a, zz):
        e = zz * 2 + self.c
        v = self.full.at[a, self.y * 2 + 1 - self.x, e, self.upper]
        w = self.full.at[a, (1 - self.y) * 2 + self.x, e, self.lower]
        s, r = self.s2.at[a, zz], self.r2.at[a, zz]
        return remote(v, v, s.at[0], r.at[0], self.yn), remote(w, w, s.at[1], r.at[1], self.xn)

    def across(self, a, zz, e):
        v = self.full.at[a, :, zz * 2 + e]
        return remote(v, v, self.sc.at[a, zz], self.rc.at[a, zz], self.mate)

    def step0(self, t):
        @pl.when(t < 8)
        def _():
            a, zz = self.item(t)

            @pl.when(zz != self.z)
            def _():
                self.arriving(a, zz).wait_recv()

            @pl.when((zz <= self.z) & (self.z < 3))
            def _():
                self.along(a, zz, 1).start()

            @pl.when((zz >= self.z) & (self.z > 0))
            def _():
                self.along(a, zz, 0).start()

    def step0_if(self, t, inner):
        inside = (self.z == 1) | (self.z == 2)

        @pl.when(inside == inner)
        def _():
            self.step0(t)

    def step1(self, t):
        @pl.when(t < 8)
        def _():
            for copy in self.first(*self.item(t)):
                copy.start()

    def step2(self, t):
        @pl.when(t < 8)
        def _():
            a, zz = self.item(t)
            from_x, from_y, _, _ = self.first(a, zz)
            to_y, to_x = self.second(a, zz)
            from_x.wait_recv()
            to_y.start()
            from_y.wait_recv()
            to_x.start()

    def step3(self, t):
        @pl.when(t < 8)
        def _():
            a, zz = self.item(t)
            for copy in (*self.first(a, zz)[2:], *self.second(a, zz)):
                copy.wait_recv()
            self.across(a, zz, self.c).start()

    def step4(self, t):
        a, zz = self.item(t)
        self.across(a, zz, 1 - self.c).wait_recv()

    def finish(self):
        @pl.loop(0, 8)
        def _(t):
            a, zz = self.item(t)
            self.across(a, zz, self.c).wait_send()
            for copy in (*self.first(a, zz), *self.second(a, zz)):
                copy.wait_send()

            @pl.when((zz <= self.z) & (self.z < 3))
            def _():
                self.along(a, zz, 1).wait_send()

            @pl.when((zz >= self.z) & (self.z > 0))
            def _():
                self.along(a, zz, 0).wait_send()


def experts_kernel(
    cap, width,
    n_own, g_own, wg_hbm, wu_hbm, wd_hbm, bg_ref, bu_ref, bd_ref,
    full, out_hbm, row_hbm, xs_hbm, eg_hbm, mid_hbm, ug_hbm, gg_hbm, cu_hbm, cg_hbm,
    sum_g, sum_u, sum_d,
    wg_ref, wu_ref, wd_ref, bin_, meta, pmat, pmat_t, gates, xs, res, mid, cub, cgb, dots, stage,
    w_sem, own_sem, in_sem, st_sem, save_sem,
    *sems,
):
    gather = Gather(full, sems)
    fs, ep, z = gather.fs, gather.ep, gather.z
    card_rows, wpad = bin_.shape[2:]
    tail = wpad - 128
    off = width - tail
    first = jnp.where(fs == 0, 1.0, 0.0).astype(F32)
    nb = 8
    rows = nb * cap
    weights = [
        pltpu.make_async_copy(src, dst, w_sem.at[n])
        for n, (src, dst) in enumerate(((wg_hbm, wg_ref), (wu_hbm, wu_ref), (wd_hbm, wd_ref)))
    ]
    keep = [
        pltpu.make_async_copy(src, full.at[a, fs, ep], own_sem.at[a])
        for a, src in enumerate((n_own, g_own))
    ]
    for copy in keep + weights:
        copy.start()
    greet(fs, ep, z)
    for copy in keep:
        copy.wait()
    gather.step0(0)
    gather.step1(0)
    gather.step0(1)
    gather.step2(0)
    gather.step1(1)
    gather.step3(0)
    gather.step0(2)

    def load(t):
        a, zz = gather.item(t)
        return pltpu.make_async_copy(full.at[a, :, pl.ds(zz * 2, 2)], bin_, in_sem)

    def save(src, dst, k, i, n):
        return pltpu.make_async_copy(src.at[k], dst.at[k, i], save_sem.at[n, k])

    def save_rows(dst, k, i):
        return pltpu.make_async_copy(xs.at[:, k], dst.at[k, i], save_sem.at[0, k])

    def fetch(src, dst, k, i, n):
        return pltpu.make_async_copy(src.at[k, i], dst.at[k], save_sem.at[n, k])

    def rows_of(ref, k, lo=0, n=width):
        return ref[:, k, :, lo : lo + n].reshape(rows, n)

    def next_load(t):
        @pl.when(t < 8)
        def _():
            gather.step4(t)
            load(t).start()

    def spread(i, prepare):
        @pl.loop(0, nb)
        def _(b):
            j, c = b // 2, b % 2
            if prepare:
                meta[...] = jnp.transpose(bin_[j, c, :, tail:].astype(F32))
                at = pl.ds(pl.multiple_of(b * cap, 16), cap)
                hits = []
                for k in range(2):
                    e = ep * 2 + k
                    place = meta[pl.ds(off + e, 1), :]
                    gate = meta[pl.ds(off + 16 + e, 1), :] + meta[pl.ds(off + 32 + e, 1), :]
                    hit = lax.broadcasted_iota(jnp.int32, (cap, card_rows), 0).astype(F32) == place
                    gates[i, k, at, :] = jnp.sum(jnp.where(hit, gate, 0.0), axis=1, keepdims=True)
                    hits.append(jnp.where(hit, 1.0, 0.0))
                hits.append(jnp.zeros((card_rows - 2 * cap, card_rows), F32))
                hits = jnp.concatenate(hits, axis=0)
                pmat[i, b] = hits[: 2 * cap].astype(BF)
                pmat_t[i, b] = jnp.transpose(hits).astype(BF)
            pick = pmat[i, b]
            for lo, n in strips(width, 768):
                got = nn(pick, bin_[j, c, :, lo : lo + n]).astype(BF)
                xs[b, :, :, lo : lo + n] = got.reshape(2, cap, n)

    def group_store(dst, zz):
        return pltpu.make_async_copy(stage, dst.at[:, pl.ds(zz * 2, 2)], st_sem)

    def combine(i, with_dots):
        column = lax.broadcasted_iota(jnp.int32, (cap, wpad - width), 1)

        @pl.loop(0, nb)
        def _(b):
            j, c = b // 2, b % 2
            pick = pmat_t[i, b, :, : 2 * cap]
            for lo, n in strips(width, 768):
                both = res[b, :, :, lo : lo + n].reshape(2 * cap, n)
                stage[j, c, :, lo : lo + n] = nn(pick, both).astype(BF)
            if with_dots:
                at = pl.ds(pl.multiple_of(b * cap, 16), cap)
                own_dots = jnp.concatenate(
                    [
                        jnp.where(column == ep * 2 + k, dots[k, at, :], 0.0).astype(BF)
                        for k in range(2)
                    ],
                    axis=0,
                )
                stage[j, c, :, width:] = nn(pick, own_dots).astype(BF)
            else:
                stage[j, c, :, width:] = jnp.zeros((card_rows, wpad - width), BF)

    next_load(0)
    for copy in weights:
        copy.wait()

    @pl.loop(0, 4)
    def _(i):
        zz = line_order(z, i)
        gather.step2(i + 1)
        gather.step1(i + 2)
        gather.step0_if(i + 3, True)
        load(i).wait()
        spread(i, True)
        for k in range(2):
            save_rows(xs_hbm, k, i).start()

        @pl.loop(0, 2)
        def _(k):
            @pl.when(k == 1)
            def _():
                gather.step3(i + 1)

            x = rows_of(xs, k)
            gate_soft = CLAMP_LIMIT * jnp.tanh((nt(x, wg_ref[k]) + bg_ref[k]) * (1.0 / CLAMP_LIMIT))
            up_soft = CLAMP_LIMIT * jnp.tanh((nt(x, wu_ref[k]) + bu_ref[k]) * (1.0 / CLAMP_LIMIT))
            sig = jax.nn.sigmoid(SWIGLU_ALPHA * gate_soft)
            glu = gate_soft * sig
            mid[k] = ((up_soft + 1.0) * glu).astype(BF)
            cub[k] = (glu * (1.0 - (up_soft * (1.0 / CLAMP_LIMIT)) ** 2)).astype(BF)
            cgb[k] = (
                (up_soft + 1.0)
                * (sig + SWIGLU_ALPHA * glu * (1.0 - sig))
                * (1.0 - (gate_soft * (1.0 / CLAMP_LIMIT)) ** 2)
            ).astype(BF)
            save(mid, mid_hbm, k, i, 1).start()
            save(cub, cu_hbm, k, i, 2).start()
            save(cgb, cg_hbm, k, i, 3).start()
            for lo, n in strips(width, 768):
                part = nn(mid[k], wd_ref[k, :, lo : lo + n]) + first * bd_ref[k, :, lo : lo + n]
                res[:, k, :, lo : lo + n] = (part * gates[i, k]).astype(BF).reshape(nb, cap, n)

        gather.step0_if(i + 3, False)
        next_load(i + 1)

        @pl.when(i > 0)
        def _():
            group_store(out_hbm, line_order(z, i - 1)).wait()

        combine(i, False)
        group_store(out_hbm, zz).start()
        for k in range(2):
            save_rows(xs_hbm, k, i).wait()
            save(mid, mid_hbm, k, i, 1).wait()
            save(cub, cu_hbm, k, i, 2).wait()
            save(cgb, cg_hbm, k, i, 3).wait()

    group_store(out_hbm, line_order(z, 3)).wait()
    sum_g[...] = jnp.zeros_like(sum_g)
    sum_u[...] = jnp.zeros_like(sum_u)
    sum_d[...] = jnp.zeros_like(sum_d)

    @pl.loop(0, 4)
    def _(i):
        zz = line_order(z, i)
        for k in range(2):
            fetch(mid_hbm, mid, k, i, 1).start()
            fetch(cu_hbm, cub, k, i, 2).start()
            fetch(cg_hbm, cgb, k, i, 3).start()
        gather.step2(i + 5)
        gather.step1(i + 6)
        gather.step0_if(i + 7, True)
        load(i + 4).wait()
        spread(i, False)

        @pl.loop(0, 2)
        def _(k):
            @pl.when(k == 1)
            def _():
                gather.step3(i + 5)

            fetch(mid_hbm, mid, k, i, 1).wait()
            fetch(cu_hbm, cub, k, i, 2).wait()
            fetch(cg_hbm, cgb, k, i, 3).wait()
            g_rows = rows_of(xs, k)
            plain = nt(g_rows, wd_ref[k])
            gate = gates[i, k]
            grad = plain * gate
            g_rows = g_rows.astype(F32)
            dots[k] = jnp.sum(plain * mid[k].astype(F32), axis=1, keepdims=True) + first * jnp.sum(
                g_rows * bd_ref[k], axis=1, keepdims=True
            )
            up_grad = (grad * cub[k].astype(F32)).astype(BF)
            cub[k] = up_grad
            sum_u[k] += jnp.sum(up_grad.astype(F32), axis=0, keepdims=True)
            gate_grad = (grad * cgb[k].astype(F32)).astype(BF)
            cgb[k] = gate_grad
            sum_g[k] += jnp.sum(gate_grad.astype(F32), axis=0, keepdims=True)
            scaled = (g_rows * gate).astype(BF)
            xs[:, k] = scaled.reshape(nb, cap, width)
            sum_d[k] += jnp.sum(scaled.astype(F32), axis=0, keepdims=True)
            save_rows(eg_hbm, k, i).start()
            save(cub, ug_hbm, k, i, 4).start()
            save(cgb, gg_hbm, k, i, 5).start()
            for lo, n in strips(width, 768):
                part = nn(cgb[k], wg_ref[k, :, lo : lo + n]) + nn(cub[k], wu_ref[k, :, lo : lo + n])
                res[:, k, :, lo : lo + n] = part.astype(BF).reshape(nb, cap, n)

        gather.step0_if(i + 7, False)
        next_load(i + 5)

        @pl.when(i > 0)
        def _():
            group_store(row_hbm, line_order(z, i - 1)).wait()

        combine(i, True)
        group_store(row_hbm, zz).start()
        for k in range(2):
            save_rows(eg_hbm, k, i).wait()
            save(cub, ug_hbm, k, i, 4).wait()
            save(cgb, gg_hbm, k, i, 5).wait()

    group_store(row_hbm, line_order(z, 3)).wait()
    gather.finish()


def experts(n_own, g_own, wg_t, b_gate, wu_t, b_up, w_down, b_down, cap, cid):
    rows, wpad = n_own.shape
    ff, width = w_down.shape[1:]
    n, m = 32 * cap, 8 * cap
    free = pl.BlockSpec(memory_space=pl.ANY)
    near = pl.BlockSpec(memory_space=pltpu.VMEM)
    shape = jax.ShapeDtypeStruct
    V = pltpu.VMEM
    D = pltpu.SemaphoreType.DMA
    biases = [b.astype(F32)[:, None] for b in (b_gate, b_up, b_down)]
    out = pl.pallas_call(
        partial(experts_kernel, cap, width),
        out_shape=[shape((2, 4, 8, rows, wpad), BF)]
        + [shape((4, 8, rows, wpad), BF)] * 2
        + [shape((2, 4, 8, cap, width), BF)] * 2
        + [shape((2, 4, m, ff), BF)] * 5
        + [shape((2, 1, ff), F32)] * 2
        + [shape((2, 1, width), F32)],
        in_specs=[near] * 2 + [free] * 3 + [near] * 3,
        out_specs=[free] * 10 + [near] * 3,
        scratch_shapes=[
            V((2, ff, width), BF), V((2, ff, width), BF), V((2, ff, width), BF),
            V((4, 2, rows, wpad), BF), V((128, rows), F32),
            V((4, 8, 2 * cap, rows), BF), V((4, 8, rows, rows), BF), V((4, 2, m, 1), F32),
            V((8, 2, cap, width), BF), V((8, 2, cap, width), BF),
            V((2, m, ff), BF), V((2, m, ff), BF), V((2, m, ff), BF),
            V((2, m, 1), F32), V((4, 2, rows, wpad), BF),
            D((3,)), D((2,)), D, D, D((6, 2)),
            D((2, 4, 2)), D((2, 4)), D((2, 4, 4)), D((2, 4, 4)), D((2, 4, 2)), D((2, 4, 2)), D((2, 4)), D((2, 4)),
        ],
        compiler_params=pltpu.CompilerParams(
            collective_id=cid, has_side_effects=True, vmem_limit_bytes=63 * 1024 * 1024
        ),
        cost_estimate=pl.CostEstimate(
            flops=24 * n * width * ff, bytes_accessed=300_000_000, transcendentals=6 * n * ff
        ),
        name="experts",
    )(n_own, g_own, wg_t, wu_t, w_down, *biases)
    saved = [v.reshape(2, n, -1) for v in out[3:8]]
    return (*out[1:3], *saved, *(total[:, 0] for total in out[10:]))


def project_sum_kernel(parts, m_ref, w_ref, out_ref, p_ref, q, v1, v2, s1, r1, s2, r2):
    fs, ep, y, x, z, c = spot()
    rows = p_ref.shape[1]
    step = rows // (2 * parts)
    xn, yn = (fs + 1 - 2 * x, ep), (fs + 2 - 4 * y, ep)

    def rem(src, dst, s, r, dev):
        return pltpu.make_async_remote_copy(src, dst, s, r, device_id=dev, device_id_type=MESH)

    def band(n, half):
        return pl.ds((2 * n + half) * step, step)

    def one(n):
        a, b = band(n, 0), band(n, 1)
        out = [
            (rem(p_ref.at[2 * j + 1 - x, a], v1.at[n, 0, j], s1.at[n, 0, j], r1.at[n, 0, j], xn))
            for j in range(2)
        ]
        return out + [
            rem(p_ref.at[2 * (1 - y) + j, b], v1.at[n, 1, j], s1.at[n, 1, j], r1.at[n, 1, j], yn)
            for j in range(2)
        ]

    def two(n):
        return (
            rem(q.at[n, 0], v2.at[n, 0], s2.at[n, 0], r2.at[n, 0], yn),
            rem(q.at[n, 1], v2.at[n, 1], s2.at[n, 1], r2.at[n, 1], xn),
        )

    def project(dev):
        m = m_ref[dev]
        for lo, n in strips(w_ref.shape[0], 768):
            p_ref[dev, :, lo : lo + n] = nt(m, w_ref[lo : lo + n, :]).astype(BF)

    def send(dx, dy):
        for n in range(parts):
            copies = one(n)
            for j in range(2):
                if dx:

                    @pl.when(y == (j + dy) % 2)
                    def _():
                        copies[j].start()

                if dy:

                    @pl.when(x == (j + dx) % 2)
                    def _():
                        copies[2 + j].start()

    project(3 - fs)
    greet(fs, ep, z)
    send(1, 1)
    project(2 * y + 1 - x)
    send(1, 0)
    project(2 * (1 - y) + x)
    send(0, 1)
    project(fs)
    for n in range(parts):
        a, b = band(n, 0), band(n, 1)
        copies = one(n)
        for copy in copies[:2]:
            copy.wait_recv()
        q[n, 0] = p_ref[2 * (1 - y) + x, a] + v1[n, 0, 1 - y]
        two(n)[0].start()
        for copy in copies[2:]:
            copy.wait_recv()
        q[n, 1] = p_ref[2 * y + 1 - x, b] + v1[n, 1, 1 - x]
        two(n)[1].start()
        out_ref[a, :] = p_ref[fs, a].astype(F32) + v1[n, 0, y].astype(F32)
        out_ref[b, :] = p_ref[fs, b].astype(F32) + v1[n, 1, x].astype(F32)
    for n in range(parts):
        for half in range(2):
            at = band(n, half)
            two(n)[half].wait_recv()
            out_ref[at, :] += v2[n, half].astype(F32)
    for n in range(parts):
        for copy in (*one(n), *two(n)):
            copy.wait_send()


def project_sum(mixed, w_t, cid, parts=2):
    _, rows, features = mixed.shape
    width = w_t.shape[0]
    near = pl.BlockSpec(memory_space=pltpu.VMEM)
    D = pltpu.SemaphoreType.DMA
    step = rows // (2 * parts)
    V = pltpu.VMEM
    return pl.pallas_call(
        partial(project_sum_kernel, parts),
        out_shape=jax.ShapeDtypeStruct((rows, width), F32),
        in_specs=[near, near],
        out_specs=near,
        scratch_shapes=[
            V((4, rows, width), BF), V((parts, 2, step, width), BF),
            V((parts, 2, 2, step, width), BF), V((parts, 2, step, width), BF),
            D((parts, 2, 2)), D((parts, 2, 2)), D((parts, 2)), D((parts, 2)),
        ],
        compiler_params=pltpu.CompilerParams(
            collective_id=cid, has_side_effects=True, vmem_limit_bytes=40 * 1024 * 1024
        ),
        cost_estimate=pl.CostEstimate(
            flops=8 * rows * features * width, bytes_accessed=20_000_000, transcendentals=0
        ),
        name="project_sum",
    )(mixed, w_t)


def weight_grads_kernel(xs, eg, mid, ug, gg, down, gate, up, rows, left, out, r_sem, l_sem, o_sem):
    width = xs.shape[2]
    jobs = [(k, w) for k in range(2) for w in range(3)]
    lefts, outs = (mid, gg, ug), (down, gate, up)

    def load_rows(n):
        return pltpu.make_async_copy((eg, xs)[n % 2].at[n // 2], rows.at[n % 2], r_sem.at[n % 2])

    def load_left(j):
        k, w = jobs[j]
        return pltpu.make_async_copy(lefts[w].at[k], left.at[j % 2], l_sem.at[j % 2])

    def store(j):
        k, w = jobs[j]
        return pltpu.make_async_copy(out.at[j % 2], outs[w].at[k], o_sem.at[j % 2])

    load_rows(0).start()
    load_left(0).start()
    load_rows(1).start()
    for j, (k, w) in enumerate(jobs):
        if j + 1 < len(jobs):
            load_left(j + 1).start()
        load_left(j).wait()
        if w < 2:
            load_rows(2 * k + w).wait()
        if j >= 2:
            store(j - 2).wait()
        right = rows.at[min(w, 1)]
        for lo, n in strips(width, 768):
            out[j % 2, :, lo : lo + n] = tn(left[j % 2], right[:, lo : lo + n])
        store(j).start()
        if k == 0 and w in (0, 2):
            load_rows(2 + (w > 0)).start()
    for j in (len(jobs) - 2, len(jobs) - 1):
        store(j).wait()


def weight_grads(xs, eg, mid, ug, gg):
    _, n, width = xs.shape
    ff = mid.shape[2]
    free = pl.BlockSpec(memory_space=pl.ANY)
    D = pltpu.SemaphoreType.DMA
    return pl.pallas_call(
        weight_grads_kernel,
        out_shape=[jax.ShapeDtypeStruct((2, ff, width), F32)] * 3,
        in_specs=[free] * 5,
        out_specs=[free] * 3,
        scratch_shapes=[
            pltpu.VMEM((2, n, width), BF), pltpu.VMEM((2, n, ff), BF), pltpu.VMEM((2, ff, width), F32),
            D((2,)), D((2,)), D((2,)),
        ],
        compiler_params=pltpu.CompilerParams(vmem_limit_bytes=60 * 1024 * 1024),
        cost_estimate=pl.CostEstimate(
            flops=12 * n * ff * width, bytes_accessed=100_000_000, transcendentals=0
        ),
        name="weight_grads",
    )(xs, eg, mid, ug, gg)


def this_slice(
    tokens,
    seq_lengths,
    routes,
    attn_gain,
    w_query,
    b_query,
    w_key,
    b_key,
    w_value,
    b_value,
    sinks,
    w_out,
    b_out,
    ffn_gain,
    w_router,
    b_router,
    w_gate,
    b_gate,
    w_up,
    b_up,
    w_down,
    b_down,
    cotangent,
):
    rows, width = tokens.shape
    fs_size = lax.axis_size("fs")
    ep_size = lax.axis_size("ep")
    my_fs = lax.axis_index("fs")
    my_ep = lax.axis_index("ep")
    blocks = fs_size * ep_size
    expert_count = EXP_DEV * ep_size
    capacity = 3 * rows * TOP // (2 * expert_count)
    shard = w_query.shape[0]
    kv_heads = KEY_VALUE_HEADS // fs_size
    group = QUERY_HEADS // KEY_VALUE_HEADS
    q_cols = kv_heads * group * HEAD_SIZE
    kv_cols = kv_heads * HEAD_SIZE

    spare = (-width) % 128
    small = jnp.concatenate(
        [attn_gain, ffn_gain, b_out, w_router.reshape(-1), b_router, seq_lengths[0].astype(BF)]
    )
    extra = -(-small.shape[0] // (16 * width)) * 16
    small = jnp.pad(small, (0, extra * width - small.shape[0])).reshape(extra, width)
    x_group, small, w_qkv = start_exchange(tokens, small, w_query, w_key, w_value, 4)
    x_group = x_group.reshape(fs_size * rows, width).astype(F32)
    small = small.reshape(fs_size, -1)
    gain_one = small[:, :shard].reshape(-1).astype(F32)
    gain_two = small[:, shard : 2 * shard].reshape(-1).astype(F32)
    bo = small[:, 2 * shard : 3 * shard].reshape(-1).astype(F32)
    at = (3 + expert_count) * shard
    wr = small[:, 3 * shard : at].reshape(width, expert_count)
    br = small[:, at : at + b_router.shape[0]].reshape(-1).astype(F32)
    at += b_router.shape[0]
    lengths = small[:, at : at + seq_lengths.shape[1]].astype(jnp.int32)

    w_qkv = w_qkv.reshape(width, q_cols + 2 * kv_cols)
    b_qkv = jnp.concatenate([b_query, b_key, b_value]).astype(jnp.float32)
    sink_score = sinks.astype(jnp.float32).reshape(1, kv_heads, group, 1)

    x_float = tokens.astype(jnp.float32)
    scale_one = norm_scale(x_float)
    scale_group = norm_scale(x_group)
    norm_attn = (x_group * scale_group * gain_one).astype(jnp.bfloat16)
    segment_ids, position = jax.vmap(lambda own: layout(own, rows))(lengths)
    cosine_table, sine_table = tables(position.reshape(-1), HEAD_SIZE // 2)
    qkv = jnp.dot(norm_attn, w_qkv, preferred_element_type=jnp.float32) + b_qkv
    many = fs_size * rows
    heads = kv_heads * group
    query = apply_rotation(
        qkv[:, :q_cols].reshape(many, heads, HEAD_SIZE), cosine_table, sine_table
    ).astype(jnp.bfloat16)
    query = query.reshape(fs_size, rows, kv_heads, group, HEAD_SIZE)
    key = apply_rotation(
        qkv[:, q_cols : q_cols + kv_cols].reshape(many, kv_heads, HEAD_SIZE),
        cosine_table,
        sine_table,
    ).astype(jnp.bfloat16)
    key = key.reshape(fs_size, rows, kv_heads, HEAD_SIZE)
    value = qkv[:, q_cols + kv_cols :].astype(jnp.bfloat16)
    value = value.reshape(fs_size, rows, kv_heads, HEAD_SIZE)
    places = jnp.arange(rows, dtype=jnp.int32)
    allowed = (segment_ids[:, :, None] == segment_ids[:, None, :]) & (
        places[:, None] >= places[None, :]
    )
    scores = mm("bqhgd,bkhd->bhgqk", query, key) * HEAD_SIZE ** (-0.5)
    masked = jnp.where(allowed[:, None, None], scores, MASKED_SCORE)
    top_score = jnp.maximum(jnp.max(masked, axis=-1), sink_score)
    exponent = jnp.exp(masked - top_score[..., None])
    sink_exp = jnp.exp(sink_score - top_score)
    denominator = jnp.sum(exponent, axis=-1) + sink_exp
    probs = exponent / denominator[..., None]
    sink_prob = sink_exp / denominator
    probs_b = probs.astype(jnp.bfloat16)
    mixed = mm("bhgqk,bkhd->bqhgd", probs_b, value).astype(jnp.bfloat16)
    mixed = mixed.reshape(many, q_cols)
    projected = project_sum(
        mixed.reshape(fs_size, rows, q_cols), jnp.swapaxes(w_out, 0, 1), 5
    )
    resid = x_float + projected + bo
    scale_two = norm_scale(resid)
    norm_ffn = (resid * scale_two * gain_two).astype(jnp.bfloat16)

    logits = jnp.dot(norm_ffn, wr, preferred_element_type=F32) + br
    one_hot = (routes[:, :, None] == jnp.arange(expert_count, dtype=jnp.int32)).astype(F32)
    member = jnp.sum(one_hot, axis=1)
    peak = jnp.max(jnp.where(member > 0, logits, MASKED_SCORE), axis=-1, keepdims=True)
    gate_exp = jnp.where(member > 0, jnp.exp(logits - peak), 0.0)
    gates_here = gate_exp / jnp.sum(gate_exp, axis=-1, keepdims=True)
    place = jnp.where(member > 0, jnp.cumsum(member, axis=0) - member, -1.0)
    gate_high = lax.reduce_precision(gates_here, 8, 7)
    block = jnp.concatenate(
        [norm_ffn]
        + [v.astype(BF) for v in (place, gate_high, gates_here - gate_high)]
        + [jnp.zeros((rows, spare - 3 * expert_count), BF)],
        axis=1,
    )
    wg_t = jnp.swapaxes(w_gate, 1, 2)
    wu_t = jnp.swapaxes(w_up, 1, 2)
    (
        out_part,
        row_part,
        x_slots,
        expert_grad,
        middle,
        up_grad,
        gate_grad_pre,
        grad_b_gate,
        grad_b_up,
        grad_b_down,
    ) = experts(
        block,
        jnp.pad(cotangent, ((0, 0), (0, spare))),
        wg_t,
        b_gate,
        wu_t,
        b_up,
        w_down,
        b_down,
        capacity,
        1,
    )
    sums = scatter_blocks([out_part, row_part], 2)
    block_out = resid + sums[0, :, :width].astype(F32)
    grad_w_down, gate_t, up_t = weight_grads(
        x_slots, expert_grad, middle, up_grad, gate_grad_pre
    )
    grad_w_gate = jnp.swapaxes(gate_t, 1, 2)
    grad_w_up = jnp.swapaxes(up_t, 1, 2)
    row_sum = sums[1].astype(F32)
    gate_grad = row_sum[:, width : width + expert_count]
    logit_grad = gates_here * (
        gate_grad - jnp.sum(gates_here * gate_grad, axis=-1, keepdims=True)
    )
    logit_grad = logit_grad.astype(jnp.bfloat16)
    grad_br = jnp.sum(logit_grad, axis=0, dtype=jnp.float32)
    grad_wr = left_dot(norm_ffn, logit_grad)
    norm_ffn_grad = row_sum[:, :width] + jnp.dot(
        logit_grad, wr.T, preferred_element_type=jnp.float32
    )
    resid_norm_grad, grad_gain_two = norm_back(resid, scale_two, gain_two, norm_ffn_grad)
    resid_grad = cotangent.astype(jnp.float32) + resid_norm_grad

    branch_grad = gather_fs(resid_grad.astype(jnp.bfloat16))
    grad_bo = jnp.sum(branch_grad, axis=0, dtype=jnp.float32)
    mixed_grad = mm("td,fd->tf", branch_grad, w_out).astype(jnp.bfloat16)
    mixed_grad = mixed_grad.reshape(fs_size, rows, kv_heads, group, HEAD_SIZE)
    grad_probs = mm("bqhgd,bkhd->bhgqk", mixed_grad, value)
    value_grad = mm("bhgqk,bqhgd->bkhd", probs_b, mixed_grad)
    row_delta = jnp.sum(probs * grad_probs, axis=-1)
    score_grad = (probs * (grad_probs - row_delta[..., None])).astype(jnp.bfloat16)
    query_grad = mm("bhgqk,bkhd->bqhgd", score_grad, key) * HEAD_SIZE ** (-0.5)
    key_grad = mm("bhgqk,bqhgd->bkhd", score_grad, query) * HEAD_SIZE ** (-0.5)
    grad_sink = -jnp.sum(sink_prob * row_delta, axis=(0, 3)).reshape(-1)
    query_pre_grad = undo_rotation(
        query_grad.reshape(many, heads, HEAD_SIZE), cosine_table, sine_table
    ).reshape(many, q_cols)
    key_pre_grad = undo_rotation(
        key_grad.reshape(many, kv_heads, HEAD_SIZE), cosine_table, sine_table
    ).reshape(many, kv_cols)
    qkv_grad = jnp.concatenate(
        [query_pre_grad, key_pre_grad, value_grad.reshape(many, kv_cols)], axis=1
    ).astype(jnp.bfloat16)
    grad_b_qkv = jnp.sum(qkv_grad, axis=0, dtype=jnp.float32)
    part = mm("tf,df->td", qkv_grad, w_qkv)
    grad_gain_one = jnp.sum(part * (x_group * scale_group), axis=0)
    norm_attn_grad = scatter_fs(part.astype(BF)).astype(F32)
    input_norm_grad, _ = norm_back(x_float, scale_one, gain_one, norm_attn_grad)
    grad_tokens = resid_grad + input_norm_grad
    by_shard = jnp.concatenate(
        [
            grad_wr.reshape(fs_size, -1),
            grad_gain_one.reshape(fs_size, -1),
            grad_gain_two.reshape(fs_size, -1),
            grad_br.reshape(fs_size, -1),
        ],
        axis=1,
    ).astype(BF)
    own = jnp.concatenate(
        [grad_b_qkv, grad_sink, lax.dynamic_slice_in_dim(grad_bo, my_fs * shard, shard)]
    ).astype(BF)
    cols = q_cols + 2 * kv_cols
    slab_rows = 768
    wide_part = 144
    own = jnp.where(jnp.arange(fs_size)[:, None] == my_fs, own, jnp.zeros((), BF))
    by_shard = jnp.concatenate([by_shard, own], axis=1)
    small_n = by_shard.shape[1]
    small_rows = -(-small_n // q_cols)
    by_shard = jnp.pad(by_shard, ((0, 0), (0, small_rows * q_cols - small_n)))
    by_shard = jnp.pad(
        by_shard.reshape(fs_size, small_rows, q_cols),
        ((0, 0), (0, slab_rows - shard - small_rows), (0, cols - q_cols)),
    )
    gq = left_dot(norm_attn, qkv_grad).astype(BF).reshape(fs_size, shard, cols)
    gw = left_dot(branch_grad, mixed).astype(BF)
    gw = gw.reshape(2, width // (2 * wide_part), wide_part, q_cols)
    tw, tq, tk, tv = reduce_parts(gw, gq, by_shard, 3, (q_cols, kv_cols, kv_cols), 3)
    sum_wo = jnp.swapaxes(tw.reshape(width, q_cols).astype(F32), 0, 1)
    sum_wq = tq[:shard].astype(F32)
    sum_wk = tk[:shard].astype(F32)
    sum_wv = tv[:shard].astype(F32)
    by_shard = jnp.sum(
        tq[shard : shard + small_rows].astype(F32).reshape(small_rows, fs_size, q_cols), axis=1
    ).reshape(-1)
    sum_wr = by_shard[: shard * expert_count].reshape(shard, expert_count)
    rest = by_shard[shard * expert_count : small_n - own.shape[1]]
    own = by_shard[small_n - own.shape[1] : small_n]
    sum_b = own[:cols]
    return (
        block_out.astype(jnp.bfloat16),
        grad_tokens,
        rest[:shard],
        sum_wq,
        sum_b[:q_cols],
        sum_wk,
        sum_b[q_cols : q_cols + kv_cols],
        sum_wv,
        sum_b[q_cols + kv_cols :],
        own[q_cols + 2 * kv_cols : q_cols + 2 * kv_cols + heads],
        sum_wo,
        own[q_cols + 2 * kv_cols + heads :],
        rest[shard : 2 * shard],
        sum_wr,
        rest[2 * shard :],
        grad_w_gate,
        grad_b_gate,
        grad_w_up,
        grad_b_up,
        grad_w_down,
        grad_b_down,
    )


def any_slice(
    tokens,
    seq_lengths,
    routes,
    attn_gain,
    w_query,
    b_query,
    w_key,
    b_key,
    w_value,
    b_value,
    sinks,
    w_out,
    b_out,
    ffn_gain,
    w_router,
    b_router,
    w_gate,
    b_gate,
    w_up,
    b_up,
    w_down,
    b_down,
    cotangent,
):
    rows, width = tokens.shape
    fs_size = lax.axis_size("fs")
    ep_size = lax.axis_size("ep")
    my_fs = lax.axis_index("fs")
    my_ep = lax.axis_index("ep")
    blocks = fs_size * ep_size
    expert_count = EXP_DEV * ep_size
    capacity = 3 * rows * TOP // (2 * expert_count)
    shard = w_query.shape[0]
    kv_heads = KEY_VALUE_HEADS // fs_size
    group = QUERY_HEADS // KEY_VALUE_HEADS
    q_cols = kv_heads * group * HEAD_SIZE
    kv_cols = kv_heads * HEAD_SIZE

    packed = jnp.concatenate(
        [attn_gain, ffn_gain, b_out, w_router.reshape(-1), b_router]
    )
    packed = lax.all_gather(packed, "fs", axis=0)
    gain_one = packed[:, :shard].reshape(-1).astype(jnp.float32)
    gain_two = packed[:, shard : 2 * shard].reshape(-1).astype(jnp.float32)
    bo = packed[:, 2 * shard : 3 * shard].reshape(-1).astype(jnp.float32)
    wr = packed[:, 3 * shard : (3 + expert_count) * shard].reshape(width, expert_count)
    br = packed[:, (3 + expert_count) * shard :].reshape(-1).astype(jnp.float32)
    whole_numbers = gather_all(
        jnp.concatenate([routes.reshape(-1), seq_lengths.reshape(-1)])[None]
    )
    routes_all = whole_numbers[:, : rows * TOP].reshape(blocks, rows, TOP)
    lengths_all = whole_numbers[:, rows * TOP :]
    lengths = lax.dynamic_index_in_dim(
        lengths_all.reshape(fs_size, ep_size, -1), my_ep, 1, keepdims=False
    )
    g_all = gather_all(cotangent)

    w_qkv = jnp.concatenate(
        [
            w_query.reshape(shard, fs_size, q_cols),
            w_key.reshape(shard, fs_size, kv_cols),
            w_value.reshape(shard, fs_size, kv_cols),
        ],
        axis=2,
    )
    w_qkv = lax.all_to_all(w_qkv, "fs", split_axis=1, concat_axis=0, tiled=True)
    w_qkv = w_qkv.reshape(width, q_cols + 2 * kv_cols)
    b_qkv = jnp.concatenate([b_query, b_key, b_value]).astype(jnp.float32)
    sink_score = sinks.astype(jnp.float32).reshape(1, kv_heads, group, 1)

    x_float = tokens.astype(jnp.float32)
    scale_one = norm_scale(x_float)
    norm_attn = gather_fs((x_float * scale_one * gain_one).astype(jnp.bfloat16))
    segment_ids, position = jax.vmap(lambda own: layout(own, rows))(lengths)
    cosine_table, sine_table = tables(position.reshape(-1), HEAD_SIZE // 2)
    qkv = jnp.dot(norm_attn, w_qkv, preferred_element_type=jnp.float32) + b_qkv
    many = fs_size * rows
    heads = kv_heads * group
    query = apply_rotation(
        qkv[:, :q_cols].reshape(many, heads, HEAD_SIZE), cosine_table, sine_table
    ).astype(jnp.bfloat16)
    query = query.reshape(fs_size, rows, kv_heads, group, HEAD_SIZE)
    key = apply_rotation(
        qkv[:, q_cols : q_cols + kv_cols].reshape(many, kv_heads, HEAD_SIZE),
        cosine_table,
        sine_table,
    ).astype(jnp.bfloat16)
    key = key.reshape(fs_size, rows, kv_heads, HEAD_SIZE)
    value = qkv[:, q_cols + kv_cols :].astype(jnp.bfloat16)
    value = value.reshape(fs_size, rows, kv_heads, HEAD_SIZE)
    places = jnp.arange(rows, dtype=jnp.int32)
    allowed = (segment_ids[:, :, None] == segment_ids[:, None, :]) & (
        places[:, None] >= places[None, :]
    )
    scores = mm("bqhgd,bkhd->bhgqk", query, key) * HEAD_SIZE ** (-0.5)
    masked = jnp.where(allowed[:, None, None], scores, MASKED_SCORE)
    top_score = jnp.maximum(jnp.max(masked, axis=-1), sink_score)
    exponent = jnp.exp(masked - top_score[..., None])
    sink_exp = jnp.exp(sink_score - top_score)
    denominator = jnp.sum(exponent, axis=-1) + sink_exp
    probs = exponent / denominator[..., None]
    sink_prob = sink_exp / denominator
    probs_b = probs.astype(jnp.bfloat16)
    mixed = mm("bhgqk,bkhd->bqhgd", probs_b, value).astype(jnp.bfloat16)
    mixed = mixed.reshape(many, q_cols)
    out_part = jnp.dot(mixed, w_out, preferred_element_type=jnp.float32)
    resid = x_float + scatter_fs(out_part.astype(jnp.bfloat16)).astype(jnp.float32) + bo
    scale_two = norm_scale(resid)
    norm_ffn = (resid * scale_two * gain_two).astype(jnp.bfloat16)

    n_all = gather_all(norm_ffn)
    logits = jnp.dot(n_all, wr, preferred_element_type=jnp.float32) + br
    logits = logits.reshape(blocks, rows, expert_count)
    one_hot = (
        routes_all[:, :, :, None] == jnp.arange(expert_count, dtype=jnp.int32)
    ).astype(jnp.float32)
    member = jnp.sum(one_hot, axis=2)
    peak = jnp.max(jnp.where(member > 0, logits, MASKED_SCORE), axis=-1, keepdims=True)
    gate_exp = jnp.where(member > 0, jnp.exp(logits - peak), 0.0)
    gates = gate_exp / jnp.sum(gate_exp, axis=-1, keepdims=True)
    own_member = lax.dynamic_slice_in_dim(member, my_ep * EXP_DEV, EXP_DEV, axis=2)
    own_gates = lax.dynamic_slice_in_dim(gates, my_ep * EXP_DEV, EXP_DEV, axis=2)
    rank = jnp.cumsum(own_member, axis=1) - own_member
    slots = jnp.arange(capacity, dtype=jnp.float32)
    pick = (rank.transpose(0, 2, 1)[:, :, None, :] == slots[:, None]) & (
        own_member.transpose(0, 2, 1)[:, :, None, :] > 0
    )
    pick_b = pick.astype(jnp.bfloat16)
    slot_gate = jnp.sum(
        jnp.where(pick, own_gates.transpose(0, 2, 1)[:, :, None, :], 0.0), axis=-1
    )
    slot_gate = slot_gate.transpose(1, 0, 2).reshape(EXP_DEV, blocks * capacity, 1)

    def spread(full):
        parts = mm("bekt,btd->ebkd", pick_b, full.reshape(blocks, rows, -1))
        return parts.astype(jnp.bfloat16).reshape(EXP_DEV, blocks * capacity, -1)

    def combine(parts):
        parts = parts.reshape(EXP_DEV, blocks, capacity, -1)
        return mm("bekt,ebkd->btd", pick_b, parts).reshape(blocks * rows, -1)

    x_slots = spread(n_all)
    g_slots = spread(g_all)
    gate_pre = mm("erd,edf->erf", x_slots, w_gate) + b_gate.astype(jnp.float32)[:, None]
    up_pre = mm("erd,edf->erf", x_slots, w_up) + b_up.astype(jnp.float32)[:, None]
    gate_soft = CLAMP_LIMIT * jnp.tanh(gate_pre / CLAMP_LIMIT)
    up_soft = CLAMP_LIMIT * jnp.tanh(up_pre / CLAMP_LIMIT)
    gate_sig = jax.nn.sigmoid(SWIGLU_ALPHA * gate_soft)
    glu_part = gate_soft * gate_sig
    middle = ((up_soft + 1.0) * glu_part).astype(jnp.bfloat16)
    first = (my_fs == 0).astype(jnp.float32)
    down_bias = b_down.astype(jnp.float32) * first
    expert_out = mm("erf,efd->erd", middle, w_down) + down_bias[:, None]
    expert_sum = scatter_all(
        combine((expert_out * slot_gate).astype(jnp.bfloat16)).astype(jnp.bfloat16)
    )
    block_out = resid + expert_sum.astype(jnp.float32)

    expert_grad = (g_slots.astype(jnp.float32) * slot_gate).astype(jnp.bfloat16)
    plain_grad = mm("erd,efd->erf", g_slots, w_down)
    middle_grad = plain_grad * slot_gate
    gate_dot = jnp.sum(plain_grad * middle.astype(jnp.float32), axis=-1) + jnp.sum(
        g_slots.astype(jnp.float32) * down_bias[:, None], axis=-1
    )
    grad_w_down = mm("erf,erd->efd", middle, expert_grad)
    grad_b_down = jnp.sum(expert_grad, axis=1, dtype=jnp.float32)
    up_grad = (middle_grad * glu_part * (1.0 - (up_soft / CLAMP_LIMIT) ** 2)).astype(jnp.bfloat16)
    gate_grad_pre = (
        middle_grad
        * (up_soft + 1.0)
        * (gate_sig + SWIGLU_ALPHA * gate_soft * gate_sig * (1.0 - gate_sig))
        * (1.0 - (gate_soft / CLAMP_LIMIT) ** 2)
    ).astype(jnp.bfloat16)
    grad_w_gate = mm("erd,erf->edf", x_slots, gate_grad_pre)
    grad_b_gate = jnp.sum(gate_grad_pre, axis=1, dtype=jnp.float32)
    grad_w_up = mm("erd,erf->edf", x_slots, up_grad)
    grad_b_up = jnp.sum(up_grad, axis=1, dtype=jnp.float32)
    row_part = mm("erf,edf->erd", gate_grad_pre, w_gate) + mm("erf,edf->erd", up_grad, w_up)
    row_sum = combine(row_part.astype(jnp.bfloat16))
    own_dot = jnp.sum(
        jnp.where(pick, gate_dot.reshape(EXP_DEV, blocks, capacity).transpose(1, 0, 2)[..., None], 0.0),
        axis=2,
    )
    dots = jnp.sum(
        own_dot[..., None]
        * (
            (my_ep * EXP_DEV + jnp.arange(EXP_DEV))[:, None] == jnp.arange(expert_count)[None]
        ).astype(jnp.float32)[None, :, None, :],
        axis=1,
    ).reshape(blocks * rows, expert_count)
    row_sum = scatter_all(jnp.concatenate([row_sum, dots], axis=1).astype(jnp.bfloat16))
    row_sum = row_sum.astype(jnp.float32)
    gate_grad = row_sum[:, width:]
    mine = my_fs * ep_size + my_ep
    gates_here = lax.dynamic_index_in_dim(gates, mine, 0, keepdims=False)
    logit_grad = gates_here * (
        gate_grad - jnp.sum(gates_here * gate_grad, axis=-1, keepdims=True)
    )
    logit_grad = logit_grad.astype(jnp.bfloat16)
    grad_br = jnp.sum(logit_grad, axis=0, dtype=jnp.float32)
    grad_wr = left_dot(norm_ffn, logit_grad)
    norm_ffn_grad = row_sum[:, :width] + jnp.dot(
        logit_grad, wr.T, preferred_element_type=jnp.float32
    )
    resid_norm_grad, grad_gain_two = norm_back(resid, scale_two, gain_two, norm_ffn_grad)
    resid_grad = cotangent.astype(jnp.float32) + resid_norm_grad

    branch_grad = gather_fs(resid_grad.astype(jnp.bfloat16))
    grad_bo = jnp.sum(branch_grad, axis=0, dtype=jnp.float32)
    mixed_grad = mm("td,fd->tf", branch_grad, w_out).astype(jnp.bfloat16)
    mixed_grad = mixed_grad.reshape(fs_size, rows, kv_heads, group, HEAD_SIZE)
    grad_wo = left_dot(mixed, branch_grad)
    grad_probs = mm("bqhgd,bkhd->bhgqk", mixed_grad, value)
    value_grad = mm("bhgqk,bqhgd->bkhd", probs_b, mixed_grad)
    row_delta = jnp.sum(probs * grad_probs, axis=-1)
    score_grad = (probs * (grad_probs - row_delta[..., None])).astype(jnp.bfloat16)
    query_grad = mm("bhgqk,bkhd->bqhgd", score_grad, key) * HEAD_SIZE ** (-0.5)
    key_grad = mm("bhgqk,bqhgd->bkhd", score_grad, query) * HEAD_SIZE ** (-0.5)
    grad_sink = -jnp.sum(sink_prob * row_delta, axis=(0, 3)).reshape(-1)
    query_pre_grad = undo_rotation(
        query_grad.reshape(many, heads, HEAD_SIZE), cosine_table, sine_table
    ).reshape(many, q_cols)
    key_pre_grad = undo_rotation(
        key_grad.reshape(many, kv_heads, HEAD_SIZE), cosine_table, sine_table
    ).reshape(many, kv_cols)
    qkv_grad = jnp.concatenate(
        [query_pre_grad, key_pre_grad, value_grad.reshape(many, kv_cols)], axis=1
    ).astype(jnp.bfloat16)
    grad_b_qkv = jnp.sum(qkv_grad, axis=0, dtype=jnp.float32)
    norm_attn_grad = scatter_fs(
        mm("tf,df->td", qkv_grad, w_qkv).astype(jnp.bfloat16)
    ).astype(jnp.float32)
    input_norm_grad, grad_gain_one = norm_back(x_float, scale_one, gain_one, norm_attn_grad)
    grad_tokens = resid_grad + input_norm_grad
    grad_qkv = left_dot(norm_attn, qkv_grad).astype(jnp.bfloat16)
    if shard % ep_size == 0:
        grad_qkv = grad_qkv.reshape(fs_size, ep_size, shard // ep_size, q_cols + 2 * kv_cols)
        grad_qkv = lax.psum_scatter(grad_qkv, "ep", scatter_dimension=1, tiled=False)
        grad_qkv = lax.all_to_all(grad_qkv, "fs", split_axis=0, concat_axis=1, tiled=False)
        grad_qkv = lax.all_gather(grad_qkv, "ep", axis=0, tiled=True).astype(jnp.float32)
    else:
        grad_qkv = lax.psum(grad_qkv.reshape(fs_size, shard, q_cols + 2 * kv_cols), "ep")
        grad_qkv = lax.all_to_all(grad_qkv, "fs", split_axis=0, concat_axis=1, tiled=False)
        grad_qkv = grad_qkv.astype(jnp.float32)
    sum_wq = grad_qkv[:, :, :q_cols].reshape(shard, -1)
    sum_wk = grad_qkv[:, :, q_cols : q_cols + kv_cols].reshape(shard, -1)
    sum_wv = grad_qkv[:, :, q_cols + kv_cols :].reshape(shard, -1)
    sum_wo = lax.psum(grad_wo.astype(jnp.bfloat16), "ep").astype(jnp.float32)
    by_shard = jnp.concatenate(
        [
            grad_wr.reshape(fs_size, -1),
            grad_gain_one.reshape(fs_size, -1),
            grad_gain_two.reshape(fs_size, -1),
            grad_br.reshape(fs_size, -1),
        ],
        axis=1,
    )
    by_shard = lax.psum(by_shard, ("fs", "ep"))
    by_shard = lax.dynamic_index_in_dim(by_shard, my_fs, 0, keepdims=False)
    sum_wr = by_shard[: shard * expert_count].reshape(shard, expert_count)
    rest = by_shard[shard * expert_count :]
    own = jnp.concatenate(
        [
            grad_b_qkv,
            grad_sink,
            lax.dynamic_slice_in_dim(grad_bo, my_fs * shard, shard),
        ]
    )
    own = lax.psum(own, "ep")
    sum_b = own[: q_cols + 2 * kv_cols]
    return (
        block_out.astype(jnp.bfloat16),
        grad_tokens,
        rest[:shard],
        sum_wq,
        sum_b[:q_cols],
        sum_wk,
        sum_b[q_cols : q_cols + kv_cols],
        sum_wv,
        sum_b[q_cols + kv_cols :],
        own[q_cols + 2 * kv_cols : q_cols + 2 * kv_cols + heads],
        sum_wo,
        own[q_cols + 2 * kv_cols + heads :],
        rest[shard : 2 * shard],
        sum_wr,
        rest[2 * shard :],
        grad_w_gate,
        grad_b_gate,
        grad_w_up,
        grad_b_up,
        grad_w_down,
        grad_b_down,
    )


def solution(mesh):
    in_specs = (
        P(("fs", "ep"), None),
        P(("fs", "ep"), None),
        P(("fs", "ep"), None),
        P("fs"),
        P("fs", None),
        P("fs"),
        P("fs", None),
        P("fs"),
        P("fs", None),
        P("fs"),
        P("fs"),
        P("fs", None),
        P("fs"),
        P("fs"),
        P("fs", None),
        P("fs"),
        P("ep", None, "fs"),
        P("ep", "fs"),
        P("ep", None, "fs"),
        P("ep", "fs"),
        P("ep", "fs", None),
        P("ep", None),
        P(("fs", "ep"), None),
    )
    out_specs = (
        P(("fs", "ep"), None),
        P(("fs", "ep"), None),
        P("fs"),
        P("fs", None),
        P("fs"),
        P("fs", None),
        P("fs"),
        P("fs", None),
        P("fs"),
        P("fs"),
        P("fs", None),
        P("fs"),
        P("fs"),
        P("fs", None),
        P("fs"),
        P("ep", None, "fs"),
        P("ep", "fs"),
        P("ep", None, "fs"),
        P("ep", "fs"),
        P("ep", "fs", None),
        P("ep", None),
    )
    run = this_slice if (mesh.shape["fs"], mesh.shape["ep"]) == (4, 8) else any_slice
    return jax.shard_map(
        run, mesh=mesh, in_specs=in_specs, out_specs=out_specs, check_vma=False
    )
```
